32 devices in a mesh: expert: 16 (over z, y, x), tensor: 2 (over core).
Axes of the slice: x: 2, y: 2, z: 4, core: 2. Of those that a mesh axis runs over, the one named last changes fastest.
Arguments:
- tokens: bfloat16 [16384, 1536], P('expert'), may hold values from -6 to 6
- cotangent: bfloat16 [16384, 1536], P('expert'), may hold values from -6 to 6
- norm_gain: float32 [1536], replicated, may hold values from 0.5 to 1.5
- ffn_gain: float32 [1536], replicated, may hold values from 0.5 to 1.5
- w_query: bfloat16 [1536, 1536], P(None, 'tensor'), may hold values from -0.15625 to 0.15625
- w_key: bfloat16 [1536, 256], P(None, 'tensor'), may hold values from -0.15625 to 0.15625
- w_value: bfloat16 [1536, 256], P(None, 'tensor'), may hold values from -0.15625 to 0.15625
- w_out: bfloat16 [1536, 1536], P('tensor'), may hold values from -1.25 to 1.25
- w_router: bfloat16 [1536, 16], replicated, may hold values from -0.078125 to 0.078125
- w_gate: bfloat16 [16, 1536, 768], P('expert', None, 'tensor'), may hold values from -0.15625 to 0.15625
- w_up: bfloat16 [16, 1536, 768], P('expert', None, 'tensor'), may hold values from -0.15625 to 0.15625
- w_down: bfloat16 [16, 768, 1536], P('expert', 'tensor'), may hold values from -0.625 to 0.625
- routes: int32 [16384, 4], P('expert'), may hold values from 0 to 15, all different within a row
- order: int32 [16, 4096], P('expert'), may hold values from 0 to 4095, each once within a row
- segments: int32 [16, 1024], P('expert'), may hold values from 0 to 5, never falling along the last dimension, each value on 1 to 256 neighbouring positions
Outputs:
- output: bfloat16 [16384, 1536], P('expert')
- input_grad: float32 [16384, 1536], P('expert')
- norm_gain_grad: float32 [1536], P('expert')
- ffn_gain_grad: float32 [1536], P('expert')
- query_grad: float32 [1536, 1536], P('expert', 'tensor')
- key_grad: float32 [1536, 256], P('expert', 'tensor')
- value_grad: float32 [1536, 256], P('expert', 'tensor')
- out_grad: float32 [1536, 1536], P('tensor', 'expert')
- router_grad: float32 [1536, 16], P('expert')
- gate_grad: float32 [16, 1536, 768], P('expert', None, 'tensor')
- up_grad: float32 [16, 1536, 768], P('expert', None, 'tensor')
- down_grad: float32 [16, 768, 1536], P('expert', 'tensor')
The draws below stay inside these ranges and needn't reach their ends.
Inputs may be any that keep to these rules, and one draw needn't show every extreme that they name: `routes`: each row names 4 different experts; every expert is named by some row. `order`: each row holds each rank once; entry t * 4 + k belongs to pair k of token t. `segments`: never falls along a row; each value covers 1 to 256 positions of its row, some one exactly 256.
All inputs are finite; a program needn't handle non-finite values.
Results may differ from the reference program's by a relative error of at most 0.025.
Values may be sent and summed in bfloat16 or wider, within the bound.
No kernel may reach another device: no remote copies, remote signals or barrier semaphores. Data moves between devices by JAX's collectives and lax.ppermute only.
A program may use at most 384 MiB of HBM per device.

```python
import math
import jax
import jax.numpy as jnp
import numpy as np
from jax import lax

D = 1536
HEADS = 12
HEAD = 128
KV = 2
FF = 768
TOP = 4
LEN = 1024
BLOCK = 256
SEQS = 16
EXPERTS = 16
TOKENS = 16384
NSEG = 6
CAP = 288
N_TENSOR = 2


def steps_of(own_key, extent, cuts, smallest, high):
    loudness = 1.0
    for axis_at, shards_of in cuts:
        heights = jax.random.uniform(jax.random.fold_in(jax.random.fold_in(own_key, 6), axis_at), (shards_of,), jnp.float32, smallest / len(cuts), high / len(cuts))
        loudness = loudness * jnp.repeat(jnp.exp(heights), extent[axis_at] // shards_of).reshape((-1,) + (1,) * (len(extent) - 1 - axis_at))
    return loudness


def distinct(own_key, rows, number_of, top, lift):
    order = jax.random.permutation(jax.random.fold_in(own_key, 1), number_of)
    boost = order
    for power in range(3):
        boost = boost * boost // number_of
    boost = boost * lift // number_of
    chance = jax.random.randint(jax.random.fold_in(own_key, 2), (rows, number_of), 0, 4096) + boost
    sure = jax.random.permutation(jax.random.fold_in(own_key, 3), rows)[jnp.arange(number_of) % rows]
    chance = jnp.where(jnp.arange(rows)[:, None] == sure[None, :], 1 << 14, chance)
    score = chance * number_of + jnp.arange(number_of)
    return lax.top_k(score.astype(jnp.int32), top)[1].astype(jnp.int32)


def split_up(amount, total, limit, lean):
    loads = [(1 << 20) // math.isqrt(rank ** lean) + 1 for rank in range(2, amount + 1)]
    rest, holding = total - limit - (amount - 1), [1] * (amount - 1)
    while rest > 0:
        free = [i for i in range(amount - 1) if holding[i] < limit]
        mass, remaining = sum([loads[i] for i in free]), rest
        for i in free:
            extra = min(limit - holding[i], max(1, remaining * loads[i] // mass), rest)
            holding[i] = holding[i] + extra
            rest = rest - extra
    return np.array([limit] + holding)


def uneven(key, count, total, limit, slope):
    if count == 2:
        one = jax.random.randint(key, (), max(1, total - limit), min(limit, total - 1) + 1)
        return jnp.stack([one, total - one])
    lengths = jnp.asarray(split_up(count, total, limit, slope), jnp.int32)
    couples = (count - 1) // 2
    giver, receiver = lengths[1:1 + 2 * couples:2], lengths[2:2 + 2 * couples:2]
    margin = jnp.minimum(giver - 1, limit - receiver)
    moved = jax.random.randint(jax.random.fold_in(key, 1), (couples,), 0, 1 << 20) % (margin + 1)
    lengths = lengths.at[1:1 + 2 * couples:2].set(giver - moved).at[2:2 + 2 * couples:2].set(receiver + moved)
    return lengths[jax.random.permutation(jax.random.fold_in(key, 2), count)]


def scatter_about(own_key, dims, spread, most, split=(), kind=jnp.bfloat16):
    drawn = spread * jax.random.normal(own_key, dims, jnp.float32)
    if split:
        drawn = drawn * steps_of(own_key, dims, split, -0.22, 0.18)
    return jnp.clip(drawn, -most, most).astype(kind)


def setup_inputs(seed: int = 0) -> dict:
    key_of = jax.random.split(jax.random.key(seed), 16)
    tokens = scatter_about(key_of[0], (TOKENS, D), 1.0, 6.0, ((0, 16),))
    cotangent = scatter_about(key_of[1], (TOKENS, D), 1.0, 6.0, ((0, 16),))
    norm_gain = jnp.clip(1.0 + 0.1 * jax.random.normal(key_of[2], (D,), jnp.float32), 0.5, 1.5)
    ffn_gain = jnp.clip(1.0 + 0.1 * jax.random.normal(key_of[3], (D,), jnp.float32), 0.5, 1.5)
    w_query = scatter_about(key_of[4], (D, HEADS * HEAD), D ** -0.5, 0.15625, ((1, 2),))
    w_key = scatter_about(key_of[5], (D, KV * HEAD), D ** -0.5, 0.15625, ((1, 2),))
    w_value = scatter_about(key_of[6], (D, KV * HEAD), D ** -0.5, 0.15625, ((1, 2),))
    w_out = scatter_about(key_of[7], (HEADS * HEAD, D), (HEADS * HEAD // 64) ** -0.5, 1.25, ((0, 2),))
    w_router = scatter_about(key_of[8], (D, EXPERTS), (4 * D) ** -0.5, 0.078125)
    w_gate = scatter_about(key_of[9], (EXPERTS, D, FF), D ** -0.5, 0.15625, ((0, 16), (2, 2)))
    w_up = scatter_about(key_of[10], (EXPERTS, D, FF), D ** -0.5, 0.15625, ((0, 16), (2, 2)))
    w_down = scatter_about(key_of[11], (EXPERTS, FF, D), (FF // 8) ** -0.5, 0.625, ((0, 16), (1, 2)))
    routes = distinct(key_of[12], TOKENS, EXPERTS, TOP, 2048)
    order = jax.vmap(lambda own: jax.random.permutation(own, LEN * TOP))(jax.random.split(key_of[13], SEQS)).reshape((SEQS, LEN * TOP)).astype(jnp.int32)
    segments = jax.vmap(lambda own: jnp.searchsorted(jnp.cumsum(uneven(own, NSEG, LEN, BLOCK, 1)), jnp.arange(LEN), side="right"))(jax.random.split(key_of[14], SEQS)).reshape((SEQS, LEN)).astype(jnp.int32)
    return dict(tokens=tokens, cotangent=cotangent, norm_gain=norm_gain, ffn_gain=ffn_gain, w_query=w_query, w_key=w_key, w_value=w_value, w_out=w_out, w_router=w_router, w_gate=w_gate, w_up=w_up, w_down=w_down, routes=routes, order=order, segments=segments)


@jax.custom_vjp
def low(v):
    return lax.optimization_barrier(v.astype(jnp.bfloat16)).astype(jnp.float32)

@jax.custom_vjp
def low_back(v):
    return v

def low_keep(v):
    return (low(v), None)

def low_pass(kept, grad):
    return (grad,)

def back_keep(v):
    return (v, None)

def back_low(kept, grad):
    return (low(grad),)
low.defvjp(low_keep, low_pass)
low_back.defvjp(back_keep, back_low)
epsilon = 1e-06
rope_base = 1000000.0
masked_score = -1e+30
highest = lax.Precision.HIGHEST

def rope_tables(seq_length, head_width):
    half_width = head_width // 2
    exponent = jnp.arange(half_width, dtype=jnp.float32) * (2.0 / head_width)
    frequency = jnp.exp(-math.log(rope_base) * exponent)
    angle = jnp.arange(seq_length, dtype=jnp.float32)[:, None] * frequency[None, :]
    return (jnp.cos(angle), jnp.sin(angle))

def rotate(inputs, cosine_table, sine_table):
    half_width = inputs.shape[-1] // 2
    first_part = inputs[..., :half_width]
    second_part = inputs[..., half_width:]
    cosine_wide = cosine_table[:, None, :]
    sine_wide = sine_table[:, None, :]
    return jnp.concatenate([first_part * cosine_wide - second_part * sine_wide, second_part * cosine_wide + first_part * sine_wide], axis=-1)

def rms_scale(inputs):
    return lax.rsqrt(lax.optimization_barrier(jnp.mean(inputs * inputs, axis=-1, keepdims=True)) + epsilon)

def slot_table(route_rows, order_row, expert_count, capacity):
    seq_length, pick_count = route_rows.shape
    pair_count = seq_length * pick_count
    flat_routes = route_rows.reshape(pair_count).astype(jnp.int32)
    order_row = order_row.astype(jnp.int32)
    pair_ids = jnp.arange(pair_count, dtype=jnp.int32)
    by_rank = jnp.zeros((pair_count,), jnp.int32).at[order_row].set(pair_ids)
    ranked = flat_routes[by_rank]
    expert_ids = jnp.arange(expert_count, dtype=jnp.int32)
    ranked_hits = (ranked[:, None] == expert_ids[None, :]).astype(jnp.int32)
    earlier = jnp.cumsum(ranked_hits, axis=0) - ranked_hits
    place_ranked = lax.optimization_barrier(jnp.sum(earlier * ranked_hits, axis=1))
    placement = place_ranked[order_row]
    sink_slot = expert_count * capacity
    pair_slot = jnp.where(placement < capacity, flat_routes * capacity + placement, sink_slot).astype(jnp.int32)
    slot_owner = jnp.full((sink_slot + 1,), seq_length, jnp.int32).at[pair_slot].set(pair_ids // pick_count)
    return (pair_slot.reshape(seq_length, pick_count), slot_owner[:sink_slot])

def reference(tokens, cotangent, norm_gain, ffn_gain, w_query, w_key, w_value, w_out, w_router, w_gate, w_up, w_down, routes, order, segments):
    route_seq = routes.reshape(SEQS, LEN, TOP)
    pair_slot, slot_owner = jax.vmap(lambda route_rows, order_row: slot_table(route_rows, order_row, EXPERTS, CAP))(route_seq, order)
    cosine_table, sine_table = rope_tables(LEN, HEAD)
    local_heads = HEADS // N_TENSOR
    local_units = FF // N_TENSOR
    head_span = local_heads * HEAD
    score_scale = 1.0 / math.sqrt(HEAD)
    expert_ids = jnp.arange(EXPERTS, dtype=jnp.int32)

    def layer(params, sequence_in, segment_row, route_rows, slot_row, owner_row):
        gain_first, gain_second, query_w, key_w, value_w, out_w, router_w, gate_w, up_w, down_w = params
        inverse_first = rms_scale(sequence_in)
        first_in = low(sequence_in * inverse_first * gain_first)
        allowed = segment_row[None, :] <= segment_row[:, None]
        attention = jnp.zeros_like(sequence_in)
        for tensor_half in range(N_TENSOR):
            col_start = tensor_half * head_span
            query_pre = low_back(jnp.dot(first_in, query_w[:, col_start:col_start + head_span], precision=highest))
            query = low(rotate(query_pre.reshape(LEN, local_heads, HEAD), cosine_table, sine_table))
            key_start = tensor_half * HEAD
            key_pre = low_back(jnp.dot(first_in, key_w[:, key_start:key_start + HEAD], precision=highest))
            keys = low(rotate(key_pre.reshape(LEN, 1, HEAD), cosine_table, sine_table))[:, 0, :]
            values = low(low_back(jnp.dot(first_in, value_w[:, key_start:key_start + HEAD], precision=highest)))
            raw_scores = low_back(jnp.einsum('qhd,kd->hqk', query, keys, precision=highest))
            scores = jnp.where(allowed[None], raw_scores * score_scale, masked_score)
            weights = low(jax.nn.softmax(scores, axis=-1))
            mixed = low_back(low(jnp.einsum('hqk,kd->qhd', weights, values, precision=highest)))
            branch_part = jnp.dot(mixed.reshape(LEN, head_span), out_w[col_start:col_start + head_span, :], precision=highest)
            attention = attention + low_back(low(branch_part))
        hidden = sequence_in + attention
        inverse_second = rms_scale(hidden)
        second_in = low(hidden * inverse_second * gain_second)
        logits = low_back(jnp.dot(second_in, router_w, precision=highest))
        picked = route_rows[:, :, None] == expert_ids[None, None, :]
        chosen = lax.optimization_barrier(jnp.sum(jnp.where(picked, logits[:, None, :], 0.0), axis=-1))
        gate_weights = jax.nn.softmax(chosen, axis=-1)
        padded = jnp.concatenate([second_in, jnp.zeros((1, D), second_in.dtype)], axis=0)
        gathered = low_back(padded[owner_row].reshape(EXPERTS, CAP, D))
        expert_sum = jnp.zeros((EXPERTS, CAP, D), jnp.float32)
        for tensor_half in range(N_TENSOR):
            unit_start = tensor_half * local_units
            half_rows = low_back(gathered)
            gate_pre = low_back(jnp.einsum('ecd,edf->ecf', half_rows, gate_w[:, :, unit_start:unit_start + local_units], precision=highest))
            up_pre = low_back(jnp.einsum('ecd,edf->ecf', half_rows, up_w[:, :, unit_start:unit_start + local_units], precision=highest))
            activation = low(jax.nn.silu(gate_pre) * up_pre)
            expert_sum = expert_sum + low(jnp.einsum('ecf,efd->ecd', activation, down_w[:, unit_start:unit_start + local_units, :], precision=highest))
        expert_out = low_back(low(expert_sum))
        out_pad = jnp.concatenate([expert_out.reshape(EXPERTS * CAP, D), jnp.zeros((1, D), expert_out.dtype)], axis=0)
        combined = jnp.zeros_like(sequence_in)
        for pick_rank in range(TOP):
            combined = combined + gate_weights[:, pick_rank:pick_rank + 1] * out_pad[slot_row[:, pick_rank]]
        return hidden + combined

    def forward(tokens_in, *params):

        def one_sequence(pieces):
            sequence_in, segment_row, route_rows, slot_row, owner_row = pieces
            return layer(params, sequence_in, segment_row, route_rows, slot_row, owner_row)
        return lax.map(jax.checkpoint(one_sequence), (tokens_in, segments, route_seq, pair_slot, slot_owner))
    params = tuple((weight_in.astype(jnp.float32) for weight_in in (norm_gain, ffn_gain, w_query, w_key, w_value, w_out, w_router, w_gate, w_up, w_down)))
    tokens_in = tokens.astype(jnp.float32).reshape(SEQS, LEN, D)
    result, pullback = jax.vjp(forward, tokens_in, *params)
    grads = pullback(cotangent.astype(jnp.float32).reshape(SEQS, LEN, D))
    return (result.reshape(TOKENS, D).astype(jnp.bfloat16), grads[0].reshape(TOKENS, D), grads[1], grads[2], grads[3], grads[4], grads[5], grads[6], grads[7], grads[8], grads[9], grads[10])
```

```python
import math

import jax
import jax.numpy as jnp
from jax import lax
from jax.sharding import PartitionSpec as P

epsilon = 1e-06
rope_base = 1000000.0
masked_score = -1e30


def rope_tables(seq_length, head_width):
    half_width = head_width // 2
    exponent = jnp.arange(half_width, dtype=jnp.float32) * (2.0 / head_width)
    frequency = jnp.exp(-math.log(rope_base) * exponent)
    angle = jnp.arange(seq_length, dtype=jnp.float32)[:, None] * frequency[None, :]
    return (jnp.cos(angle), jnp.sin(angle))


def rotate(inputs, cosine_table, sine_table):
    half_width = inputs.shape[-1] // 2
    first_part = inputs[..., :half_width]
    second_part = inputs[..., half_width:]
    cosine_wide = cosine_table[:, None, :]
    sine_wide = sine_table[:, None, :]
    return jnp.concatenate(
        [
            first_part * cosine_wide - second_part * sine_wide,
            second_part * cosine_wide + first_part * sine_wide,
        ],
        axis=-1,
    )


def rotate_back(grads_in, cosine_table, sine_table):
    half_width = grads_in.shape[-1] // 2
    first_part = grads_in[..., :half_width]
    second_part = grads_in[..., half_width:]
    cosine_wide = cosine_table[:, None, :]
    sine_wide = sine_table[:, None, :]
    return jnp.concatenate(
        [
            first_part * cosine_wide + second_part * sine_wide,
            second_part * cosine_wide - first_part * sine_wide,
        ],
        axis=-1,
    )


def rms_scale(inputs):
    return lax.rsqrt(jnp.mean(inputs * inputs, axis=-1, keepdims=True) + epsilon)


def contract_rows(left, right):
    return lax.dot_general(
        left, right, (((0,), (0,)), ((), ())), preferred_element_type=jnp.float32
    )


def times_transposed(left, right):
    return lax.dot_general(
        left, right, (((1,), (1,)), ((), ())), preferred_element_type=jnp.float32
    )


def attention_scores(query, keys, allowed, score_scale):
    raw_scores = jnp.einsum("qhd,kd->hqk", query, keys, preferred_element_type=jnp.float32)
    return jnp.where(allowed[None], raw_scores * score_scale, masked_score)


def expert_front(expert_rows, gate_matrix, up_matrix):
    gate_pre = jnp.dot(expert_rows, gate_matrix, preferred_element_type=jnp.float32)
    up_pre = jnp.dot(expert_rows, up_matrix, preferred_element_type=jnp.float32)
    activation = (jax.nn.silu(gate_pre) * up_pre).astype(jnp.bfloat16)
    return (gate_pre, up_pre, activation)


def line_depth(count):
    depth = 1
    while depth * depth * 4 <= count:
        depth *= 2
    return depth


def place_table(routes, order, me, expert_count, capacity):
    relabeled = routes ^ me
    ranks = order.reshape(routes.shape)
    labels = jnp.arange(expert_count, dtype=jnp.int32)
    hit = relabeled[:, :, None] == labels[None, None, :]
    routed = jnp.any(hit, axis=1)
    rank = jnp.sum(jnp.where(hit, ranks[:, :, None], 0), axis=1)
    rank = jnp.where(routed, rank, order.size)
    earlier = rank.T[:, None, :] < rank.T[:, :, None]
    place = jnp.sum(earlier.astype(jnp.int32), axis=-1)
    return jnp.where(routed.T & (place < capacity), place, -1)


class Exchange:
    def __init__(self, count):
        self.count = count
        self.depth = line_depth(count)
        self.width = count // self.depth
        self.me = lax.axis_index("expert")
        self.line = self.me // self.width
        self.short = self.depth == 4

    def send(self, rows, pairs):
        width = self.width
        flat = [(a * width + s, b * width + s) for a, b in pairs for s in range(width)]
        return lax.ppermute(rows, "expert", flat)

    def flip(self, rows, mask):
        return lax.ppermute(rows, "expert", [(d, d ^ mask) for d in range(self.count)])

    def spread(self, rows):
        if not self.short:
            slots, bit = [rows], 1
            while bit < self.depth:
                slots = slots + [self.flip(s, bit * self.width) for s in slots]
                bit *= 2
            return slots
        middle = (self.line == 1) | (self.line == 2)
        beside = self.send(rows, [(0, 1), (1, 0), (2, 3), (3, 2)])
        across = self.send(rows, [(1, 2), (2, 1)])
        inner = self.send(beside, [(1, 2), (2, 1)])
        outer = self.send(across, [(1, 0), (2, 3)])
        second = jnp.where(middle, inner, outer)
        far = self.send(second, [(1, 0), (2, 3)])
        return [rows, beside, second, jnp.where(middle, across, far)]

    def collect(self, parts):
        def low(v):
            return v.astype(jnp.bfloat16)

        def wide(v):
            return v.astype(jnp.float32)

        if not self.short:
            bit = self.depth // 2
            while bit >= 1:
                sent = [self.flip(low(p), bit * self.width) for p in parts[bit : 2 * bit]]
                parts = [wide(p) + wide(s) for p, s in zip(parts[:bit], sent)]
                bit //= 2
            return parts[0]
        own, beside, second, third = parts
        second = low(wide(second) + wide(self.send(low(third), [(0, 1), (3, 2)])))
        inner = self.send(second, [(1, 2), (2, 1)])
        outer = self.send(second, [(0, 1), (3, 2)])
        beside = low(wide(beside) + wide(inner))
        third = low(wide(third) + wide(outer))
        first = self.send(beside, [(0, 1), (1, 0), (2, 3), (3, 2)])
        other = self.send(third, [(1, 2), (2, 1)])
        return wide(own) + wide(first) + wide(other)

    def plane(self, blocks):
        return [blocks[0]] + [self.flip(blocks[b], b) for b in range(1, self.width)]

    def scatter_sum(self, grads):
        rows = grads.shape[0] // self.count
        held = grads.reshape(self.count, rows, grads.shape[1])
        blocks, bit = self.count, 1
        while bit < self.width:
            parted = held.reshape(blocks // 2, 2, rows, -1)
            side = (self.me // bit) % 2
            kept = lax.dynamic_index_in_dim(parted, side, 1, keepdims=False)
            gone = lax.dynamic_index_in_dim(parted, 1 - side, 1, keepdims=False)
            came = self.flip(gone.astype(jnp.bfloat16), bit)
            held = kept.astype(jnp.float32) + came.astype(jnp.float32)
            blocks, bit = blocks // 2, bit * 2
        parts = [
            lax.dynamic_index_in_dim(held, self.line ^ g, 0, keepdims=False)
            for g in range(self.depth)
        ]
        return self.collect(parts)


def swap(rows):
    return lax.ppermute(rows, "tensor", [(0, 1), (1, 0)])


def half_of(array, side):
    width = array.shape[-1] // 2
    return lax.dynamic_slice_in_dim(array, side * width, width, array.ndim - 1)


def join_halves(mine, other, side):
    first = jnp.where(side == 0, mine, other)
    last = jnp.where(side == 0, other, mine)
    return jnp.concatenate([first, last], axis=-1)


def on_device(
    tokens,
    cotangent,
    norm_gain,
    ffn_gain,
    w_query,
    w_key,
    w_value,
    w_out,
    w_router,
    w_gate,
    w_up,
    w_down,
    routes,
    order,
    segments,
):
    seq_length, model_width = tokens.shape
    expert_count = w_router.shape[1]
    pick_count = routes.shape[1]
    capacity = 9 * seq_length * pick_count // (8 * expert_count)
    head_width = w_key.shape[1]
    local_heads = w_query.shape[1] // head_width
    score_scale = 1.0 / math.sqrt(head_width)
    link = Exchange(expert_count)
    depth, width = link.depth, link.width
    side = lax.axis_index("tensor")
    slot_ids = jnp.arange(capacity, dtype=jnp.float32)

    placed = place_table(routes, order[0], link.me, expert_count, capacity).astype(jnp.float32)
    routes_t = routes.T.astype(jnp.float32)
    tables = []
    for g in range(depth):
        table = jnp.concatenate([placed[g * width : (g + 1) * width], routes_t], axis=0)
        tables.append(table if g == 0 else link.flip(table, g * width))
    selectors = [
        (table[:width, None, :] == slot_ids[None, :, None]).astype(jnp.bfloat16)
        for table in tables
    ]

    def pick_rows(g, rows):
        return jnp.einsum(
            "bst,td->bsd", selectors[g], rows, preferred_element_type=jnp.float32
        ).astype(jnp.bfloat16)

    def spread_rows(rows_half):
        arrived = []
        for g, slot in enumerate(link.spread(rows_half)):
            picked = pick_rows(g, slot)
            came = link.plane([picked[b] for b in range(width)])
            mine = jnp.concatenate(came, axis=0)
            arrived.append((mine, swap(mine)))
        return arrived

    cot_rows = spread_rows(half_of(cotangent, side))
    route_rows = []
    for g in range(depth):
        slots = pick_rows(g, tables[g][width:].T.astype(jnp.bfloat16))
        route_rows.append(jnp.concatenate(link.plane([slots[b] for b in range(width)]), axis=0))

    cosine_table, sine_table = rope_tables(seq_length, head_width)
    allowed = segments[0][None, :] <= segments[0][:, None]
    source = tokens.astype(jnp.float32)
    inverse_first = rms_scale(source)
    normed_first = source * inverse_first
    first_in = (normed_first * norm_gain).astype(jnp.bfloat16)
    query_pre = jnp.dot(first_in, w_query, preferred_element_type=jnp.float32).reshape(
        seq_length, local_heads, head_width
    )
    query = rotate(query_pre, cosine_table, sine_table).astype(jnp.bfloat16)
    key_pre = jnp.dot(first_in, w_key, preferred_element_type=jnp.float32)[:, None, :]
    keys = rotate(key_pre, cosine_table, sine_table)[:, 0, :].astype(jnp.bfloat16)
    values = jnp.dot(first_in, w_value, preferred_element_type=jnp.float32).astype(jnp.bfloat16)
    scores = attention_scores(query, keys, allowed, score_scale)
    log_total = jax.nn.logsumexp(scores, axis=-1, keepdims=True)
    weights = jnp.exp(scores - log_total).astype(jnp.bfloat16)
    mixed = jnp.einsum("hqk,kd->qhd", weights, values, preferred_element_type=jnp.float32)
    mixed = mixed.astype(jnp.bfloat16).reshape(seq_length, local_heads * head_width)
    branch = jnp.dot(mixed, w_out, preferred_element_type=jnp.float32).astype(jnp.bfloat16)
    hidden = source + (branch.astype(jnp.float32) + swap(branch).astype(jnp.float32))
    inverse_second = rms_scale(hidden)
    normed_second = hidden * inverse_second
    second_in = (normed_second * ffn_gain).astype(jnp.bfloat16)
    logits = jnp.dot(second_in, w_router, preferred_element_type=jnp.float32)
    picked = routes[:, :, None] == jnp.arange(expert_count, dtype=jnp.int32)[None, None, :]
    chosen = jnp.sum(jnp.where(picked, logits[:, None, :], 0.0), axis=-1)
    gate_weights = jax.nn.softmax(chosen, axis=-1)

    in_rows = spread_rows(half_of(second_in, side))

    def fold(matrix, axis):
        half = matrix.shape[axis] // 2
        return (
            lax.dynamic_slice_in_dim(matrix, side * half, half, axis),
            lax.dynamic_slice_in_dim(matrix, (1 - side) * half, half, axis),
        )

    gate_up = jnp.concatenate([w_gate[0], w_up[0]], axis=-1)
    unit_count = w_down.shape[1]
    front_mine, front_other = fold(gate_up, 0)
    down_mine, down_other = fold(w_down[0], 1)
    router_mine, router_other = fold(w_router, 0)
    expert_ids = jnp.arange(expert_count, dtype=jnp.bfloat16)
    gate_up_grad = jnp.zeros((2, model_width // 2, 2 * unit_count), jnp.float32)
    down_grad = jnp.zeros((2, unit_count, model_width // 2), jnp.float32)
    out_rows, back_rows, term_rows = [], [], []
    for g in range(depth):
        x_mine, x_other = in_rows[g]
        c_mine, c_other = cot_rows[g]

        def both(a, b, wa, wb):
            return jnp.dot(a, wa, preferred_element_type=jnp.float32) + jnp.dot(
                b, wb, preferred_element_type=jnp.float32
            )

        pre = both(x_mine, x_other, front_mine, front_other)
        row_logits = both(x_mine, x_other, router_mine, router_other)
        raw = times_transposed(c_mine, down_mine) + times_transposed(c_other, down_other)
        mask = jnp.any(route_rows[g][:, :, None] == expert_ids[None, None, :], axis=1)
        masked = jnp.where(mask, row_logits, masked_score)
        spread_out = jnp.exp(masked - jnp.max(masked, axis=-1, keepdims=True))
        chance = spread_out / jnp.sum(spread_out, axis=-1, keepdims=True)
        own = jnp.arange(expert_count, dtype=jnp.int32) == link.me
        gate = jnp.sum(jnp.where(own[None, :], chance, 0.0), axis=-1, keepdims=True)
        gate_pre, up_pre = pre[:, :unit_count], pre[:, unit_count:]
        sig = jax.nn.sigmoid(gate_pre)
        silu = gate_pre * sig
        act = silu * up_pre
        term_rows.append(jnp.sum(act * raw, axis=-1).reshape(width, capacity))
        act_gated = (act * gate).astype(jnp.bfloat16)
        d_act = raw * gate
        d_pre = jnp.concatenate(
            [d_act * up_pre * sig * (1.0 + gate_pre * (1.0 - sig)), d_act * silu], axis=-1
        ).astype(jnp.bfloat16)
        back_mine = times_transposed(d_pre, front_mine)
        back_other = times_transposed(d_pre, front_other).astype(jnp.bfloat16)
        out_mine = jnp.dot(act_gated, down_mine, preferred_element_type=jnp.float32)
        out_other = jnp.dot(act_gated, down_other, preferred_element_type=jnp.float32)
        back_rows.append((back_mine + swap(back_other).astype(jnp.float32)).astype(jnp.bfloat16))
        out_rows.append(
            (out_mine + swap(out_other.astype(jnp.bfloat16)).astype(jnp.float32)).astype(
                jnp.bfloat16
            )
        )
        gate_up_grad += jnp.stack([contract_rows(x_mine, d_pre), contract_rows(x_other, d_pre)])
        down_grad += jnp.stack(
            [contract_rows(act_gated, c_mine), contract_rows(act_gated, c_other)]
        )
    gate_up_grad = jnp.where(side == 0, gate_up_grad, gate_up_grad[::-1])
    gate_up_grad = gate_up_grad.reshape(1, model_width, 2 * unit_count)
    gate_grad, up_grad = gate_up_grad[..., :unit_count], gate_up_grad[..., unit_count:]
    down_grad = join_halves(down_grad[0], down_grad[1], side)[None]

    def gather_back(rows):
        parts = [None] * depth
        for g in reversed(range(depth)):
            blocks = rows[g].reshape(width, capacity, model_width // 2)
            came = jnp.stack(link.plane([blocks[b] for b in range(width)]))
            parts[g] = jnp.einsum(
                "bst,bsd->td", selectors[g], came, preferred_element_type=jnp.float32
            )
        return link.collect(parts)

    terms = jnp.stack(link.plane([jnp.stack([t[b] for t in term_rows]) for b in range(width)]), 1)
    tables_back = []
    for g in range(depth):
        local = jnp.sum(
            jnp.where(selectors[g] > 0, terms[g][:, :, None], 0.0), axis=1
        )
        tables_back.append(local if g == 0 else link.flip(local, g * width))
    term_table = jnp.concatenate(tables_back, axis=0)
    term_table = term_table + swap(term_table)
    labels = jnp.arange(expert_count, dtype=jnp.int32)
    relabeled = (routes ^ link.me)[:, :, None] == labels[None, None, :]
    gate_total = jnp.sum(jnp.where(relabeled, term_table.T[:, None, :], 0.0), axis=-1)

    row_half = gather_back(back_rows).astype(jnp.bfloat16)
    row_total = join_halves(row_half, swap(row_half), side).astype(jnp.float32)
    combined = gather_back(out_rows)
    output_half = (half_of(hidden, side) + combined).astype(jnp.bfloat16)
    output = join_halves(output_half, swap(output_half), side)

    upstream = cotangent.astype(jnp.float32)
    d_chosen = gate_weights * (
        gate_total - jnp.sum(gate_weights * gate_total, axis=-1, keepdims=True)
    )
    d_logits = jnp.sum(jnp.where(picked, d_chosen[:, :, None], 0.0), axis=1).astype(jnp.bfloat16)
    router_grad = contract_rows(second_in, d_logits)
    d_second = row_total + times_transposed(d_logits, w_router)
    scaled_second = d_second * ffn_gain
    ffn_gain_grad = jnp.sum(d_second * normed_second, axis=0)
    d_hidden = upstream + inverse_second * (
        scaled_second
        - normed_second * jnp.mean(scaled_second * normed_second, axis=-1, keepdims=True)
    )
    d_branch = d_hidden.astype(jnp.bfloat16)
    small = jnp.concatenate([router_grad, ffn_gain_grad[:, None]], axis=1)
    small = lax.psum_scatter(small, "expert", scatter_dimension=0, tiled=True)
    out_grad = link.scatter_sum(contract_rows(d_branch, mixed)).T
    d_mixed = (
        times_transposed(d_branch, w_out)
        .astype(jnp.bfloat16)
        .reshape(seq_length, local_heads, head_width)
    )
    scores = attention_scores(query, keys, allowed, score_scale)
    probs = jnp.exp(scores - log_total)
    d_probs = jnp.einsum("qhd,kd->hqk", d_mixed, values, preferred_element_type=jnp.float32)
    row_dot = jnp.sum(probs * d_probs, axis=-1, keepdims=True)
    d_scores = (score_scale * probs * (d_probs - row_dot)).astype(jnp.bfloat16)
    d_query_turned = jnp.einsum("hqk,kd->qhd", d_scores, keys, preferred_element_type=jnp.float32)
    d_keys_turned = jnp.einsum("hqk,qhd->kd", d_scores, query, preferred_element_type=jnp.float32)
    d_values = jnp.einsum(
        "hqk,qhd->kd", probs.astype(jnp.bfloat16), d_mixed, preferred_element_type=jnp.float32
    ).astype(jnp.bfloat16)
    d_query = (
        rotate_back(d_query_turned, cosine_table, sine_table)
        .astype(jnp.bfloat16)
        .reshape(seq_length, local_heads * head_width)
    )
    d_keys = rotate_back(d_keys_turned[:, None, :], cosine_table, sine_table)[:, 0, :].astype(
        jnp.bfloat16
    )
    d_all = jnp.concatenate([d_query, d_keys, d_values], axis=1)
    w_all = jnp.concatenate([w_query, w_key, w_value], axis=1)
    d_first = times_transposed(d_all, w_all).astype(jnp.bfloat16)
    qkv_grad = link.scatter_sum(contract_rows(first_in, d_all))
    d_first = d_first.astype(jnp.float32) + swap(d_first).astype(jnp.float32)
    scaled_first = d_first * norm_gain
    input_grad = d_hidden + inverse_first * (
        scaled_first - normed_first * jnp.mean(scaled_first * normed_first, axis=-1, keepdims=True)
    )
    rows = model_width // expert_count
    w_mine = lax.dynamic_slice_in_dim(w_all, link.me * rows, rows, 0).astype(jnp.float32)
    gain_mine = lax.dynamic_slice_in_dim(norm_gain, link.me * rows, rows, 0)
    gain_part = jnp.sum(qkv_grad * w_mine, axis=1) / gain_mine
    norm_gain_grad = gain_part + swap(gain_part)
    span = local_heads * head_width
    return (
        output,
        input_grad,
        norm_gain_grad,
        small[:, expert_count],
        qkv_grad[:, :span],
        qkv_grad[:, span : span + head_width],
        qkv_grad[:, span + head_width :],
        out_grad,
        small[:, :expert_count],
        gate_grad,
        up_grad,
        down_grad,
    )


def solution(mesh):
    placed = (
        P("expert", None),
        P("expert", None),
        P(),
        P(),
        P(None, "tensor"),
        P(None, "tensor"),
        P(None, "tensor"),
        P("tensor", None),
        P(),
        P("expert", None, "tensor"),
        P("expert", None, "tensor"),
        P("expert", "tensor", None),
        P("expert", None),
        P("expert", None),
        P("expert", None),
    )
    return jax.shard_map(
        on_device,
        mesh=mesh,
        in_specs=placed,
        out_specs=(
            P("expert", None),
            P("expert", None),
            P("expert"),
            P("expert"),
            P("expert", "tensor"),
            P("expert", "tensor"),
            P("expert", "tensor"),
            P("tensor", "expert"),
            P("expert", None),
            P("expert", None, "tensor"),
            P("expert", None, "tensor"),
            P("expert", "tensor", None),
        ),
        check_vma=False,
    )
```

```python
import functools
import math

import jax
import jax.numpy as jnp
import numpy as np
from jax import lax
from jax.experimental import pallas as pl
from jax.experimental.pallas import tpu as pltpu
from jax.sharding import PartitionSpec as P

epsilon = 1e-06
rope_base = 1000000.0
masked_score = -1e30


def contract_rows(left, right):
    return lax.dot_general(
        left, right, (((0,), (0,)), ((), ())), preferred_element_type=jnp.float32
    )


def times_transposed(left, right):
    return lax.dot_general(
        left, right, (((1,), (1,)), ((), ())), preferred_element_type=jnp.float32
    )


def line_depth(count):
    depth = 1
    while depth * depth * 4 <= count:
        depth *= 2
    return depth


VMEM_LIMIT = 56 * 1024 * 1024


def kernel_params(*semantics):
    return pltpu.CompilerParams(vmem_limit_bytes=VMEM_LIMIT)


def lasting(microseconds):
    return pl.CostEstimate(
        flops=int(microseconds * 1.0e9), bytes_accessed=1024, transcendentals=0
    )


def whole(array):
    return pl.BlockSpec(array.shape, lambda *_: (0,) * array.ndim)


def anywhere(arrays):
    return [pl.BlockSpec(memory_space=pl.ANY)] * len(arrays)


SCALAR = pl.BlockSpec(memory_space=pltpu.SMEM)


def dot(left, right, left_axis=1, right_axis=0):
    return lax.dot_general(
        left,
        right,
        (((left_axis,), (right_axis,)), ((), ())),
        preferred_element_type=jnp.float32,
    )


def rope_constants(seq_length, head_width):
    half = head_width // 2
    frequency = np.exp(-math.log(rope_base) * np.arange(half) * (2.0 / head_width))
    angle = np.arange(seq_length)[:, None] * frequency[None, :]
    cosine, sine = np.cos(angle), np.sin(angle)
    return (
        np.concatenate([cosine, cosine], axis=1).astype(np.float32),
        np.concatenate([-sine, sine], axis=1).astype(np.float32),
    )


def place_kernel(seq_length, capacity, keys_ref, out_ref):
    block = keys_ref[...]
    columns = block.T
    limit = seq_length * 1024
    for row in range(block.shape[0]):
        mine = block[row : row + 1, :]
        total = jnp.zeros((1, seq_length), jnp.float32)
        for start in range(0, seq_length, 256):
            less = columns[start : start + 256, row : row + 1] < mine
            total = total + jnp.sum(jnp.where(less, 1.0, 0.0), axis=0, keepdims=True)
        kept = (mine < limit) & (total < capacity)
        out_ref[row : row + 1, :] = jnp.where(kept, total, -1.0).astype(jnp.int32)


def place_table(routes, order, me, expert_count, capacity):
    seq_length = routes.shape[0]
    relabeled = (routes ^ me).T
    ranks = order.reshape(routes.shape).T
    labels = jnp.arange(expert_count, dtype=jnp.int32)
    hit = relabeled[:, None, :] == labels[None, :, None]
    rank = jnp.sum(jnp.where(hit, ranks[:, None, :] + 1, 0), axis=0)
    rank = jnp.where(rank > 0, rank, seq_length * 1024)
    spec = pl.BlockSpec((8, seq_length), lambda e: (e, 0))
    return pl.pallas_call(
        functools.partial(place_kernel, seq_length, capacity),
        grid=(expert_count // 8,),
        out_shape=jax.ShapeDtypeStruct(rank.shape, jnp.int32),
        in_specs=[spec],
        out_specs=spec,
        compiler_params=kernel_params(),
        cost_estimate=lasting(9.0 * expert_count / 16),
    )(rank)


def turn(values, cosine, sine):
    return values * cosine + pltpu.roll(values, values.shape[1] // 2, 1) * sine


def project_kernel(
    heads, x_ref, gain_ref, wq_ref, wk_ref, wv_ref, cos_ref, sin_ref, in_ref, q_ref, k_ref, v_ref, inv_ref
):
    source = x_ref[...].astype(jnp.float32)
    inverse = lax.rsqrt(jnp.mean(source * source, axis=1, keepdims=True) + epsilon)
    first = (source * inverse * gain_ref[...]).astype(jnp.bfloat16)
    in_ref[...] = first
    inv_ref[...] = inverse
    cosine, sine = cos_ref[...], sin_ref[...]
    size = cosine.shape[1]
    query = dot(first, wq_ref[...])
    for head in range(heads):
        span = slice(head * size, (head + 1) * size)
        q_ref[:, span] = turn(query[:, span], cosine, sine).astype(jnp.bfloat16)
    k_ref[...] = turn(dot(first, wk_ref[...]), cosine, sine).astype(jnp.bfloat16)
    v_ref[...] = dot(first, wv_ref[...]).astype(jnp.bfloat16)


def project(tokens, gain, w_query, w_key, w_value, cosine, sine, tile):
    length, model = tokens.shape
    size = w_key.shape[1]
    span = w_query.shape[1]

    def rows(columns):
        return pl.BlockSpec((tile, columns), lambda i: (i, 0))

    def shape(columns, kind=jnp.bfloat16):
        return jax.ShapeDtypeStruct((length, columns), kind)

    return pl.pallas_call(
        functools.partial(project_kernel, span // size),
        grid=(length // tile,),
        in_specs=[
            rows(model),
            whole(gain),
            whole(w_query),
            whole(w_key),
            whole(w_value),
            rows(size),
            rows(size),
        ],
        out_specs=[rows(model), rows(span), rows(size), rows(size), rows(1)],
        out_shape=[shape(model), shape(span), shape(size), shape(size), shape(1, jnp.float32)],
        compiler_params=kernel_params(),
        cost_estimate=lasting(9.0),
    )(tokens, gain, w_query, w_key, w_value, cosine, sine)


def attend_kernel(
    heads, scale, q_ref, k_ref, v_ref, segq_ref, segk_ref, wo_ref, mix_ref, lse_ref, branch_ref
):
    allowed = segk_ref[...] <= segq_ref[...]
    keys = k_ref[...]
    values = v_ref[...].T
    size = keys.shape[1]
    for head in range(heads):
        span = slice(head * size, (head + 1) * size)
        scores = dot(keys, q_ref[:, span], 1, 1)
        scores = jnp.where(allowed, scores * scale, masked_score)
        top = jnp.max(scores, axis=0, keepdims=True)
        spread = jnp.exp(scores - top)
        total = jnp.sum(spread, axis=0, keepdims=True)
        mixed = dot(values, spread.astype(jnp.bfloat16)) / total
        mix_ref[:, span] = mixed.T.astype(jnp.bfloat16)
        lse_ref[head : head + 1, :] = top + jnp.log(total)
    branch_ref[...] = dot(mix_ref[...], wo_ref[...]).astype(jnp.bfloat16)


def attend(query, keys, values, seg_row, seg_col, w_out, scale, tile):
    length, span = query.shape
    size = keys.shape[1]
    heads = span // size
    model = w_out.shape[1]
    rows = pl.BlockSpec((tile, span), lambda i: (i, 0))
    return pl.pallas_call(
        functools.partial(attend_kernel, heads, scale),
        grid=(length // tile,),
        in_specs=[
            rows,
            whole(keys),
            whole(values),
            pl.BlockSpec((1, tile), lambda i: (0, i)),
            whole(seg_col),
            whole(w_out),
        ],
        out_specs=[
            rows,
            pl.BlockSpec((heads, tile), lambda i: (0, i)),
            pl.BlockSpec((tile, model), lambda i: (i, 0)),
        ],
        out_shape=[
            jax.ShapeDtypeStruct((length, span), jnp.bfloat16),
            jax.ShapeDtypeStruct((heads, length), jnp.float32),
            jax.ShapeDtypeStruct((length, model), jnp.bfloat16),
        ],
        compiler_params=kernel_params(),
        cost_estimate=lasting(20.0),
    )(query, keys, values, seg_row, seg_col, w_out)


def second_kernel(
    side_ref, x_ref, a_ref, b_ref, gain_ref, router_ref, routes_ref, *refs
):
    hidden_ref, in_ref, half_ref, inv_ref, gate_ref = refs[-5:]
    hidden = x_ref[...].astype(jnp.float32) + (
        a_ref[...].astype(jnp.float32) + b_ref[...].astype(jnp.float32)
    )
    inverse = lax.rsqrt(jnp.mean(hidden * hidden, axis=1, keepdims=True) + epsilon)
    second = (hidden * inverse * gain_ref[...]).astype(jnp.bfloat16)
    hidden_ref[...] = hidden
    in_ref[...] = second
    inv_ref[...] = inverse
    half = half_ref.shape[1]
    half_ref[...] = jnp.where(side_ref[0] == 0, second[:, :half], second[:, half:])
    logits = dot(second, router_ref[...])
    gate_ref[...] = routed_softmax(logits, routes_ref[...])


def routed_softmax(logits, routes):
    labels = lax.broadcasted_iota(jnp.int32, logits.shape, 1)
    picked = routes[:, 0:1] == labels
    for k in range(1, routes.shape[1]):
        picked = picked | (routes[:, k : k + 1] == labels)
    masked = jnp.where(picked, logits, masked_score)
    spread = jnp.exp(masked - jnp.max(masked, axis=1, keepdims=True))
    return spread / jnp.sum(spread, axis=1, keepdims=True)


def second_norm(side, tokens, mine, other, gain, router, routes, tile, earlier):
    length, model = tokens.shape
    count = router.shape[1]

    def rows(columns):
        return pl.BlockSpec((tile, columns), lambda i: (i, 0))

    def shape(columns, kind=jnp.float32):
        return jax.ShapeDtypeStruct((length, columns), kind)

    return pl.pallas_call(
        second_kernel,
        grid=(length // tile,),
        in_specs=[
            SCALAR,
            rows(model),
            rows(model),
            rows(model),
            whole(gain),
            whole(router),
            rows(routes.shape[1]),
        ]
        + anywhere(earlier),
        out_specs=[rows(model), rows(model), rows(model // 2), rows(1), rows(count)],
        out_shape=[
            shape(model),
            shape(model, jnp.bfloat16),
            shape(model // 2, jnp.bfloat16),
            shape(1),
            shape(count),
        ],
        compiler_params=kernel_params(),
        cost_estimate=lasting(9.0),
    )(side, tokens, mine, other, gain, router, routes, *earlier)


def chosen_slots(place_row, capacity):
    slot = lax.broadcasted_iota(jnp.int32, (capacity, place_row.shape[1]), 0)
    return jnp.where(place_row == slot, 1.0, 0.0).astype(jnp.bfloat16)


def pick_kernel(width, capacity, outputs, line_ref, tab_ref, slot_ref, *refs):
    outs = refs[len(refs) - outputs :]
    chosen = jnp.concatenate([chosen_slots(tab_ref[0, b], capacity) for b in range(width)])

    def give(rows, targets):
        for b in range(width):
            targets[b][0] = rows[b * capacity : (b + 1) * capacity].astype(jnp.bfloat16)

    give(dot(chosen, slot_ref[0]), outs[:width])
    if len(outs) > width:
        give(dot(chosen, refs[0][0]), outs[width:])


def pick_rows(line, tables, slots, capacity, small=None, earlier=()):
    count, width, _, length = tables.shape
    columns = slots.shape[2]
    if capacity % 16:
        slot = jnp.arange(capacity, dtype=jnp.int32)
        chosen = low(tables == slot[None, None, :, None])

        def taken(rows):
            picked = jnp.einsum("gbst,gtd->bgsd", chosen, rows, preferred_element_type=jnp.float32)
            return [low(picked[b]) for b in range(width)]

        near = slots[jnp.arange(count, dtype=jnp.int32) ^ line[0]]
        return taken(near) + ([] if small is None else taken(small))
    in_specs = [
        pl.BlockSpec((1, width, 1, length), lambda g, line: (g, 0, 0, 0)),
        pl.BlockSpec((1, length, columns), lambda g, line: (g ^ line[0], 0, 0)),
    ]
    out_specs = [pl.BlockSpec((1, capacity, columns), lambda g, line: (g, 0, 0))] * width
    out_shape = [jax.ShapeDtypeStruct((count, capacity, columns), jnp.bfloat16)] * width
    operands = [tables, slots]
    if small is not None:
        picks = small.shape[2]
        in_specs.append(pl.BlockSpec((1, length, picks), lambda g, line: (g, 0, 0)))
        out_specs += [pl.BlockSpec((1, capacity, picks), lambda g, line: (g, 0, 0))] * width
        out_shape += [jax.ShapeDtypeStruct((count, capacity, picks), jnp.bfloat16)] * width
        operands.append(small)
    return pl.pallas_call(
        functools.partial(pick_kernel, width, capacity, len(out_shape)),
        grid_spec=pltpu.PrefetchScalarGridSpec(
            num_scalar_prefetch=1,
            grid=(count,),
            in_specs=in_specs + anywhere(earlier),
            out_specs=out_specs,
        ),
        out_shape=out_shape,
        compiler_params=kernel_params(),
        cost_estimate=lasting(3.0 * count * columns / 768),
    )(line, *operands, *earlier)


def combine_kernel(width, capacity, line_ref, tab_ref, *refs):
    out_ref = refs[-1]
    places = tab_ref[0]
    slot = lax.broadcasted_iota(jnp.int32, (places.shape[0], capacity), 1)
    total = None
    for b in range(width):
        chosen = jnp.where(places[:, b : b + 1] == slot, 1.0, 0.0).astype(jnp.bfloat16)
        part = dot(chosen, refs[b][0])
        total = part if total is None else total + part
    out_ref[0] = total.astype(out_ref.dtype)


def combine(line, table_columns, came, earlier=()):
    count, length, width = table_columns.shape
    _, capacity, columns = came[0].shape
    if capacity % 16:
        slot = jnp.arange(capacity, dtype=jnp.int32)
        chosen = low(table_columns[:, :, :, None] == slot)
        rows = jnp.stack(came)
        total = jnp.einsum("gtbs,bgsd->gtd", chosen, rows, preferred_element_type=jnp.float32)
        return low(total[jnp.arange(count, dtype=jnp.int32) ^ line[0]])
    return pl.pallas_call(
        functools.partial(combine_kernel, width, capacity),
        grid_spec=pltpu.PrefetchScalarGridSpec(
            num_scalar_prefetch=1,
            grid=(count,),
            in_specs=[pl.BlockSpec((1, length, width), lambda g, line: (g, 0, 0))]
            + [pl.BlockSpec((1, capacity, columns), lambda g, line: (g, 0, 0))] * width
            + anywhere(earlier),
            out_specs=pl.BlockSpec((1, length, columns), lambda g, line: (g ^ line[0], 0, 0)),
        ),
        out_shape=jax.ShapeDtypeStruct((count, length, columns), jnp.bfloat16),
        compiler_params=kernel_params(),
        cost_estimate=lasting(4.0 * count * columns / 768),
    )(line, table_columns, *came, *earlier)


def expert_kernel(chunks, width, me_ref, *refs):
    x_refs = refs[: 2 * chunks]
    cm_ref, co_ref, route_ref, wg_ref, wu_ref, wd_ref, wr_ref, *outs = refs[2 * chunks :]
    pre_ref, act_ref, term_ref = outs[:3]
    aways = outs[3 : 3 + chunks]
    homes = outs[3 + chunks :]
    side = me_ref[1]
    batch, _, capacity, half = cm_ref.shape
    chunk = half // chunks

    def flat(ref):
        return ref[...].reshape(batch * capacity, ref.shape[3])

    def keep(ref, rows):
        ref[...] = rows.reshape(ref.shape).astype(ref.dtype)

    def columns(which, part, size):
        start = which * half + part * size
        return pl.ds(pl.multiple_of(start, size), size)

    mine, other = columns(side, 0, half), columns(1 - side, 0, half)
    spans = [columns(side, c, chunk) for c in range(chunks)]
    spans += [columns(1 - side, c, chunk) for c in range(chunks)]
    pieces = [flat(ref) for ref in x_refs]

    def through(weight_ref):
        total = None
        for piece, at in zip(pieces, spans):
            part = dot(piece, weight_ref[at, :])
            total = part if total is None else total + part
        return total

    gate_pre, up_pre, logits = through(wg_ref), through(wu_ref), through(wr_ref)
    raw = dot(flat(cm_ref), wd_ref[:, mine], 1, 1) + dot(flat(co_ref), wd_ref[:, other], 1, 1)
    chance = routed_softmax(logits, flat(route_ref).astype(jnp.float32).astype(jnp.int32))
    label = lax.broadcasted_iota(jnp.int32, chance.shape, 1)
    gate = jnp.sum(jnp.where(label == me_ref[0], chance, 0.0), axis=1, keepdims=True)
    sig = jax.nn.sigmoid(gate_pre)
    silu = gate_pre * sig
    act = silu * up_pre
    keep(term_ref, jnp.sum(act * raw, axis=1, keepdims=True))
    keep(act_ref, act * gate)
    d_act = raw * gate
    units = act.shape[1]
    d_gate = (d_act * up_pre * sig * (1.0 + gate_pre * (1.0 - sig))).astype(jnp.bfloat16)
    d_up = (d_act * silu).astype(jnp.bfloat16)
    pre_ref[:, :, :, :units] = d_gate.reshape(batch, 1, capacity, units)
    pre_ref[:, :, :, units:] = d_up.reshape(batch, 1, capacity, units)
    for c in range(chunks):
        at = spans[chunks + c]
        keep(aways[c], dot(d_gate, wg_ref[at, :], 1, 1) + dot(d_up, wu_ref[at, :], 1, 1))
        at = spans[c]
        home = dot(d_gate, wg_ref[at, :], 1, 1) + dot(d_up, wu_ref[at, :], 1, 1)
        home = home.astype(jnp.bfloat16).reshape(batch, capacity, chunk)
        give_homes(home, homes[c * width : (c + 1) * width])


def give_homes(rows, homes):
    batch = rows.shape[0]
    for b in range(len(homes)):

        @pl.when(pl.program_id(0) == b // batch)
        def _(b=b):
            homes[b][0] = rows[b % batch]


def block_batch(width, capacity):
    return 1 if capacity % 16 else min(2, width)


def home_specs(width, batch, count, capacity, columns):
    return [
        pl.BlockSpec((1, capacity, columns), functools.partial(home_block, k // batch, count))
        for k in range(width)
    ]


def expert_rows(me, pieces, c_mine, c_other, routes, w_gate, w_up, w_down, router):
    chunks = len(pieces) // 2
    width, count, capacity, chunk = pieces[0].shape
    half = c_mine.shape[3]
    units = w_gate.shape[1]
    batch = block_batch(width, capacity)

    def rows(columns):
        return pl.BlockSpec((batch, 1, capacity, columns), lambda b, g: (b, g, 0, 0))

    def shape(columns, kind=jnp.bfloat16):
        return jax.ShapeDtypeStruct((width, count, capacity, columns), kind)

    outs = pl.pallas_call(
        functools.partial(expert_kernel, chunks, width),
        grid=(width // batch, count),
        in_specs=[SCALAR]
        + [rows(chunk)] * (2 * chunks)
        + [
            rows(half),
            rows(half),
            rows(routes.shape[3]),
            whole(w_gate),
            whole(w_up),
            whole(w_down),
            whole(router),
        ],
        out_specs=[rows(2 * units), rows(units), rows(1)]
        + [rows(chunk)] * chunks
        + home_specs(width, batch, count, capacity, chunk) * chunks,
        out_shape=[shape(2 * units), shape(units), shape(1, jnp.float32)]
        + [shape(chunk)] * chunks
        + [jax.ShapeDtypeStruct((count, capacity, chunk), jnp.bfloat16)] * (width * chunks),
        compiler_params=kernel_params(),
        cost_estimate=lasting(10.0 * count),
    )(me, *pieces, c_mine, c_other, routes, w_gate, w_up, w_down, router)
    aways, homes = outs[3 : 3 + chunks], outs[3 + chunks :]
    return (
        *outs[:3],
        [(aways[c], homes[c * width : (c + 1) * width]) for c in range(chunks)],
    )


def home_block(k, count, b, g):
    return (jnp.where(b < k, 0, jnp.where(b > k, count - 1, g)), 0, 0)


def down_kernel(width, me_ref, act_ref, wd_ref, *refs):
    outs = refs[-1 - width :]
    away_ref, homes = outs[0], outs[1:]
    side = me_ref[1]
    batch, _, capacity, half = away_ref.shape
    mine = pl.ds(pl.multiple_of(side * half, half), half)
    other = pl.ds(pl.multiple_of((1 - side) * half, half), half)
    act = act_ref[...].reshape(batch * capacity, act_ref.shape[3])
    away_ref[...] = low(dot(act, wd_ref[:, other])).reshape(away_ref.shape)
    give_homes(low(dot(act, wd_ref[:, mine])).reshape(batch, capacity, half), homes)


def down_rows(me, act, w_down, earlier):
    width, count, capacity, units = act.shape
    half = w_down.shape[1] // 2
    batch = block_batch(width, capacity)

    def rows(columns):
        return pl.BlockSpec((batch, 1, capacity, columns), lambda b, g: (b, g, 0, 0))

    return pl.pallas_call(
        functools.partial(down_kernel, width),
        grid=(width // batch, count),
        in_specs=[SCALAR, rows(units), whole(w_down)] + anywhere(earlier),
        out_specs=[rows(half)] + home_specs(width, batch, count, capacity, half),
        out_shape=[jax.ShapeDtypeStruct((width, count, capacity, half), jnp.bfloat16)]
        + [jax.ShapeDtypeStruct((count, capacity, half), jnp.bfloat16)] * width,
        compiler_params=kernel_params(),
        cost_estimate=lasting(3.0 * count),
    )(me, act, w_down, *earlier)


def attend_back_kernel(
    heads,
    scale,
    tile,
    q_ref,
    k_ref,
    v_ref,
    segq_ref,
    segk_ref,
    lse_ref,
    db_ref,
    wo_ref,
    cos_ref,
    sin_ref,
    *refs,
):
    out_ref, dk_ref, dv_ref = refs[-3:]
    step = pl.program_id(0)
    allowed = segk_ref[...] <= segq_ref[...]
    keys = k_ref[...]
    values = v_ref[...]
    size = keys.shape[1]
    here = pl.ds(pl.multiple_of(step * tile, tile), tile)
    cosine, sine = cos_ref[here, :], sin_ref[here, :]
    keys_t = keys.T
    d_mixed = dot(db_ref[...], wo_ref[...], 1, 1).astype(jnp.bfloat16)
    dk_total = jnp.zeros(keys.shape, jnp.float32)
    dv_total = jnp.zeros(keys.shape, jnp.float32)
    for head in range(heads):
        span = slice(head * size, (head + 1) * size)
        query = q_ref[:, span]
        d_head = d_mixed[:, span]
        scores = dot(keys, query, 1, 1) * scale - lse_ref[head : head + 1, :]
        probs = jnp.where(allowed, jnp.exp(scores), 0.0)
        d_probs = dot(values, d_head, 1, 1)
        scaled = probs * d_probs
        row_dot = jnp.sum(scaled, axis=0, keepdims=True)
        d_scores = (scale * (scaled - probs * row_dot)).astype(jnp.bfloat16)
        dv_total = dv_total + dot(probs.astype(jnp.bfloat16), d_head)
        dk_total = dk_total + dot(d_scores, query)
        d_query = dot(keys_t, d_scores).T
        out_ref[here, span] = turn(d_query, cosine, -sine).astype(jnp.bfloat16)

    @pl.when(step == 0)
    def _():
        dk_ref[...] = dk_total
        dv_ref[...] = dv_total

    @pl.when(step > 0)
    def _():
        dk_ref[...] += dk_total
        dv_ref[...] += dv_total

    @pl.when(step == pl.num_programs(0) - 1)
    def _():
        base = heads * size
        turned = turn(dk_ref[...], cos_ref[...], -sin_ref[...])
        out_ref[:, base : base + size] = turned.astype(jnp.bfloat16)
        out_ref[:, base + size : base + 2 * size] = dv_ref[...].astype(jnp.bfloat16)


def attend_back(
    query, keys, values, seg_row, seg_col, lse, d_branch, w_out, cosine, sine, scale, tile, earlier
):
    length, span = query.shape
    size = keys.shape[1]
    heads = span // size
    model = w_out.shape[1]
    out = jax.ShapeDtypeStruct((length, span + 2 * size), jnp.bfloat16)
    return pl.pallas_call(
        functools.partial(attend_back_kernel, heads, scale, tile),
        grid=(length // tile,),
        in_specs=[
            pl.BlockSpec((tile, span), lambda i: (i, 0)),
            whole(keys),
            whole(values),
            pl.BlockSpec((1, tile), lambda i: (0, i)),
            whole(seg_col),
            pl.BlockSpec((heads, tile), lambda i: (0, i)),
            pl.BlockSpec((tile, model), lambda i: (i, 0)),
            whole(w_out),
            whole(cosine),
            whole(sine),
        ]
        + anywhere(earlier),
        out_specs=whole(out),
        out_shape=out,
        scratch_shapes=[pltpu.VMEM((length, size), jnp.float32)] * 2,
        compiler_params=kernel_params(),
        cost_estimate=lasting(28.0),
    )(query, keys, values, seg_row, seg_col, lse, d_branch, w_out, cosine, sine, *earlier)


def first_grad_kernel(d_ref, wq_ref, wk_ref, wv_ref, *refs):
    out_ref = refs[-1]
    span, size = wq_ref.shape[1], wk_ref.shape[1]
    total = dot(d_ref[:, :span], wq_ref[...], 1, 1)
    total = total + dot(d_ref[:, span : span + size], wk_ref[...], 1, 1)
    total = total + dot(d_ref[:, span + size :], wv_ref[...], 1, 1)
    out_ref[...] = total.astype(jnp.bfloat16)


def first_grad(d_all, w_query, w_key, w_value, tile, earlier):
    length, columns = d_all.shape
    model = w_query.shape[0]
    return pl.pallas_call(
        first_grad_kernel,
        grid=(length // tile,),
        in_specs=[
            pl.BlockSpec((tile, columns), lambda i: (i, 0)),
            whole(w_query),
            whole(w_key),
            whole(w_value),
        ]
        + anywhere(earlier),
        out_specs=pl.BlockSpec((tile, model), lambda i: (i, 0)),
        out_shape=jax.ShapeDtypeStruct((length, model), jnp.bfloat16),
        compiler_params=kernel_params(),
        cost_estimate=lasting(8.0),
    )(d_all, w_query, w_key, w_value, *earlier)


class Exchange:
    def __init__(self, count):
        self.count = count
        self.depth = line_depth(count)
        self.width = count // self.depth
        self.me = lax.axis_index("expert")
        self.line = self.me // self.width
        self.lines = [[l * self.width + s for l in range(self.depth)] for s in range(self.width)]

    def flip(self, rows, mask):
        return lax.ppermute(rows, "expert", [(d, d ^ mask) for d in range(self.count)])

    def spread(self, rows):
        return lax.all_gather(rows, "expert", axis_index_groups=self.lines)

    def collect(self, parts):
        flat = parts.reshape(-1, parts.shape[-1])
        return lax.psum_scatter(
            flat, "expert", scatter_dimension=0, axis_index_groups=self.lines, tiled=True
        )

    def plane(self, blocks):
        return [blocks[0]] + [self.flip(blocks[b], b) for b in range(1, self.width)]

    def scatter_sum(self, grads):
        rows = grads.shape[0] // self.count
        held = grads.reshape(self.count, rows, grads.shape[1])
        blocks, bit = self.count, 1
        while bit < self.width:
            parted = held.reshape(blocks // 2, 2, rows, -1)
            side = (self.me // bit) % 2
            kept = lax.dynamic_index_in_dim(parted, side, 1, keepdims=False)
            gone = lax.dynamic_index_in_dim(parted, 1 - side, 1, keepdims=False)
            came = self.flip(gone.astype(jnp.bfloat16), bit)
            held = kept.astype(jnp.float32) + came.astype(jnp.float32)
            blocks, bit = blocks // 2, bit * 2
        total = lax.dynamic_index_in_dim(held, self.line, 0, keepdims=False)
        for g in range(1, self.depth):
            part = lax.dynamic_index_in_dim(held, self.line ^ g, 0, keepdims=False)
            total = total + wide(self.flip(low(part), g * self.width))
        return total


def low(array):
    return array.astype(jnp.bfloat16)


def wide(array):
    return array.astype(jnp.float32)


def swap(rows):
    return lax.ppermute(rows, "tensor", [(0, 1), (1, 0)])


def half_of(array, side):
    width = array.shape[-1] // 2
    return lax.dynamic_slice_in_dim(array, side * width, width, array.ndim - 1)


def join_halves(mine, other, side):
    first = jnp.where(side == 0, mine, other)
    last = jnp.where(side == 0, other, mine)
    return jnp.concatenate([first, last], axis=-1)


def on_device(
    tokens,
    cotangent,
    norm_gain,
    ffn_gain,
    w_query,
    w_key,
    w_value,
    w_out,
    w_router,
    w_gate,
    w_up,
    w_down,
    routes,
    order,
    segments,
):
    seq_length, model_width = tokens.shape
    half_width = model_width // 2
    expert_count = w_router.shape[1]
    pick_count = routes.shape[1]
    capacity = 9 * seq_length * pick_count // (8 * expert_count)
    head_width = w_key.shape[1]
    span = w_query.shape[1]
    unit_count = w_down.shape[1]
    score_scale = 1.0 / math.sqrt(head_width)
    tile = 256
    link = Exchange(expert_count)
    depth, width = link.depth, link.width
    chunks = 2
    chunk_width = half_width // chunks
    side = lax.axis_index("tensor")
    side_ref = side.astype(jnp.int32)[None]
    me_ref = jnp.stack([link.me, side]).astype(jnp.int32)
    line_ref = link.line.astype(jnp.int32)[None]

    cot_slots = link.spread(half_of(cotangent, side))
    placed = place_table(routes, order[0], link.me, expert_count, capacity)
    tables = []
    for g in range(depth):
        table = jnp.concatenate([placed[g * width : (g + 1) * width], routes.T], axis=0)
        tables.append(table if g == 0 else link.flip(table, g * width))
    places = jnp.stack([table[:width] for table in tables])
    place_rows = places[:, :, None, :]
    place_columns = jnp.stack([table[:width].T for table in tables])
    route_columns = jnp.stack([low(table[width:].T) for table in tables])

    cosine, sine = (jnp.asarray(t) for t in rope_constants(seq_length, head_width))
    first_in, query, keys, values, inverse_first = project(
        tokens, norm_gain[None], w_query, w_key, w_value, cosine, sine, tile
    )
    seg_row, seg_col = segments, segments[0][:, None]
    mixed, lse, branch = attend(
        query, keys, values, seg_row, seg_col, w_out, score_scale, tile
    )
    hidden, second_in, in_half, inverse_second, gates = second_norm(
        side_ref,
        tokens,
        branch,
        swap(branch),
        ffn_gain[None],
        w_router,
        routes,
        tile,
        (),
    )

    def to_expert(blocks):
        mine = jnp.stack(link.plane(blocks))
        return mine, swap(mine)

    in_slots = [
        link.spread(in_half[:, c * chunk_width : (c + 1) * chunk_width]) for c in range(chunks)
    ]
    picked = pick_rows(line_ref, place_rows, cot_slots, capacity, route_columns, (in_half,))
    cot_mine, cot_other = to_expert(picked[:width])
    route_rows = jnp.stack(link.plane(picked[width:]))
    in_rows = [
        to_expert(pick_rows(line_ref, place_rows, slots, capacity)) for slots in in_slots
    ]
    pieces = [rows[0] for rows in in_rows] + [rows[1] for rows in in_rows]

    pre, acts, terms, backs = expert_rows(
        me_ref, pieces, cot_mine, cot_other, route_rows, w_gate[0], w_up[0], w_down[0], w_router
    )
    terms = terms[..., 0]

    def to_token(away, homes):
        swapped = swap(away)
        return link.plane([low(wide(homes[b]) + wide(swapped[b])) for b in range(width)])

    came_back = [to_token(away, homes) for away, homes in backs]

    terms = jnp.stack(link.plane([terms[b] for b in range(width)]), axis=1)
    slot_ids = jnp.arange(capacity, dtype=jnp.int32)
    local = jnp.sum(
        jnp.where(
            places[:, :, None, :] == slot_ids[None, None, :, None], terms[:, :, :, None], 0.0
        ),
        axis=2,
    )
    term_table = jnp.concatenate(
        [local[g] if g == 0 else link.flip(local[g], g * width) for g in range(depth)]
    )
    term_table = term_table + swap(term_table)
    term_table = term_table[jnp.arange(expert_count, dtype=jnp.int32) ^ link.me].T

    row_half = jnp.concatenate(
        [link.collect(combine(line_ref, place_columns, came)) for came in came_back], axis=1
    )
    row_total = wide(join_halves(row_half, swap(row_half), side))

    arrived = [block for came in came_back for block in came]
    away, *homes = down_rows(me_ref, acts, w_down[0], arrived)
    out_came = to_token(away, homes)
    out_parts = combine(line_ref, place_columns, out_came, (row_half,))
    combined = wide(link.collect(out_parts))
    output_half = low(half_of(hidden, side) + combined)
    output = join_halves(output_half, swap(output_half), side)

    pre = pre.reshape(-1, 2 * unit_count)
    grads = [contract_rows(piece.reshape(-1, chunk_width), pre) for piece in pieces]
    first, second = grads[:chunks], grads[chunks:]
    joined = [jnp.where(side == 0, a, b) for a, b in zip(first + second, second + first)]
    gate_grad = jnp.concatenate([part[:, :unit_count] for part in joined])[None]
    up_grad = jnp.concatenate([part[:, unit_count:] for part in joined])[None]
    act_rows = acts.reshape(-1, unit_count)
    down_grad = join_halves(
        contract_rows(act_rows, cot_mine.reshape(-1, half_width)),
        contract_rows(act_rows, cot_other.reshape(-1, half_width)),
        side,
    )[None]

    upstream = wide(cotangent)
    normed_second = hidden * inverse_second
    d_logits = low(
        gates * (term_table - jnp.sum(gates * term_table, axis=-1, keepdims=True))
    )
    router_grad = contract_rows(second_in, d_logits)
    d_second = row_total + times_transposed(d_logits, w_router)
    scaled_second = d_second * ffn_gain
    ffn_gain_grad = jnp.sum(d_second * normed_second, axis=0)
    d_hidden = upstream + inverse_second * (
        scaled_second
        - normed_second * jnp.mean(scaled_second * normed_second, axis=-1, keepdims=True)
    )
    d_branch = low(d_hidden)
    pad = jnp.zeros((model_width, -(expert_count + 1) % 128), jnp.float32)
    early = jnp.concatenate(
        [contract_rows(d_branch, mixed), router_grad, ffn_gain_grad[:, None], pad], axis=1
    )
    early = link.scatter_sum(early)
    out_grad, small = early[:, :span].T, early[:, span:]

    d_all = attend_back(
        query,
        keys,
        values,
        seg_row,
        seg_col,
        lse,
        d_branch,
        w_out,
        cosine,
        sine,
        score_scale,
        tile,
        (out_parts,),
    )
    d_first = first_grad(d_all, w_query, w_key, w_value, tile, ())
    qkv_grad = link.scatter_sum(contract_rows(first_in, d_all))
    d_first = wide(d_first) + wide(swap(d_first))
    normed_first = wide(tokens) * inverse_first
    scaled_first = d_first * norm_gain
    input_grad = d_hidden + inverse_first * (
        scaled_first - normed_first * jnp.mean(scaled_first * normed_first, axis=-1, keepdims=True)
    )
    rows = model_width // expert_count
    gain_part = jnp.zeros((rows,), jnp.float32)
    start = 0
    for weight in (w_query, w_key, w_value):
        mine = lax.dynamic_slice_in_dim(weight, link.me * rows, rows, 0)
        grads = qkv_grad[:, start : start + weight.shape[1]]
        gain_part = gain_part + jnp.sum(grads * wide(mine), axis=1)
        start += weight.shape[1]
    gain_part = gain_part / lax.dynamic_slice_in_dim(norm_gain, link.me * rows, rows, 0)
    norm_gain_grad = gain_part + swap(gain_part)
    return (
        output,
        input_grad,
        norm_gain_grad,
        small[:, expert_count],
        qkv_grad[:, :span],
        qkv_grad[:, span : span + head_width],
        qkv_grad[:, span + head_width :],
        out_grad,
        small[:, :expert_count],
        gate_grad,
        up_grad,
        down_grad,
    )


def solution(mesh):
    placed = (
        P("expert", None),
        P("expert", None),
        P(),
        P(),
        P(None, "tensor"),
        P(None, "tensor"),
        P(None, "tensor"),
        P("tensor", None),
        P(),
        P("expert", None, "tensor"),
        P("expert", None, "tensor"),
        P("expert", "tensor", None),
        P("expert", None),
        P("expert", None),
        P("expert", None),
    )
    return jax.shard_map(
        on_device,
        mesh=mesh,
        in_specs=placed,
        out_specs=(
            P("expert", None),
            P("expert", None),
            P("expert"),
            P("expert"),
            P("expert", "tensor"),
            P("expert", "tensor"),
            P("expert", "tensor"),
            P("tensor", "expert"),
            P("expert", None),
            P("expert", None, "tensor"),
            P("expert", None, "tensor"),
            P("expert", "tensor", None),
        ),
        check_vma=False,
    )
```

```python
import functools
import math

import jax
import jax.numpy as jnp
import numpy as np
from jax import lax
from jax.experimental import pallas as pl
from jax.experimental.pallas import tpu as pltpu
from jax.sharding import PartitionSpec as P

epsilon = 1e-06
rope_base = 1000000.0
masked_score = -1e30


def contract_rows(left, right):
    return lax.dot_general(
        left, right, (((0,), (0,)), ((), ())), preferred_element_type=jnp.float32
    )


def times_transposed(left, right):
    return lax.dot_general(
        left, right, (((1,), (1,)), ((), ())), preferred_element_type=jnp.float32
    )


def line_depth(count):
    depth = 1
    while depth * depth * 4 <= count:
        depth *= 2
    return depth


VMEM_LIMIT = 56 * 1024 * 1024


def kernel_params(*semantics):
    return pltpu.CompilerParams(vmem_limit_bytes=VMEM_LIMIT)


def lasting(microseconds):
    return pl.CostEstimate(
        flops=int(microseconds * 1.0e6), bytes_accessed=1024, transcendentals=0
    )


def hold_kernel(*refs):
    del refs


def hold(array, *earlier):
    return pl.pallas_call(
        hold_kernel,
        in_specs=anywhere((array, *earlier)),
        out_specs=pl.BlockSpec(memory_space=pl.ANY),
        out_shape=jax.ShapeDtypeStruct(array.shape, array.dtype),
        input_output_aliases={0: 0},
    )(array, *earlier)


def whole(array):
    return pl.BlockSpec(array.shape, lambda *_: (0,) * array.ndim)


def anywhere(arrays):
    return [pl.BlockSpec(memory_space=pl.ANY)] * len(arrays)


SCALAR = pl.BlockSpec(memory_space=pltpu.SMEM)


def dot(left, right, left_axis=1, right_axis=0):
    return lax.dot_general(
        left,
        right,
        (((left_axis,), (right_axis,)), ((), ())),
        preferred_element_type=jnp.float32,
    )


def rope_constants(seq_length, head_width):
    half = head_width // 2
    frequency = np.exp(-math.log(rope_base) * np.arange(half) * (2.0 / head_width))
    angle = np.arange(seq_length)[:, None] * frequency[None, :]
    cosine, sine = np.cos(angle), np.sin(angle)
    return (
        np.concatenate([cosine, cosine], axis=1).astype(np.float32),
        np.concatenate([-sine, sine], axis=1).astype(np.float32),
    )


def place_kernel(seq_length, capacity, keys_ref, out_ref):
    block = keys_ref[...]
    columns = block.T
    limit = seq_length * 1024
    for row in range(block.shape[0]):
        mine = block[row : row + 1, :]
        total = jnp.zeros((1, seq_length), jnp.float32)
        for start in range(0, seq_length, 256):
            less = columns[start : start + 256, row : row + 1] < mine
            total = total + jnp.sum(jnp.where(less, 1.0, 0.0), axis=0, keepdims=True)
        kept = (mine < limit) & (total < capacity)
        out_ref[row : row + 1, :] = jnp.where(kept, total, -1.0).astype(jnp.int32)


def place_table(routes, order, me, expert_count, capacity):
    seq_length = routes.shape[0]
    relabeled = (routes ^ me).T
    ranks = order.reshape(routes.shape).T
    labels = jnp.arange(expert_count, dtype=jnp.int32)
    hit = relabeled[:, None, :] == labels[None, :, None]
    rank = jnp.sum(jnp.where(hit, ranks[:, None, :] + 1, 0), axis=0)
    rank = jnp.where(rank > 0, rank, seq_length * 1024)
    spec = pl.BlockSpec((8, seq_length), lambda e: (e, 0))
    return pl.pallas_call(
        functools.partial(place_kernel, seq_length, capacity),
        grid=(expert_count // 8,),
        out_shape=jax.ShapeDtypeStruct(rank.shape, jnp.int32),
        in_specs=[spec],
        out_specs=spec,
        compiler_params=kernel_params(),
        cost_estimate=lasting(9.0 * expert_count / 16),
    )(rank)


def turn(values, cosine, sine):
    return values * cosine + pltpu.roll(values, values.shape[1] // 2, 1) * sine


def project_kernel(
    heads, x_ref, gain_ref, wq_ref, wk_ref, wv_ref, cos_ref, sin_ref, in_ref, q_ref, k_ref, v_ref, inv_ref
):
    source = x_ref[...].astype(jnp.float32)
    inverse = lax.rsqrt(jnp.mean(source * source, axis=1, keepdims=True) + epsilon)
    first = (source * inverse * gain_ref[...]).astype(jnp.bfloat16)
    in_ref[...] = first
    inv_ref[...] = inverse
    cosine, sine = cos_ref[...], sin_ref[...]
    size = cosine.shape[1]
    query = dot(first, wq_ref[...])
    for head in range(heads):
        span = slice(head * size, (head + 1) * size)
        q_ref[:, span] = turn(query[:, span], cosine, sine).astype(jnp.bfloat16)
    k_ref[...] = turn(dot(first, wk_ref[...]), cosine, sine).astype(jnp.bfloat16)
    v_ref[...] = dot(first, wv_ref[...]).astype(jnp.bfloat16)


def project(tokens, gain, w_query, w_key, w_value, cosine, sine, tile):
    length, model = tokens.shape
    size = w_key.shape[1]
    span = w_query.shape[1]

    def rows(columns):
        return pl.BlockSpec((tile, columns), lambda i: (i, 0))

    def shape(columns, kind=jnp.bfloat16):
        return jax.ShapeDtypeStruct((length, columns), kind)

    return pl.pallas_call(
        functools.partial(project_kernel, span // size),
        grid=(length // tile,),
        in_specs=[
            rows(model),
            whole(gain),
            whole(w_query),
            whole(w_key),
            whole(w_value),
            rows(size),
            rows(size),
        ],
        out_specs=[rows(model), rows(span), rows(size), rows(size), rows(1)],
        out_shape=[shape(model), shape(span), shape(size), shape(size), shape(1, jnp.float32)],
        compiler_params=kernel_params(),
        cost_estimate=lasting(9.0),
    )(tokens, gain, w_query, w_key, w_value, cosine, sine)


def attend_kernel(
    heads, scale, q_ref, k_ref, v_ref, segq_ref, segk_ref, wo_ref, mix_ref, lse_ref, branch_ref
):
    allowed = segk_ref[...] <= segq_ref[...]
    keys = k_ref[...]
    values = v_ref[...].T
    size = keys.shape[1]
    for head in range(heads):
        span = slice(head * size, (head + 1) * size)
        scores = dot(keys, q_ref[:, span], 1, 1)
        scores = jnp.where(allowed, scores * scale, masked_score)
        top = jnp.max(scores, axis=0, keepdims=True)
        spread = jnp.exp(scores - top)
        total = jnp.sum(spread, axis=0, keepdims=True)
        mixed = dot(values, spread.astype(jnp.bfloat16)) / total
        mix_ref[:, span] = mixed.T.astype(jnp.bfloat16)
        lse_ref[head : head + 1, :] = top + jnp.log(total)
    branch_ref[...] = dot(mix_ref[...], wo_ref[...]).astype(jnp.bfloat16)


def attend(query, keys, values, seg_row, seg_col, w_out, scale, tile):
    length, span = query.shape
    size = keys.shape[1]
    heads = span // size
    model = w_out.shape[1]
    rows = pl.BlockSpec((tile, span), lambda i: (i, 0))
    return pl.pallas_call(
        functools.partial(attend_kernel, heads, scale),
        grid=(length // tile,),
        in_specs=[
            rows,
            whole(keys),
            whole(values),
            pl.BlockSpec((1, tile), lambda i: (0, i)),
            whole(seg_col),
            whole(w_out),
        ],
        out_specs=[
            rows,
            pl.BlockSpec((heads, tile), lambda i: (0, i)),
            pl.BlockSpec((tile, model), lambda i: (i, 0)),
        ],
        out_shape=[
            jax.ShapeDtypeStruct((length, span), jnp.bfloat16),
            jax.ShapeDtypeStruct((heads, length), jnp.float32),
            jax.ShapeDtypeStruct((length, model), jnp.bfloat16),
        ],
        compiler_params=kernel_params(),
        cost_estimate=lasting(20.0),
    )(query, keys, values, seg_row, seg_col, w_out)


def second_kernel(
    outputs, side_ref, x_ref, a_ref, b_ref, gain_ref, router_ref, routes_ref, *refs
):
    refs = refs[len(refs) - outputs :]
    hidden_ref, in_ref, inv_ref, gate_ref, *parts = refs
    hidden = x_ref[...].astype(jnp.float32) + (
        a_ref[...].astype(jnp.float32) + b_ref[...].astype(jnp.float32)
    )
    inverse = lax.rsqrt(jnp.mean(hidden * hidden, axis=1, keepdims=True) + epsilon)
    second = (hidden * inverse * gain_ref[...]).astype(jnp.bfloat16)
    hidden_ref[...] = hidden
    in_ref[...] = second
    inv_ref[...] = inverse
    half = second.shape[1] // 2
    sent = jnp.where(side_ref[0] == 0, second[:, :half], second[:, half:])
    start = 0
    for part in parts:
        part[...] = sent[:, start : start + part.shape[1]]
        start += part.shape[1]
    logits = dot(second, router_ref[...])
    gate_ref[...] = routed_softmax(logits, routes_ref[...])


def routed_softmax(logits, routes):
    labels = lax.broadcasted_iota(jnp.int32, logits.shape, 1)
    picked = routes[:, 0:1] == labels
    for k in range(1, routes.shape[1]):
        picked = picked | (routes[:, k : k + 1] == labels)
    masked = jnp.where(picked, logits, masked_score)
    spread = jnp.exp(masked - jnp.max(masked, axis=1, keepdims=True))
    return spread / jnp.sum(spread, axis=1, keepdims=True)


def second_norm(side, tokens, mine, other, gain, router, routes, tile, widths, earlier):
    length, model = tokens.shape
    count = router.shape[1]

    def rows(columns):
        return pl.BlockSpec((tile, columns), lambda i: (i, 0))

    def shape(columns, kind=jnp.float32):
        return jax.ShapeDtypeStruct((length, columns), kind)

    return pl.pallas_call(
        functools.partial(second_kernel, 4 + len(widths)),
        grid=(length // tile,),
        in_specs=[
            SCALAR,
            rows(model),
            rows(model),
            rows(model),
            whole(gain),
            whole(router),
            rows(routes.shape[1]),
        ]
        + anywhere(earlier),
        out_specs=[rows(model), rows(model), rows(1), rows(count)] + [rows(w) for w in widths],
        out_shape=[shape(model), shape(model, jnp.bfloat16), shape(1), shape(count)]
        + [shape(w, jnp.bfloat16) for w in widths],
        compiler_params=kernel_params(),
        cost_estimate=lasting(9.0),
    )(side, tokens, mine, other, gain, router, routes, *earlier)


def chosen_slots(place_row, capacity):
    slot = lax.broadcasted_iota(jnp.int32, (capacity, place_row.shape[1]), 0)
    return jnp.where(place_row == slot, 1.0, 0.0).astype(jnp.bfloat16)


def pick_kernel(width, capacity, outputs, line_ref, tab_ref, slot_ref, *refs):
    outs = refs[len(refs) - outputs :]
    chosen = jnp.concatenate([chosen_slots(tab_ref[0, b], capacity) for b in range(width)])

    def give(rows, targets):
        for b in range(width):
            targets[b][0] = rows[b * capacity : (b + 1) * capacity].astype(jnp.bfloat16)

    give(dot(chosen, slot_ref[0]), outs[:width])
    if len(outs) > width:
        give(dot(chosen, refs[0][0]), outs[width:])


def pick_rows(line, tables, slots, capacity, small=None, earlier=()):
    count, width, _, length = tables.shape
    columns = slots.shape[2]
    if capacity % 16:
        slot = jnp.arange(capacity, dtype=jnp.int32)
        chosen = low(tables == slot[None, None, :, None])

        def taken(rows):
            picked = jnp.einsum("gbst,gtd->bgsd", chosen, rows, preferred_element_type=jnp.float32)
            return [low(picked[b]) for b in range(width)]

        near = slots[jnp.arange(count, dtype=jnp.int32) ^ line[0]]
        return taken(near) + ([] if small is None else taken(small))
    in_specs = [
        pl.BlockSpec((1, width, 1, length), lambda g, line: (g, 0, 0, 0)),
        pl.BlockSpec((1, length, columns), lambda g, line: (g ^ line[0], 0, 0)),
    ]
    out_specs = [pl.BlockSpec((1, capacity, columns), lambda g, line: (g, 0, 0))] * width
    out_shape = [jax.ShapeDtypeStruct((count, capacity, columns), jnp.bfloat16)] * width
    operands = [tables, slots]
    if small is not None:
        picks = small.shape[2]
        in_specs.append(pl.BlockSpec((1, length, picks), lambda g, line: (g, 0, 0)))
        out_specs += [pl.BlockSpec((1, capacity, picks), lambda g, line: (g, 0, 0))] * width
        out_shape += [jax.ShapeDtypeStruct((count, capacity, picks), jnp.bfloat16)] * width
        operands.append(small)
    return pl.pallas_call(
        functools.partial(pick_kernel, width, capacity, len(out_shape)),
        grid_spec=pltpu.PrefetchScalarGridSpec(
            num_scalar_prefetch=1,
            grid=(count,),
            in_specs=in_specs + anywhere(earlier),
            out_specs=out_specs,
        ),
        out_shape=out_shape,
        compiler_params=kernel_params(),
        cost_estimate=lasting(3.0 * count * columns / 768),
    )(line, *operands, *earlier)


def combine_kernel(width, capacity, line_ref, tab_ref, *refs):
    out_ref = refs[-1]
    codes = tab_ref[0]
    total = width * capacity
    chosen = []
    for start in range(0, total, 128):
        size = min(128, total - start)
        slot = lax.broadcasted_iota(jnp.int32, (codes.shape[0], size), 1) + start
        hit = None
        for b in range(start // capacity, (start + size - 1) // capacity + 1):
            same = codes[:, b : b + 1] == slot
            hit = same if hit is None else hit | same
        chosen.append(jnp.where(hit, 1.0, 0.0).astype(jnp.bfloat16))
    rows = jnp.concatenate([refs[b][0] for b in range(width)])
    out_ref[0] = dot(jnp.concatenate(chosen, axis=1), rows).astype(out_ref.dtype)


def combine(line, table_columns, came, earlier=()):
    count, length, width = table_columns.shape
    _, capacity, columns = came[0].shape
    if capacity % 16:
        slot = jnp.arange(width * capacity, dtype=jnp.int32).reshape(width, capacity)
        chosen = low(table_columns[:, :, :, None] == slot)
        rows = jnp.stack(came)
        total = jnp.einsum("gtbs,bgsd->gtd", chosen, rows, preferred_element_type=jnp.float32)
        return low(total[jnp.arange(count, dtype=jnp.int32) ^ line[0]])
    return pl.pallas_call(
        functools.partial(combine_kernel, width, capacity),
        grid_spec=pltpu.PrefetchScalarGridSpec(
            num_scalar_prefetch=1,
            grid=(count,),
            in_specs=[pl.BlockSpec((1, length, width), lambda g, line: (g, 0, 0))]
            + [pl.BlockSpec((1, capacity, columns), lambda g, line: (g, 0, 0))] * width
            + anywhere(earlier),
            out_specs=pl.BlockSpec((1, length, columns), lambda g, line: (g ^ line[0], 0, 0)),
        ),
        out_shape=jax.ShapeDtypeStruct((count, length, columns), jnp.bfloat16),
        compiler_params=kernel_params(),
        cost_estimate=lasting(3.0 * count * columns / 768),
    )(line, table_columns, *came, *earlier)


def expert_kernel(count_in, count_cot, widths, width, me_ref, *refs):
    x_refs, refs = refs[: 2 * count_in], refs[2 * count_in :]
    c_refs, refs = refs[: 2 * count_cot], refs[2 * count_cot :]
    route_ref, wgu_ref, wd_ref, wr_ref, *outs = refs
    pre_ref, act_ref, term_ref = outs[:3]
    aways = outs[3 : 3 + len(widths)]
    homes = outs[3 + len(widths) :]
    side = me_ref[1]
    batch, _, capacity, _ = x_refs[0].shape
    half = sum(ref.shape[3] for ref in x_refs[:count_in])

    def flat(ref):
        return ref[...].reshape(batch * capacity, ref.shape[3])

    def keep(ref, rows):
        ref[...] = rows.reshape(ref.shape).astype(ref.dtype)

    def columns(which, start, size):
        return pl.ds(pl.multiple_of(which * half + start, 128), size)

    def spans(array_refs):
        count = len(array_refs) // 2
        for index, ref in enumerate(array_refs):
            which = side if index < count else 1 - side
            start = sum(r.shape[3] for r in array_refs[: index % count])
            yield flat(ref), columns(which, start, ref.shape[3])

    def through(weight_ref):
        total = None
        for rows, at in spans(x_refs):
            part = dot(rows, weight_ref[at, :])
            total = part if total is None else total + part
        return total

    both, logits = through(wgu_ref), through(wr_ref)
    units = both.shape[1] // 2
    gate_pre, up_pre = both[:, :units], both[:, units:]
    raw = None
    for rows, at in spans(c_refs):
        part = dot(rows, wd_ref[:, at], 1, 1)
        raw = part if raw is None else raw + part
    chance = routed_softmax(logits, flat(route_ref).astype(jnp.float32).astype(jnp.int32))
    label = lax.broadcasted_iota(jnp.int32, chance.shape, 1)
    gate = jnp.sum(jnp.where(label == me_ref[0], chance, 0.0), axis=1, keepdims=True)
    sig = jax.nn.sigmoid(gate_pre)
    silu = gate_pre * sig
    act = silu * up_pre
    keep(term_ref, jnp.sum(act * raw, axis=1, keepdims=True))
    keep(act_ref, act * gate)
    d_act = raw * gate
    d_gate = (d_act * up_pre * sig * (1.0 + gate_pre * (1.0 - sig))).astype(jnp.bfloat16)
    d_up = (d_act * silu).astype(jnp.bfloat16)
    d_both = jnp.concatenate([d_gate, d_up], axis=1)
    keep(pre_ref, d_both)
    start = 0
    for c, size in enumerate(widths):
        keep(aways[c], dot(d_both, wgu_ref[columns(1 - side, start, size), :], 1, 1))
        home = dot(d_both, wgu_ref[columns(side, start, size), :], 1, 1)
        home = home.astype(jnp.bfloat16).reshape(batch, capacity, size)
        give_homes(home, homes[c * width : (c + 1) * width])
        start += size


def give_homes(rows, homes):
    batch = rows.shape[0]
    for b in range(len(homes)):

        @pl.when(pl.program_id(0) == b // batch)
        def _(b=b):
            homes[b][0] = rows[b % batch]


def block_batch(width, capacity):
    return 1 if capacity % 16 else min(2, width)


def home_specs(width, batch, count, capacity, columns):
    return [
        pl.BlockSpec((1, capacity, columns), functools.partial(home_block, k // batch, count))
        for k in range(width)
    ]


def expert_rows(me, pieces, c_pieces, widths, routes, w_both, w_down, router):
    width, count, capacity, _ = pieces[0].shape
    units = w_down.shape[0]
    batch = block_batch(width, capacity)

    def rows(columns):
        return pl.BlockSpec((batch, 1, capacity, columns), lambda b, g: (b, g, 0, 0))

    def shape(columns, kind=jnp.bfloat16):
        return jax.ShapeDtypeStruct((width, count, capacity, columns), kind)

    out_specs = [rows(2 * units), rows(units), rows(1)] + [rows(size) for size in widths]
    out_shape = [shape(2 * units), shape(units), shape(1, jnp.float32)]
    out_shape += [shape(size) for size in widths]
    for size in widths:
        out_specs += home_specs(width, batch, count, capacity, size)
        out_shape += [jax.ShapeDtypeStruct((count, capacity, size), jnp.bfloat16)] * width
    outs = pl.pallas_call(
        functools.partial(expert_kernel, len(pieces) // 2, len(c_pieces) // 2, widths, width),
        grid=(width // batch, count),
        in_specs=[SCALAR]
        + [rows(piece.shape[3]) for piece in (*pieces, *c_pieces)]
        + [
            rows(routes.shape[3]),
            whole(w_both),
            whole(w_down),
            whole(router),
        ],
        out_specs=out_specs,
        out_shape=out_shape,
        compiler_params=kernel_params(),
        cost_estimate=lasting(10.0 * count),
    )(me, *pieces, *c_pieces, routes, w_both, w_down, router)
    aways, homes = outs[3 : 3 + len(widths)], outs[3 + len(widths) :]
    return (
        *outs[:3],
        [(aways[c], homes[c * width : (c + 1) * width]) for c in range(len(widths))],
    )


def pile_kernel(count, *refs):
    blocks, out_ref = refs[:count], refs[-1]
    for b in range(count):
        out_ref[b] = blocks[b][...]


def pile(blocks, earlier):
    slots, capacity, columns = blocks[0].shape
    count = len(blocks)
    return pl.pallas_call(
        functools.partial(pile_kernel, count),
        grid=(slots,),
        in_specs=[pl.BlockSpec((1, capacity, columns), lambda g: (g, 0, 0))] * count
        + anywhere(earlier),
        out_specs=pl.BlockSpec((count, 1, capacity, columns), lambda g: (0, g, 0, 0)),
        out_shape=jax.ShapeDtypeStruct((count, slots, capacity, columns), blocks[0].dtype),
        compiler_params=kernel_params(),
        cost_estimate=lasting(5.0),
    )(*blocks, *earlier)


def join_kernel(count, *refs):
    homes, swapped_ref, outs = refs[:count], refs[count], refs[len(refs) - count :]
    for b in range(count):
        total = homes[b][...].astype(jnp.float32) + swapped_ref[b].astype(jnp.float32)
        outs[b][...] = total.astype(jnp.bfloat16)


def join_cores(homes, swapped, earlier):
    slots, capacity, columns = homes[0].shape
    count = len(homes)
    block = pl.BlockSpec((1, capacity, columns), lambda g: (g, 0, 0))
    return pl.pallas_call(
        functools.partial(join_kernel, count),
        grid=(slots,),
        in_specs=[block] * count
        + [pl.BlockSpec((count, 1, capacity, columns), lambda g: (0, g, 0, 0))]
        + anywhere(earlier),
        out_specs=[block] * count,
        out_shape=[jax.ShapeDtypeStruct(homes[0].shape, jnp.bfloat16)] * count,
        compiler_params=kernel_params(),
        cost_estimate=lasting(7.0),
    )(*homes, swapped, *earlier)


def settle_kernel(pieces, side_ref, *refs):
    halves, refs = refs[: 2 * pieces], refs[2 * pieces :]
    hid_ref, inv_ref, cot_ref, gate_ref, term_ref, router_ref, gain_ref = refs[:7]
    dh_ref, db_ref, dl_ref, gg_ref = refs[-4:]
    gates, terms = gate_ref[...], term_ref[...]
    d_logits = gates * (terms - jnp.sum(gates * terms, axis=1, keepdims=True))
    d_logits = d_logits.astype(jnp.bfloat16)
    dl_ref[...] = jnp.zeros_like(dl_ref)
    dl_ref[:, : d_logits.shape[1]] = d_logits
    mine = jnp.concatenate([ref[...] for ref in halves[:pieces]], axis=1)
    other = jnp.concatenate([ref[...] for ref in halves[pieces:]], axis=1)
    first = side_ref[0] == 0
    rows = jnp.concatenate([jnp.where(first, mine, other), jnp.where(first, other, mine)], axis=1)
    d_second = rows.astype(jnp.float32) + dot(d_logits, router_ref[...], 1, 1)
    inverse = inv_ref[...]
    normed = hid_ref[...] * inverse
    scaled = d_second * gain_ref[...]
    gain_grad = jnp.sum(d_second * normed, axis=0, keepdims=True)

    @pl.when(pl.program_id(0) == 0)
    def _():
        gg_ref[...] = gain_grad

    @pl.when(pl.program_id(0) > 0)
    def _():
        gg_ref[...] += gain_grad

    center = jnp.mean(scaled * normed, axis=1, keepdims=True)
    d_hidden = cot_ref[...].astype(jnp.float32) + inverse * (scaled - normed * center)
    dh_ref[...] = d_hidden
    db_ref[...] = d_hidden.astype(jnp.bfloat16)


def settle(
    side, mine, other, hidden, inverse, cotangent, gates, terms, router, gain, tile, earlier
):
    length, model = hidden.shape
    count = router.shape[1]
    padded = count + 128 - count % 128

    def rows(columns):
        return pl.BlockSpec((tile, columns), lambda i: (i, 0))

    def shape(columns, kind=jnp.float32):
        return jax.ShapeDtypeStruct((length, columns), kind)

    return pl.pallas_call(
        functools.partial(settle_kernel, len(mine)),
        grid=(length // tile,),
        in_specs=[SCALAR]
        + [rows(piece.shape[1]) for piece in (*mine, *other)]
        + [rows(model), rows(1), rows(model), rows(count), rows(count), whole(router), whole(gain)]
        + anywhere(earlier),
        out_specs=[rows(model), rows(model), rows(padded), whole(gain)],
        out_shape=[
            shape(model),
            shape(model, jnp.bfloat16),
            shape(padded, jnp.bfloat16),
            jax.ShapeDtypeStruct(gain.shape, jnp.float32),
        ],
        compiler_params=kernel_params(),
        cost_estimate=lasting(10.0),
    )(side, *mine, *other, hidden, inverse, cotangent, gates, terms, router, gain, *earlier)


def finish_kernel(a_ref, b_ref, x_ref, inv_ref, dh_ref, gain_ref, out_ref):
    d_first = a_ref[...].astype(jnp.float32) + b_ref[...].astype(jnp.float32)
    inverse = inv_ref[...]
    normed = x_ref[...].astype(jnp.float32) * inverse
    scaled = d_first * gain_ref[...]
    center = jnp.mean(scaled * normed, axis=1, keepdims=True)
    out_ref[...] = dh_ref[...] + inverse * (scaled - normed * center)


def finish(mine, other, tokens, inverse, d_hidden, gain, tile):
    length, model = tokens.shape

    def rows(columns):
        return pl.BlockSpec((tile, columns), lambda i: (i, 0))

    return pl.pallas_call(
        finish_kernel,
        grid=(length // tile,),
        in_specs=[rows(model), rows(model), rows(model), rows(1), rows(model), whole(gain)],
        out_specs=rows(model),
        out_shape=jax.ShapeDtypeStruct((length, model), jnp.float32),
        compiler_params=kernel_params(),
        cost_estimate=lasting(8.0),
    )(mine, other, tokens, inverse, d_hidden, gain)


def home_block(k, count, b, g):
    return (jnp.where(b < k, 0, jnp.where(b > k, count - 1, g)), 0, 0)


def down_kernel(width, me_ref, act_ref, wd_ref, *refs):
    outs = refs[-1 - width :]
    away_ref, homes = outs[0], outs[1:]
    side = me_ref[1]
    batch, _, capacity, half = away_ref.shape
    mine = pl.ds(pl.multiple_of(side * half, half), half)
    other = pl.ds(pl.multiple_of((1 - side) * half, half), half)
    act = act_ref[...].reshape(batch * capacity, act_ref.shape[3])
    away_ref[...] = low(dot(act, wd_ref[:, other])).reshape(away_ref.shape)
    give_homes(low(dot(act, wd_ref[:, mine])).reshape(batch, capacity, half), homes)


def down_rows(me, act, w_down, earlier):
    width, count, capacity, units = act.shape
    half = w_down.shape[1] // 2
    batch = block_batch(width, capacity)

    def rows(columns):
        return pl.BlockSpec((batch, 1, capacity, columns), lambda b, g: (b, g, 0, 0))

    return pl.pallas_call(
        functools.partial(down_kernel, width),
        grid=(width // batch, count),
        in_specs=[SCALAR, rows(units), whole(w_down)] + anywhere(earlier),
        out_specs=[rows(half)] + home_specs(width, batch, count, capacity, half),
        out_shape=[jax.ShapeDtypeStruct((width, count, capacity, half), jnp.bfloat16)]
        + [jax.ShapeDtypeStruct((count, capacity, half), jnp.bfloat16)] * width,
        compiler_params=kernel_params(),
        cost_estimate=lasting(3.0 * count),
    )(me, act, w_down, *earlier)


def attend_back_kernel(
    heads,
    scale,
    tile,
    q_ref,
    k_ref,
    v_ref,
    segq_ref,
    segk_ref,
    lse_ref,
    db_ref,
    wo_ref,
    cos_ref,
    sin_ref,
    *refs,
):
    out_ref, dk_ref, dv_ref = refs[-3:]
    step = pl.program_id(0)
    allowed = segk_ref[...] <= segq_ref[...]
    keys = k_ref[...]
    values = v_ref[...]
    size = keys.shape[1]
    here = pl.ds(pl.multiple_of(step * tile, tile), tile)
    cosine, sine = cos_ref[here, :], sin_ref[here, :]
    keys_t = keys.T

    def put(rows, start, array):
        out_ref[rows, start : start + size] = array.astype(jnp.bfloat16)

    d_mixed = dot(db_ref[...], wo_ref[...], 1, 1).astype(jnp.bfloat16)
    dk_total = jnp.zeros(keys.shape, jnp.float32)
    dv_total = jnp.zeros(keys.shape, jnp.float32)
    for head in range(heads):
        span = slice(head * size, (head + 1) * size)
        query = q_ref[:, span]
        d_head = d_mixed[:, span]
        scores = dot(keys, query, 1, 1) * scale - lse_ref[head : head + 1, :]
        probs = jnp.where(allowed, jnp.exp(scores), 0.0)
        d_probs = dot(values, d_head, 1, 1)
        scaled = probs * d_probs
        row_dot = jnp.sum(scaled, axis=0, keepdims=True)
        d_scores = (scale * (scaled - probs * row_dot)).astype(jnp.bfloat16)
        dv_total = dv_total + dot(probs.astype(jnp.bfloat16), d_head)
        dk_total = dk_total + dot(d_scores, query)
        d_query = dot(keys_t, d_scores).T
        put(here, head * size, turn(d_query, cosine, -sine))

    @pl.when(step == 0)
    def _():
        dk_ref[...] = dk_total
        dv_ref[...] = dv_total

    @pl.when(step > 0)
    def _():
        dk_ref[...] += dk_total
        dv_ref[...] += dv_total

    @pl.when(step == pl.num_programs(0) - 1)
    def _():
        base = heads * size
        put(slice(None), base, turn(dk_ref[...], cos_ref[...], -sin_ref[...]))
        put(slice(None), base + size, dv_ref[...])


def attend_back(
    query, keys, values, seg_row, seg_col, lse, d_branch, w_out, cosine, sine, scale, tile, earlier
):
    length, span = query.shape
    size = keys.shape[1]
    heads = span // size
    model = w_out.shape[1]
    out = jax.ShapeDtypeStruct((length, span + 2 * size), jnp.bfloat16)
    return pl.pallas_call(
        functools.partial(attend_back_kernel, heads, scale, tile),
        grid=(length // tile,),
        in_specs=[
            pl.BlockSpec((tile, span), lambda i: (i, 0)),
            whole(keys),
            whole(values),
            pl.BlockSpec((1, tile), lambda i: (0, i)),
            whole(seg_col),
            pl.BlockSpec((heads, tile), lambda i: (0, i)),
            pl.BlockSpec((tile, model), lambda i: (i, 0)),
            whole(w_out),
            whole(cosine),
            whole(sine),
        ]
        + anywhere(earlier),
        out_specs=whole(out),
        out_shape=out,
        scratch_shapes=[pltpu.VMEM((length, size), jnp.float32)] * 2,
        compiler_params=kernel_params(),
        cost_estimate=lasting(28.0),
    )(query, keys, values, seg_row, seg_col, lse, d_branch, w_out, cosine, sine, *earlier)


def first_grad_kernel(d_ref, wq_ref, wk_ref, wv_ref, *refs):
    out_ref = refs[-1]
    span, size = wq_ref.shape[1], wk_ref.shape[1]
    total = dot(d_ref[:, :span], wq_ref[...], 1, 1)
    total = total + dot(d_ref[:, span : span + size], wk_ref[...], 1, 1)
    total = total + dot(d_ref[:, span + size :], wv_ref[...], 1, 1)
    out_ref[...] = total.astype(jnp.bfloat16)


def first_grad(d_all, w_query, w_key, w_value, tile, earlier):
    length, columns = d_all.shape
    model = w_query.shape[0]
    return pl.pallas_call(
        first_grad_kernel,
        grid=(length // tile,),
        in_specs=[
            pl.BlockSpec((tile, columns), lambda i: (i, 0)),
            whole(w_query),
            whole(w_key),
            whole(w_value),
        ]
        + anywhere(earlier),
        out_specs=pl.BlockSpec((tile, model), lambda i: (i, 0)),
        out_shape=jax.ShapeDtypeStruct((length, model), jnp.bfloat16),
        compiler_params=kernel_params(),
        cost_estimate=lasting(8.0),
    )(d_all, w_query, w_key, w_value, *earlier)


def share_kernel(width, rows, extra, spot_ref, left_ref, right_ref, *refs):
    kept_ref, *gone = refs[3 * extra : 3 * extra + width]
    hold_ref = refs[3 * extra + width]
    products = [(0, dot(left_ref[...], right_ref[...], 0, 0))]
    if extra:
        also_ref, picks_ref, row_ref = refs[:3]
        column = jnp.broadcast_to(row_ref[...], (8, row_ref.shape[1])).T[:, :1]
        more = dot(also_ref[...], picks_ref[...], 0, 0)
        lane = lax.broadcasted_iota(jnp.int32, more.shape, 1)
        last = more.shape[1] - 1
        products.append((right_ref.shape[1], jnp.where(lane == last, column, more)))
    for start, product in products:
        for s in range(width):
            part = product[s * rows : (s + 1) * rows]
            hold_ref[s, :, start : start + product.shape[1]] = part
    kept_ref[0] = hold_ref[spot_ref[0]]
    for b in range(1, width):
        gone[b - 1][0] = hold_ref[spot_ref[0] ^ b].astype(jnp.bfloat16)


def share_grads(spot, left, right, depth, width, extra=()):
    length, model = left.shape
    columns = right.shape[1] + (extra[1].shape[1] if extra else 0)
    rows = model // (depth * width)
    if (width * rows) % 128:
        product = dot(left, right, 0, 0)
        if extra:
            more = jnp.concatenate([dot(extra[0], extra[1], 0, 0)[:, :-1], extra[2].T], axis=1)
            product = jnp.concatenate([product, more], axis=1)
        parted = product.reshape(depth, width, rows, columns)
        blocks = [
            lax.dynamic_index_in_dim(parted, spot[0] ^ b, 1, keepdims=False) for b in range(width)
        ]
        return [blocks[0]] + [low(block) for block in blocks[1:]]
    block = pl.BlockSpec((1, rows, columns), lambda l: (l, 0, 0))
    stripe = pl.BlockSpec((length, width * rows), lambda l: (0, l))
    more_specs = []
    if extra:
        more_specs = [stripe, whole(extra[1]), pl.BlockSpec((1, width * rows), lambda l: (0, l))]
    return pl.pallas_call(
        functools.partial(share_kernel, width, rows, int(bool(extra))),
        grid=(depth,),
        in_specs=[SCALAR, stripe, whole(right)] + more_specs,
        out_specs=[block] * width,
        out_shape=[jax.ShapeDtypeStruct((depth, rows, columns), jnp.float32)]
        + [jax.ShapeDtypeStruct((depth, rows, columns), jnp.bfloat16)] * (width - 1),
        scratch_shapes=[pltpu.VMEM((width, rows, columns), jnp.float32)],
        compiler_params=kernel_params(),
        cost_estimate=lasting(6.0),
    )(spot, left, right, *extra)


class Exchange:
    def __init__(self, count):
        self.count = count
        self.depth = line_depth(count)
        self.width = count // self.depth
        self.me = lax.axis_index("expert")
        self.line = self.me // self.width
        self.lines = [[l * self.width + s for l in range(self.depth)] for s in range(self.width)]

    def flip(self, rows, mask):
        return lax.ppermute(rows, "expert", [(d, d ^ mask) for d in range(self.count)])

    def spread(self, rows):
        return lax.all_gather(rows, "expert", axis_index_groups=self.lines)

    def collect(self, parts):
        flat = parts.reshape(-1, parts.shape[-1])
        return lax.psum_scatter(
            flat, "expert", scatter_dimension=0, axis_index_groups=self.lines, tiled=True
        )

    def plane(self, blocks):
        return [blocks[0]] + [self.flip(blocks[b], b) for b in range(1, self.width)]

    def sum_plane(self, blocks):
        held = wide(blocks[0])
        for b in range(1, self.width):
            held = held + wide(self.flip(blocks[b], b))
        return held

    def sum_line(self, held):
        total = lax.dynamic_index_in_dim(held, self.line, 0, keepdims=False)
        for g in range(1, self.depth):
            part = lax.dynamic_index_in_dim(held, self.line ^ g, 0, keepdims=False)
            total = total + wide(self.flip(low(part), g * self.width))
        return total


def low(array):
    return array.astype(jnp.bfloat16)


def wide(array):
    return array.astype(jnp.float32)


def swap(rows):
    return lax.ppermute(rows, "tensor", [(0, 1), (1, 0)])


def half_of(array, side):
    width = array.shape[-1] // 2
    return lax.dynamic_slice_in_dim(array, side * width, width, array.ndim - 1)


def join_halves(mine, other, side):
    first = jnp.where(side == 0, mine, other)
    last = jnp.where(side == 0, other, mine)
    return jnp.concatenate([first, last], axis=-1)


def on_device(
    tokens,
    cotangent,
    norm_gain,
    ffn_gain,
    w_query,
    w_key,
    w_value,
    w_out,
    w_router,
    w_gate,
    w_up,
    w_down,
    routes,
    order,
    segments,
):
    seq_length, model_width = tokens.shape
    half_width = model_width // 2
    expert_count = w_router.shape[1]
    pick_count = routes.shape[1]
    capacity = 9 * seq_length * pick_count // (8 * expert_count)
    head_width = w_key.shape[1]
    span = w_query.shape[1]
    unit_count = w_down.shape[1]
    score_scale = 1.0 / math.sqrt(head_width)
    tile = 256
    link = Exchange(expert_count)
    depth, width = link.depth, link.width
    side = lax.axis_index("tensor")
    side_ref = side.astype(jnp.int32)[None]
    me_ref = jnp.stack([link.me, side]).astype(jnp.int32)
    line_ref = link.line.astype(jnp.int32)[None]

    third = half_width // 3
    widths = (2 * third, third)
    cot_slots = link.spread(half_of(cotangent, side))
    placed = place_table(routes, order[0], link.me, expert_count, capacity)
    tables = []
    for g in range(depth):
        table = jnp.concatenate([placed[g * width : (g + 1) * width], routes.T], axis=0)
        tables.append(table if g == 0 else link.flip(table, g * width))
    places = jnp.stack([table[:width] for table in tables])
    place_rows = places[:, :, None, :]
    starts = capacity * jnp.arange(width, dtype=jnp.int32)
    place_columns = jnp.where(places >= 0, places + starts[None, :, None], -1)
    place_columns = jnp.swapaxes(place_columns, 1, 2)
    route_columns = jnp.stack([low(table[width:].T) for table in tables])

    route_blocks = link.plane(
        pick_rows(jnp.zeros_like(line_ref), place_rows, route_columns, capacity)
    )
    route_rows = jnp.stack(route_blocks)

    cosine, sine = (jnp.asarray(t) for t in rope_constants(seq_length, head_width))
    first_in, query, keys, values, inverse_first = project(
        tokens, norm_gain[None], w_query, w_key, w_value, cosine, sine, tile
    )
    seg_row, seg_col = segments, segments[0][:, None]
    mixed, lse, branch = attend(
        query, keys, values, seg_row, seg_col, w_out, score_scale, tile
    )
    hidden, second_in, inverse_second, gates, *in_parts = second_norm(
        side_ref,
        tokens,
        branch,
        swap(branch),
        ffn_gain[None],
        w_router,
        routes,
        tile,
        widths,
        (place_rows, *route_blocks[1:]),
    )
    w_both = jnp.concatenate([w_gate[0], w_up[0]], axis=1)
    in_slots = [link.spread(hold(in_parts[0], cot_slots))]
    cot_blocks = pick_rows(line_ref, place_rows, cot_slots, capacity, None, (second_in, w_both))
    cot_came = link.plane(cot_blocks)
    in_slots.append(link.spread(hold(in_parts[1], in_slots[0], *cot_came[1:])))
    in_first = pick_rows(line_ref, place_rows, in_slots[0], capacity)
    in_came = [link.plane(in_first)]
    in_last = pick_rows(line_ref, place_rows, in_slots[1], capacity, None, in_came[0][1:])
    in_came.append(link.plane(in_last))
    cot_mine = pile(cot_came, in_last[1:])
    cot_other = swap(cot_mine)
    in_mine = [pile(in_came[0], (cot_mine,))]
    in_other = [swap(in_mine[0])]
    in_mine.append(pile(in_came[1], (in_other[0], cot_other)))
    in_other.append(swap(in_mine[1]))
    pieces, c_pieces = in_mine + in_other, [cot_mine, cot_other]

    pre, acts, terms, backs = expert_rows(
        me_ref, pieces, c_pieces, widths, route_rows, w_both, w_down[0], w_router
    )
    swapped = [swap(away) for away, _ in backs]
    first_came = link.plane(join_cores(backs[0][1], swapped[0], ()))
    out_away, *out_homes = down_rows(me_ref, acts, w_down[0], ())
    terms = hold(terms, out_away)[..., 0]
    terms = jnp.stack(link.plane([terms[b] for b in range(width)]), axis=1)
    blocks = join_cores(backs[1][1], swapped[1], (*first_came[1:], out_away))
    row_parts = [combine(line_ref, place_columns, first_came, blocks[1:])]
    came = link.plane(blocks)
    row_parts.append(combine(line_ref, place_columns, came, (row_parts[0],)))
    out_blocks = join_cores(out_homes, swap(out_away), (row_parts[1], terms))
    out_came = link.plane(out_blocks)
    row_mine = [hold(link.collect(row_parts[0]), *out_blocks[1:])]
    row_mine.append(link.collect(hold(row_parts[1], row_mine[0])))
    row_other = [swap(part) for part in row_mine]

    act_rows = hold(acts, *out_blocks[1:]).reshape(-1, unit_count)
    grads = [contract_rows(act_rows, piece.reshape(-1, piece.shape[3])) for piece in c_pieces]
    down_grad = join_halves(
        *grads, side
    )[None]
    pre = hold(pre, *out_blocks[1:]).reshape(-1, 2 * unit_count)
    grads = [contract_rows(piece.reshape(-1, piece.shape[3]), pre) for piece in pieces]
    first, last = jnp.concatenate(grads[:2]), jnp.concatenate(grads[2:])
    upper, lower = jnp.where(side == 0, first, last), jnp.where(side == 0, last, first)
    gate_grad = jnp.concatenate([upper[:, :unit_count], lower[:, :unit_count]])[None]
    up_grad = jnp.concatenate([upper[:, unit_count:], lower[:, unit_count:]])[None]

    terms = hold(terms, *out_blocks[1:])
    slot_ids = jnp.arange(capacity, dtype=jnp.int32)
    local = jnp.sum(
        jnp.where(
            places[:, :, None, :] == slot_ids[None, None, :, None], terms[:, :, :, None], 0.0
        ),
        axis=2,
    )
    term_table = jnp.concatenate(
        [local[g] if g == 0 else link.flip(local[g], g * width) for g in range(depth)]
    )
    term_table = term_table + swap(term_table)
    term_table = term_table[jnp.arange(expert_count, dtype=jnp.int32) ^ link.me].T

    d_hidden, d_branch, d_logits, ffn_gain_grad = settle(
        side_ref,
        row_mine,
        row_other,
        hidden,
        inverse_second,
        cotangent,
        gates,
        term_table,
        w_router,
        ffn_gain[None],
        tile,
        (down_grad, gate_grad, up_grad),
    )

    out_parts = combine(line_ref, place_columns, out_came, (d_branch,))
    out_held = hold(out_parts, row_mine[1])
    spot_ref = (link.me % width).astype(jnp.int32)[None]
    shared_early = share_grads(
        spot_ref, d_branch, mixed, depth, width, (second_in, d_logits, ffn_gain_grad)
    )
    early_held = link.sum_plane(shared_early)

    d_all = attend_back(
        query,
        keys,
        values,
        seg_row,
        seg_col,
        lse,
        d_branch,
        w_out,
        cosine,
        sine,
        score_scale,
        tile,
        (*shared_early[1:], out_held),
    )
    d_first = first_grad(d_all, w_query, w_key, w_value, tile, (early_held,))
    input_grad = finish(
        d_first, swap(d_first), tokens, inverse_first, d_hidden, norm_gain[None], tile
    )
    shared = share_grads(spot_ref, first_in, hold(d_all, d_first), depth, width)
    shared = [hold(shared[0], input_grad), *shared[1:]]
    summed = link.sum_line(jnp.concatenate([link.sum_plane(shared), early_held], axis=2))
    columns = span + 2 * head_width
    qkv_grad, early_sum = summed[:, :columns], summed[:, columns:]
    out_grad = early_sum[:, :span].T
    router_grad, ffn_gain_grad = early_sum[:, span : span + expert_count], early_sum[:, -1]
    combined = wide(hold(link.collect(out_held), qkv_grad))
    output_half = low(half_of(hidden, side) + combined)
    output = join_halves(output_half, swap(output_half), side)
    rows = model_width // expert_count
    gain_part = jnp.zeros((rows,), jnp.float32)
    start = 0
    for weight in (w_query, w_key, w_value):
        mine = lax.dynamic_slice_in_dim(weight, link.me * rows, rows, 0)
        grads = qkv_grad[:, start : start + weight.shape[1]]
        gain_part = gain_part + jnp.sum(grads * wide(mine), axis=1)
        start += weight.shape[1]
    gain_part = gain_part / lax.dynamic_slice_in_dim(norm_gain, link.me * rows, rows, 0)
    norm_gain_grad = gain_part + swap(gain_part)
    return (
        output,
        input_grad,
        norm_gain_grad,
        ffn_gain_grad,
        qkv_grad[:, :span],
        qkv_grad[:, span : span + head_width],
        qkv_grad[:, span + head_width :],
        out_grad,
        router_grad,
        gate_grad,
        up_grad,
        down_grad,
    )


def solution(mesh):
    placed = (
        P("expert", None),
        P("expert", None),
        P(),
        P(),
        P(None, "tensor"),
        P(None, "tensor"),
        P(None, "tensor"),
        P("tensor", None),
        P(),
        P("expert", None, "tensor"),
        P("expert", None, "tensor"),
        P("expert", "tensor", None),
        P("expert", None),
        P("expert", None),
        P("expert", None),
    )
    return jax.shard_map(
        on_device,
        mesh=mesh,
        in_specs=placed,
        out_specs=(
            P("expert", None),
            P("expert", None),
            P("expert"),
            P("expert"),
            P("expert", "tensor"),
            P("expert", "tensor"),
            P("expert", "tensor"),
            P("tensor", "expert"),
            P("expert", None),
            P("expert", None, "tensor"),
            P("expert", None, "tensor"),
            P("expert", "tensor", None),
        ),
        check_vma=False,
    )
```

```python
import functools
import math

import jax
import jax.numpy as jnp
import numpy as np
from jax import lax
from jax.experimental import pallas as pl
from jax.experimental.pallas import tpu as pltpu
from jax.sharding import PartitionSpec as P

epsilon = 1e-06
rope_base = 1000000.0
masked_score = -1e30


def contract_rows(left, right):
    return lax.dot_general(
        left, right, (((0,), (0,)), ((), ())), preferred_element_type=jnp.float32
    )


def times_transposed(left, right):
    return lax.dot_general(
        left, right, (((1,), (1,)), ((), ())), preferred_element_type=jnp.float32
    )


def line_depth(count):
    depth = 1
    while depth * depth * 4 <= count:
        depth *= 2
    return depth


longest_block = 256
VMEM_LIMIT = 56 * 1024 * 1024


def kernel_params(*semantics):
    return pltpu.CompilerParams(vmem_limit_bytes=VMEM_LIMIT)


def lasting(microseconds):
    return pl.CostEstimate(
        flops=int(microseconds * 1.0e6), bytes_accessed=1024, transcendentals=0
    )


def hold_kernel(*refs):
    del refs


def hold(array, *earlier):
    return pl.pallas_call(
        hold_kernel,
        in_specs=anywhere((array, *earlier)),
        out_specs=pl.BlockSpec(memory_space=pl.ANY),
        out_shape=jax.ShapeDtypeStruct(array.shape, array.dtype),
        input_output_aliases={0: 0},
    )(array, *earlier)


def whole(array):
    return pl.BlockSpec(array.shape, lambda *_: (0,) * array.ndim)


def anywhere(arrays):
    return [pl.BlockSpec(memory_space=pl.ANY)] * len(arrays)


SCALAR = pl.BlockSpec(memory_space=pltpu.SMEM)


def dot(left, right, left_axis=1, right_axis=0):
    return lax.dot_general(
        left,
        right,
        (((left_axis,), (right_axis,)), ((), ())),
        preferred_element_type=jnp.float32,
    )


def rope_constants(seq_length, head_width):
    half = head_width // 2
    frequency = np.exp(-math.log(rope_base) * np.arange(half) * (2.0 / head_width))
    angle = np.arange(seq_length)[:, None] * frequency[None, :]
    cosine, sine = np.cos(angle), np.sin(angle)
    return (
        np.concatenate([cosine, cosine], axis=1).astype(np.float32),
        np.concatenate([-sine, sine], axis=1).astype(np.float32),
    )


def place_kernel(seq_length, capacity, keys_ref, out_ref):
    block = keys_ref[...]
    columns = block.T
    limit = seq_length * 1024
    for row in range(block.shape[0]):
        mine = block[row : row + 1, :]
        total = jnp.zeros((1, seq_length), jnp.float32)
        for start in range(0, seq_length, 256):
            less = columns[start : start + 256, row : row + 1] < mine
            total = total + jnp.sum(jnp.where(less, 1.0, 0.0), axis=0, keepdims=True)
        kept = (mine < limit) & (total < capacity)
        out_ref[row : row + 1, :] = jnp.where(kept, total, -1.0).astype(jnp.int32)


def place_table(routes, order, me, expert_count, capacity):
    seq_length = routes.shape[0]
    relabeled = (routes ^ me).T
    ranks = order.reshape(routes.shape).T
    labels = jnp.arange(expert_count, dtype=jnp.int32)
    hit = relabeled[:, None, :] == labels[None, :, None]
    rank = jnp.sum(jnp.where(hit, ranks[:, None, :] + 1, 0), axis=0)
    rank = jnp.where(rank > 0, rank, seq_length * 1024)
    spec = pl.BlockSpec((8, seq_length), lambda e: (e, 0))
    return pl.pallas_call(
        functools.partial(place_kernel, seq_length, capacity),
        grid=(expert_count // 8,),
        out_shape=jax.ShapeDtypeStruct(rank.shape, jnp.int32),
        in_specs=[spec],
        out_specs=spec,
        compiler_params=kernel_params(),
        cost_estimate=lasting(9.0 * expert_count / 16),
    )(rank)


def turn(values, cosine, sine):
    return values * cosine + pltpu.roll(values, values.shape[1] // 2, 1) * sine


def project_kernel(
    heads, x_ref, gain_ref, wq_ref, wk_ref, wv_ref, cos_ref, sin_ref, in_ref, q_ref, k_ref, v_ref, inv_ref
):
    source = x_ref[...].astype(jnp.float32)
    inverse = lax.rsqrt(jnp.mean(source * source, axis=1, keepdims=True) + epsilon)
    first = (source * inverse * gain_ref[...]).astype(jnp.bfloat16)
    in_ref[...] = first
    inv_ref[...] = inverse
    cosine, sine = cos_ref[...], sin_ref[...]
    size = cosine.shape[1]
    query = dot(first, wq_ref[...])
    for head in range(heads):
        span = slice(head * size, (head + 1) * size)
        q_ref[:, span] = turn(query[:, span], cosine, sine).astype(jnp.bfloat16)
    k_ref[...] = turn(dot(first, wk_ref[...]), cosine, sine).astype(jnp.bfloat16)
    v_ref[...] = dot(first, wv_ref[...]).astype(jnp.bfloat16)


def project(tokens, gain, w_query, w_key, w_value, cosine, sine, tile):
    length, model = tokens.shape
    size = w_key.shape[1]
    span = w_query.shape[1]

    def rows(columns):
        return pl.BlockSpec((tile, columns), lambda i: (i, 0))

    def shape(columns, kind=jnp.bfloat16):
        return jax.ShapeDtypeStruct((length, columns), kind)

    return pl.pallas_call(
        functools.partial(project_kernel, span // size),
        grid=(length // tile,),
        in_specs=[
            rows(model),
            whole(gain),
            whole(w_query),
            whole(w_key),
            whole(w_value),
            rows(size),
            rows(size),
        ],
        out_specs=[rows(model), rows(span), rows(size), rows(size), rows(1)],
        out_shape=[shape(model), shape(span), shape(size), shape(size), shape(1, jnp.float32)],
        compiler_params=kernel_params(),
        cost_estimate=lasting(9.0),
    )(tokens, gain, w_query, w_key, w_value, cosine, sine)


def attend_kernel(
    heads, scale, q_ref, k_ref, v_ref, segq_ref, segk_ref, wo_ref, mix_ref, lse_ref, branch_ref
):
    allowed = segk_ref[...] <= segq_ref[...]
    keys = k_ref[...]
    values = v_ref[...].T
    size = keys.shape[1]
    for head in range(heads):
        span = slice(head * size, (head + 1) * size)
        scores = dot(keys, q_ref[:, span], 1, 1)
        scores = jnp.where(allowed, scores * scale, masked_score)
        top = jnp.max(scores, axis=0, keepdims=True)
        spread = jnp.exp(scores - top)
        total = jnp.sum(spread, axis=0, keepdims=True)
        mixed = dot(values, spread.astype(jnp.bfloat16)) / total
        mix_ref[:, span] = mixed.T.astype(jnp.bfloat16)
        lse_ref[head : head + 1, :] = top + jnp.log(total)
    branch_ref[...] = dot(mix_ref[...], wo_ref[...]).astype(jnp.bfloat16)


def attend(query, keys, values, seg_row, seg_col, w_out, scale, tile):
    length, span = query.shape
    size = keys.shape[1]
    heads = span // size
    model = w_out.shape[1]
    rows = pl.BlockSpec((tile, span), lambda i: (i, 0))
    return pl.pallas_call(
        functools.partial(attend_kernel, heads, scale),
        grid=(length // tile,),
        in_specs=[
            rows,
            whole(keys),
            whole(values),
            pl.BlockSpec((1, tile), lambda i: (0, i)),
            whole(seg_col),
            whole(w_out),
        ],
        out_specs=[
            rows,
            pl.BlockSpec((heads, tile), lambda i: (0, i)),
            pl.BlockSpec((tile, model), lambda i: (i, 0)),
        ],
        out_shape=[
            jax.ShapeDtypeStruct((length, span), jnp.bfloat16),
            jax.ShapeDtypeStruct((heads, length), jnp.float32),
            jax.ShapeDtypeStruct((length, model), jnp.bfloat16),
        ],
        compiler_params=kernel_params(),
        cost_estimate=lasting(20.0),
    )(query, keys, values, seg_row, seg_col, w_out)


def second_kernel(
    outputs, side_ref, x_ref, a_ref, b_ref, gain_ref, router_ref, routes_ref, *refs
):
    refs = refs[len(refs) - outputs :]
    hidden_ref, in_ref, inv_ref, gate_ref, *parts = refs
    hidden = x_ref[...].astype(jnp.float32) + (
        a_ref[...].astype(jnp.float32) + b_ref[...].astype(jnp.float32)
    )
    inverse = lax.rsqrt(jnp.mean(hidden * hidden, axis=1, keepdims=True) + epsilon)
    second = (hidden * inverse * gain_ref[...]).astype(jnp.bfloat16)
    hidden_ref[...] = hidden
    in_ref[...] = second
    inv_ref[...] = inverse
    half = second.shape[1] // 2
    sent = jnp.where(side_ref[0] == 0, second[:, :half], second[:, half:])
    start = 0
    for part in parts:
        part[...] = sent[:, start : start + part.shape[1]]
        start += part.shape[1]
    logits = dot(second, router_ref[...])
    gate_ref[...] = routed_softmax(logits, routes_ref[...])


def routed_softmax(logits, routes):
    labels = lax.broadcasted_iota(jnp.int32, logits.shape, 1)
    picked = routes[:, 0:1] == labels
    for k in range(1, routes.shape[1]):
        picked = picked | (routes[:, k : k + 1] == labels)
    masked = jnp.where(picked, logits, masked_score)
    spread = jnp.exp(masked - jnp.max(masked, axis=1, keepdims=True))
    return spread / jnp.sum(spread, axis=1, keepdims=True)


def second_norm(side, tokens, mine, other, gain, router, routes, tile, widths, earlier):
    length, model = tokens.shape
    count = router.shape[1]

    def rows(columns):
        return pl.BlockSpec((tile, columns), lambda i: (i, 0))

    def shape(columns, kind=jnp.float32):
        return jax.ShapeDtypeStruct((length, columns), kind)

    return pl.pallas_call(
        functools.partial(second_kernel, 4 + len(widths)),
        grid=(length // tile,),
        in_specs=[
            SCALAR,
            rows(model),
            rows(model),
            rows(model),
            whole(gain),
            whole(router),
            rows(routes.shape[1]),
        ]
        + anywhere(earlier),
        out_specs=[rows(model), rows(model), rows(1), rows(count)] + [rows(w) for w in widths],
        out_shape=[shape(model), shape(model, jnp.bfloat16), shape(1), shape(count)]
        + [shape(w, jnp.bfloat16) for w in widths],
        compiler_params=kernel_params(),
        cost_estimate=lasting(9.0),
    )(side, tokens, mine, other, gain, router, routes, *earlier)


def chosen_slots(place_row, capacity):
    slot = lax.broadcasted_iota(jnp.int32, (capacity, place_row.shape[1]), 0)
    return jnp.where(place_row == slot, 1.0, 0.0).astype(jnp.bfloat16)


def pick_kernel(width, capacity, outputs, line_ref, tab_ref, slot_ref, *refs):
    outs = refs[len(refs) - outputs :]
    chosen = jnp.concatenate([chosen_slots(tab_ref[0, b], capacity) for b in range(width)])

    def give(rows, targets):
        for b in range(width):
            targets[b][0] = rows[b * capacity : (b + 1) * capacity].astype(jnp.bfloat16)

    give(dot(chosen, slot_ref[0]), outs[:width])
    if len(outs) > width:
        give(dot(chosen, refs[0][0]), outs[width:])


def pick_rows(line, tables, slots, capacity, small=None, earlier=()):
    count, width, _, length = tables.shape
    columns = slots.shape[2]
    if capacity % 16:
        slot = jnp.arange(capacity, dtype=jnp.int32)
        chosen = low(tables == slot[None, None, :, None])

        def taken(rows):
            picked = jnp.einsum("gbst,gtd->bgsd", chosen, rows, preferred_element_type=jnp.float32)
            return [low(picked[b]) for b in range(width)]

        near = slots[jnp.arange(count, dtype=jnp.int32) ^ line[0]]
        return taken(near) + ([] if small is None else taken(small))
    in_specs = [
        pl.BlockSpec((1, width, 1, length), lambda g, line: (g, 0, 0, 0)),
        pl.BlockSpec((1, length, columns), lambda g, line: (g ^ line[0], 0, 0)),
    ]
    out_specs = [pl.BlockSpec((1, capacity, columns), lambda g, line: (g, 0, 0))] * width
    out_shape = [jax.ShapeDtypeStruct((count, capacity, columns), jnp.bfloat16)] * width
    operands = [tables, slots]
    if small is not None:
        picks = small.shape[2]
        in_specs.append(pl.BlockSpec((1, length, picks), lambda g, line: (g, 0, 0)))
        out_specs += [pl.BlockSpec((1, capacity, picks), lambda g, line: (g, 0, 0))] * width
        out_shape += [jax.ShapeDtypeStruct((count, capacity, picks), jnp.bfloat16)] * width
        operands.append(small)
    return pl.pallas_call(
        functools.partial(pick_kernel, width, capacity, len(out_shape)),
        grid_spec=pltpu.PrefetchScalarGridSpec(
            num_scalar_prefetch=1,
            grid=(count,),
            in_specs=in_specs + anywhere(earlier),
            out_specs=out_specs,
        ),
        out_shape=out_shape,
        compiler_params=kernel_params(),
        cost_estimate=lasting(3.0 * count * columns / 768),
    )(line, *operands, *earlier)


def combine_kernel(width, capacity, line_ref, tab_ref, *refs):
    out_ref, token_ref = refs[-2:]
    token_ref[...] = jnp.zeros_like(token_ref)
    codes = tab_ref[0]
    total = width * capacity
    chosen = []
    for start in range(0, total, 128):
        size = min(128, total - start)
        slot = lax.broadcasted_iota(jnp.int32, (codes.shape[0], size), 1) + start
        hit = None
        for b in range(start // capacity, (start + size - 1) // capacity + 1):
            same = codes[:, b : b + 1] == slot
            hit = same if hit is None else hit | same
        chosen.append(jnp.where(hit, 1.0, 0.0).astype(jnp.bfloat16))
    rows = jnp.concatenate([refs[b][0] for b in range(width)])
    out_ref[0] = dot(jnp.concatenate(chosen, axis=1), rows).astype(out_ref.dtype)


def combine(line, table_columns, came, earlier=()):
    count, length, width = table_columns.shape
    _, capacity, columns = came[0].shape
    if capacity % 16:
        slot = jnp.arange(width * capacity, dtype=jnp.int32).reshape(width, capacity)
        chosen = low(table_columns[:, :, :, None] == slot)
        rows = jnp.stack(came)
        total = jnp.einsum("gtbs,bgsd->gtd", chosen, rows, preferred_element_type=jnp.float32)
        total = low(total[jnp.arange(count, dtype=jnp.int32) ^ line[0]])
        return total, total[:1, :8, :128]
    return pl.pallas_call(
        functools.partial(combine_kernel, width, capacity),
        grid_spec=pltpu.PrefetchScalarGridSpec(
            num_scalar_prefetch=1,
            grid=(count,),
            in_specs=[pl.BlockSpec((1, length, width), lambda g, line: (g, 0, 0))]
            + [pl.BlockSpec((1, capacity, columns), lambda g, line: (g, 0, 0))] * width
            + anywhere(earlier),
            out_specs=[
                pl.BlockSpec((1, length, columns), lambda g, line: (g ^ line[0], 0, 0)),
                pl.BlockSpec((1, 8, 128), lambda g, line: (0, 0, 0)),
            ],
        ),
        out_shape=[
            jax.ShapeDtypeStruct((count, length, columns), jnp.bfloat16),
            jax.ShapeDtypeStruct((1, 8, 128), jnp.float32),
        ],
        compiler_params=kernel_params(),
        cost_estimate=lasting(3.0 * count * columns / 768),
    )(line, table_columns, *came, *earlier)


def expert_kernel(count_in, count_cot, widths, width, me_ref, *refs):
    x_refs, refs = refs[: 2 * count_in], refs[2 * count_in :]
    c_refs, refs = refs[: 2 * count_cot], refs[2 * count_cot :]
    route_ref, wgu_ref, wd_ref, wr_ref, *outs = refs
    pre_ref, act_ref, term_ref = outs[:3]
    aways = outs[3 : 3 + len(widths)]
    homes = outs[3 + len(widths) :]
    side = me_ref[1]
    batch, _, capacity, _ = x_refs[0].shape
    half = sum(ref.shape[3] for ref in x_refs[:count_in])

    def flat(ref):
        return ref[...].reshape(batch * capacity, ref.shape[3])

    def keep(ref, rows):
        ref[...] = rows.reshape(ref.shape).astype(ref.dtype)

    def columns(which, start, size):
        return pl.ds(pl.multiple_of(which * half + start, 128), size)

    def spans(array_refs):
        count = len(array_refs) // 2
        for index, ref in enumerate(array_refs):
            which = side if index < count else 1 - side
            start = sum(r.shape[3] for r in array_refs[: index % count])
            yield flat(ref), columns(which, start, ref.shape[3])

    def through(weight_ref):
        total = None
        for rows, at in spans(x_refs):
            part = dot(rows, weight_ref[at, :])
            total = part if total is None else total + part
        return total

    both, logits = through(wgu_ref), through(wr_ref)
    units = both.shape[1] // 2
    gate_pre, up_pre = both[:, :units], both[:, units:]
    raw = None
    for rows, at in spans(c_refs):
        part = dot(rows, wd_ref[:, at], 1, 1)
        raw = part if raw is None else raw + part
    chance = routed_softmax(logits, flat(route_ref).astype(jnp.float32).astype(jnp.int32))
    label = lax.broadcasted_iota(jnp.int32, chance.shape, 1)
    gate = jnp.sum(jnp.where(label == me_ref[0], chance, 0.0), axis=1, keepdims=True)
    sig = jax.nn.sigmoid(gate_pre)
    silu = gate_pre * sig
    act = silu * up_pre
    keep(term_ref, jnp.sum(act * raw, axis=1, keepdims=True))
    keep(act_ref, act * gate)
    d_act = raw * gate
    d_gate = (d_act * up_pre * sig * (1.0 + gate_pre * (1.0 - sig))).astype(jnp.bfloat16)
    d_up = (d_act * silu).astype(jnp.bfloat16)
    d_both = jnp.concatenate([d_gate, d_up], axis=1)
    keep(pre_ref, d_both)
    start = 0
    for c, size in enumerate(widths):
        keep(aways[c], dot(d_both, wgu_ref[columns(1 - side, start, size), :], 1, 1))
        home = dot(d_both, wgu_ref[columns(side, start, size), :], 1, 1)
        home = home.astype(jnp.bfloat16).reshape(batch, capacity, size)
        give_homes(home, homes[c * width : (c + 1) * width])
        start += size


def give_homes(rows, homes):
    batch = rows.shape[0]
    for b in range(len(homes)):

        @pl.when(pl.program_id(0) == b // batch)
        def _(b=b):
            homes[b][0] = rows[b % batch]


def block_batch(width, capacity):
    return 1 if capacity % 16 else min(2, width)


def home_specs(width, batch, count, capacity, columns):
    return [
        pl.BlockSpec((1, capacity, columns), functools.partial(home_block, k // batch, count))
        for k in range(width)
    ]


def expert_rows(me, pieces, c_pieces, widths, routes, w_both, w_down, router):
    width, count, capacity, _ = pieces[0].shape
    units = w_down.shape[0]
    batch = block_batch(width, capacity)

    def rows(columns):
        return pl.BlockSpec((batch, 1, capacity, columns), lambda b, g: (b, g, 0, 0))

    def shape(columns, kind=jnp.bfloat16):
        return jax.ShapeDtypeStruct((width, count, capacity, columns), kind)

    out_specs = [rows(2 * units), rows(units), rows(1)] + [rows(size) for size in widths]
    out_shape = [shape(2 * units), shape(units), shape(1, jnp.float32)]
    out_shape += [shape(size) for size in widths]
    for size in widths:
        out_specs += home_specs(width, batch, count, capacity, size)
        out_shape += [jax.ShapeDtypeStruct((count, capacity, size), jnp.bfloat16)] * width
    outs = pl.pallas_call(
        functools.partial(expert_kernel, len(pieces) // 2, len(c_pieces) // 2, widths, width),
        grid=(width // batch, count),
        in_specs=[SCALAR]
        + [rows(piece.shape[3]) for piece in (*pieces, *c_pieces)]
        + [
            rows(routes.shape[3]),
            whole(w_both),
            whole(w_down),
            whole(router),
        ],
        out_specs=out_specs,
        out_shape=out_shape,
        compiler_params=kernel_params(),
        cost_estimate=lasting(10.0 * count),
    )(me, *pieces, *c_pieces, routes, w_both, w_down, router)
    aways, homes = outs[3 : 3 + len(widths)], outs[3 + len(widths) :]
    return (
        *outs[:3],
        [(aways[c], homes[c * width : (c + 1) * width]) for c in range(len(widths))],
    )


def pile_kernel(count, *refs):
    blocks, out_ref = refs[:count], refs[-1]
    for b in range(count):
        out_ref[b] = blocks[b][...]


def pile(blocks, earlier):
    slots, capacity, columns = blocks[0].shape
    count = len(blocks)
    return pl.pallas_call(
        functools.partial(pile_kernel, count),
        grid=(slots,),
        in_specs=[pl.BlockSpec((1, capacity, columns), lambda g: (g, 0, 0))] * count
        + anywhere(earlier),
        out_specs=pl.BlockSpec((count, 1, capacity, columns), lambda g: (0, g, 0, 0)),
        out_shape=jax.ShapeDtypeStruct((count, slots, capacity, columns), blocks[0].dtype),
        compiler_params=kernel_params(),
        cost_estimate=lasting(5.0),
    )(*blocks, *earlier)


def join_kernel(count, *refs):
    homes, swapped_ref, outs = refs[:count], refs[count], refs[len(refs) - count :]
    for b in range(count):
        total = homes[b][...].astype(jnp.float32) + swapped_ref[b].astype(jnp.float32)
        outs[b][...] = total.astype(jnp.bfloat16)


def join_cores(homes, swapped, earlier):
    slots, capacity, columns = homes[0].shape
    count = len(homes)
    block = pl.BlockSpec((1, capacity, columns), lambda g: (g, 0, 0))
    return pl.pallas_call(
        functools.partial(join_kernel, count),
        grid=(slots,),
        in_specs=[block] * count
        + [pl.BlockSpec((count, 1, capacity, columns), lambda g: (0, g, 0, 0))]
        + anywhere(earlier),
        out_specs=[block] * count,
        out_shape=[jax.ShapeDtypeStruct(homes[0].shape, jnp.bfloat16)] * count,
        compiler_params=kernel_params(),
        cost_estimate=lasting(7.0),
    )(*homes, swapped, *earlier)


def settle_kernel(pieces, side_ref, *refs):
    halves, refs = refs[: 2 * pieces], refs[2 * pieces :]
    hid_ref, inv_ref, cot_ref, gate_ref, term_ref, router_ref, gain_ref = refs[:7]
    dh_ref, db_ref, dl_ref, gg_ref = refs[-4:]
    gates, terms = gate_ref[...], term_ref[...]
    d_logits = gates * (terms - jnp.sum(gates * terms, axis=1, keepdims=True))
    d_logits = d_logits.astype(jnp.bfloat16)
    dl_ref[...] = jnp.zeros_like(dl_ref)
    dl_ref[:, : d_logits.shape[1]] = d_logits
    mine = jnp.concatenate([ref[...] for ref in halves[:pieces]], axis=1)
    other = jnp.concatenate([ref[...] for ref in halves[pieces:]], axis=1)
    first = side_ref[0] == 0
    rows = jnp.concatenate([jnp.where(first, mine, other), jnp.where(first, other, mine)], axis=1)
    d_second = rows.astype(jnp.float32) + dot(d_logits, router_ref[...], 1, 1)
    inverse = inv_ref[...]
    normed = hid_ref[...] * inverse
    scaled = d_second * gain_ref[...]
    gain_grad = jnp.sum(d_second * normed, axis=0, keepdims=True)

    @pl.when(pl.program_id(0) == 0)
    def _():
        gg_ref[...] = gain_grad

    @pl.when(pl.program_id(0) > 0)
    def _():
        gg_ref[...] += gain_grad

    center = jnp.mean(scaled * normed, axis=1, keepdims=True)
    d_hidden = cot_ref[...].astype(jnp.float32) + inverse * (scaled - normed * center)
    dh_ref[...] = d_hidden
    db_ref[...] = d_hidden.astype(jnp.bfloat16)


def settle(
    side, mine, other, hidden, inverse, cotangent, gates, terms, router, gain, tile, earlier
):
    length, model = hidden.shape
    count = router.shape[1]
    padded = count + 128 - count % 128

    def rows(columns):
        return pl.BlockSpec((tile, columns), lambda i: (i, 0))

    def shape(columns, kind=jnp.float32):
        return jax.ShapeDtypeStruct((length, columns), kind)

    return pl.pallas_call(
        functools.partial(settle_kernel, len(mine)),
        grid=(length // tile,),
        in_specs=[SCALAR]
        + [rows(piece.shape[1]) for piece in (*mine, *other)]
        + [rows(model), rows(1), rows(model), rows(count), rows(count), whole(router), whole(gain)]
        + anywhere(earlier),
        out_specs=[rows(model), rows(model), rows(padded), whole(gain)],
        out_shape=[
            shape(model),
            shape(model, jnp.bfloat16),
            shape(padded, jnp.bfloat16),
            jax.ShapeDtypeStruct(gain.shape, jnp.float32),
        ],
        compiler_params=kernel_params(),
        cost_estimate=lasting(10.0),
    )(side, *mine, *other, hidden, inverse, cotangent, gates, terms, router, gain, *earlier)


def finish_kernel(a_ref, b_ref, x_ref, inv_ref, dh_ref, gain_ref, out_ref):
    d_first = a_ref[...].astype(jnp.float32) + b_ref[...].astype(jnp.float32)
    inverse = inv_ref[...]
    normed = x_ref[...].astype(jnp.float32) * inverse
    scaled = d_first * gain_ref[...]
    center = jnp.mean(scaled * normed, axis=1, keepdims=True)
    out_ref[...] = dh_ref[...] + inverse * (scaled - normed * center)


def finish(mine, other, tokens, inverse, d_hidden, gain, tile):
    length, model = tokens.shape

    def rows(columns):
        return pl.BlockSpec((tile, columns), lambda i: (i, 0))

    return pl.pallas_call(
        finish_kernel,
        grid=(length // tile,),
        in_specs=[rows(model), rows(model), rows(model), rows(1), rows(model), whole(gain)],
        out_specs=rows(model),
        out_shape=jax.ShapeDtypeStruct((length, model), jnp.float32),
        compiler_params=kernel_params(),
        cost_estimate=lasting(8.0),
    )(mine, other, tokens, inverse, d_hidden, gain)


def home_block(k, count, b, g):
    return (jnp.where(b < k, 0, jnp.where(b > k, count - 1, g)), 0, 0)


def down_kernel(width, me_ref, act_ref, wd_ref, *refs):
    outs = refs[-1 - width :]
    away_ref, homes = outs[0], outs[1:]
    side = me_ref[1]
    batch, _, capacity, half = away_ref.shape
    mine = pl.ds(pl.multiple_of(side * half, half), half)
    other = pl.ds(pl.multiple_of((1 - side) * half, half), half)
    act = act_ref[...].reshape(batch * capacity, act_ref.shape[3])
    away_ref[...] = low(dot(act, wd_ref[:, other])).reshape(away_ref.shape)
    give_homes(low(dot(act, wd_ref[:, mine])).reshape(batch, capacity, half), homes)


def down_rows(me, act, w_down, earlier):
    width, count, capacity, units = act.shape
    half = w_down.shape[1] // 2
    batch = block_batch(width, capacity)

    def rows(columns):
        return pl.BlockSpec((batch, 1, capacity, columns), lambda b, g: (b, g, 0, 0))

    return pl.pallas_call(
        functools.partial(down_kernel, width),
        grid=(width // batch, count),
        in_specs=[SCALAR, rows(units), whole(w_down)] + anywhere(earlier),
        out_specs=[rows(half)] + home_specs(width, batch, count, capacity, half),
        out_shape=[jax.ShapeDtypeStruct((width, count, capacity, half), jnp.bfloat16)]
        + [jax.ShapeDtypeStruct((count, capacity, half), jnp.bfloat16)] * width,
        compiler_params=kernel_params(),
        cost_estimate=lasting(3.0 * count),
    )(me, act, w_down, *earlier)


def attend_back_kernel(
    heads,
    scale,
    tile,
    block,
    q_ref,
    k_ref,
    v_ref,
    segq_ref,
    segk_ref,
    lse_ref,
    db_ref,
    wo_ref,
    cos_ref,
    sin_ref,
    *refs,
):
    out_ref, dk_ref, dv_ref = refs[-3:]
    step = pl.program_id(0)
    length, size = k_ref.shape
    here = pl.ds(pl.multiple_of(step * tile, tile), tile)
    cosine, sine = cos_ref[here, :], sin_ref[here, :]

    def put(rows, start, array):
        out_ref[rows, start : start + size] = array.astype(jnp.bfloat16)

    @pl.when(step == 0)
    def _():
        dk_ref[...] = jnp.zeros_like(dk_ref)
        dv_ref[...] = jnp.zeros_like(dv_ref)

    d_mixed = dot(db_ref[...], wo_ref[...], 1, 1).astype(jnp.bfloat16)

    def work(seen):
        allowed = segk_ref[:seen] <= segq_ref[...]
        keys, values = k_ref[:seen], v_ref[:seen]
        keys_t = keys.T
        dk_total = jnp.zeros(keys.shape, jnp.float32)
        dv_total = jnp.zeros(keys.shape, jnp.float32)
        for head in range(heads):
            span = slice(head * size, (head + 1) * size)
            query = q_ref[:, span]
            d_head = d_mixed[:, span]
            scores = dot(keys, query, 1, 1) * scale - lse_ref[head : head + 1, :]
            probs = jnp.where(allowed, jnp.exp(scores), 0.0)
            d_probs = dot(values, d_head, 1, 1)
            scaled = probs * d_probs
            row_dot = jnp.sum(scaled, axis=0, keepdims=True)
            d_scores = (scale * (scaled - probs * row_dot)).astype(jnp.bfloat16)
            dv_total = dv_total + dot(probs.astype(jnp.bfloat16), d_head)
            dk_total = dk_total + dot(d_scores, query)
            d_query = dot(keys_t, d_scores).T
            put(here, head * size, turn(d_query, cosine, -sine))
        dk_ref[:seen] += dk_total
        dv_ref[:seen] += dv_total

    for at in range(length // tile):

        @pl.when(step == at)
        def _(at=at):
            work(min((at + 1) * tile + block, length))

    @pl.when(step == pl.num_programs(0) - 1)
    def _():
        base = heads * size
        put(slice(None), base, turn(dk_ref[...], cos_ref[...], -sin_ref[...]))
        put(slice(None), base + size, dv_ref[...])


def attend_back(
    query, keys, values, seg_row, seg_col, lse, d_branch, w_out, cosine, sine, scale, tile, earlier
):
    length, span = query.shape
    size = keys.shape[1]
    heads = span // size
    model = w_out.shape[1]
    out = jax.ShapeDtypeStruct((length, span + 2 * size), jnp.bfloat16)
    return pl.pallas_call(
        functools.partial(attend_back_kernel, heads, scale, tile, longest_block),
        grid=(length // tile,),
        in_specs=[
            pl.BlockSpec((tile, span), lambda i: (i, 0)),
            whole(keys),
            whole(values),
            pl.BlockSpec((1, tile), lambda i: (0, i)),
            whole(seg_col),
            pl.BlockSpec((heads, tile), lambda i: (0, i)),
            pl.BlockSpec((tile, model), lambda i: (i, 0)),
            whole(w_out),
            whole(cosine),
            whole(sine),
        ]
        + anywhere(earlier),
        out_specs=whole(out),
        out_shape=out,
        scratch_shapes=[pltpu.VMEM((length, size), jnp.float32)] * 2,
        compiler_params=kernel_params(),
        cost_estimate=lasting(28.0),
    )(query, keys, values, seg_row, seg_col, lse, d_branch, w_out, cosine, sine, *earlier)


def first_grad_kernel(d_ref, wq_ref, wk_ref, wv_ref, *refs):
    out_ref = refs[-1]
    span, size = wq_ref.shape[1], wk_ref.shape[1]
    total = dot(d_ref[:, :span], wq_ref[...], 1, 1)
    total = total + dot(d_ref[:, span : span + size], wk_ref[...], 1, 1)
    total = total + dot(d_ref[:, span + size :], wv_ref[...], 1, 1)
    out_ref[...] = total.astype(jnp.bfloat16)


def first_grad(d_all, w_query, w_key, w_value, tile, earlier):
    length, columns = d_all.shape
    model = w_query.shape[0]
    return pl.pallas_call(
        first_grad_kernel,
        grid=(length // tile,),
        in_specs=[
            pl.BlockSpec((tile, columns), lambda i: (i, 0)),
            whole(w_query),
            whole(w_key),
            whole(w_value),
        ]
        + anywhere(earlier),
        out_specs=pl.BlockSpec((tile, model), lambda i: (i, 0)),
        out_shape=jax.ShapeDtypeStruct((length, model), jnp.bfloat16),
        compiler_params=kernel_params(),
        cost_estimate=lasting(8.0),
    )(d_all, w_query, w_key, w_value, *earlier)


def share_kernel(width, rows, extra, spot_ref, left_ref, right_ref, *refs):
    kept_ref, *gone = refs[3 * extra : 3 * extra + width]
    hold_ref = refs[3 * extra + width]
    products = [(0, dot(left_ref[...], right_ref[...], 0, 0))]
    if extra:
        also_ref, picks_ref, row_ref = refs[:3]
        column = jnp.broadcast_to(row_ref[...], (8, row_ref.shape[1])).T[:, :1]
        more = dot(also_ref[...], picks_ref[...], 0, 0)
        lane = lax.broadcasted_iota(jnp.int32, more.shape, 1)
        last = more.shape[1] - 1
        products.append((right_ref.shape[1], jnp.where(lane == last, column, more)))
    for start, product in products:
        for s in range(width):
            part = product[s * rows : (s + 1) * rows]
            hold_ref[s, :, start : start + product.shape[1]] = part
    kept_ref[0] = hold_ref[spot_ref[0]]
    for b in range(1, width):
        gone[b - 1][0] = hold_ref[spot_ref[0] ^ b].astype(jnp.bfloat16)


def share_grads(spot, left, right, depth, width, extra=()):
    length, model = left.shape
    columns = right.shape[1] + (extra[1].shape[1] if extra else 0)
    rows = model // (depth * width)
    if (width * rows) % 128:
        product = dot(left, right, 0, 0)
        if extra:
            more = jnp.concatenate([dot(extra[0], extra[1], 0, 0)[:, :-1], extra[2].T], axis=1)
            product = jnp.concatenate([product, more], axis=1)
        parted = product.reshape(depth, width, rows, columns)
        blocks = [
            lax.dynamic_index_in_dim(parted, spot[0] ^ b, 1, keepdims=False) for b in range(width)
        ]
        return [blocks[0]] + [low(block) for block in blocks[1:]]
    block = pl.BlockSpec((1, rows, columns), lambda l: (l, 0, 0))
    stripe = pl.BlockSpec((length, width * rows), lambda l: (0, l))
    more_specs = []
    if extra:
        more_specs = [stripe, whole(extra[1]), pl.BlockSpec((1, width * rows), lambda l: (0, l))]
    return pl.pallas_call(
        functools.partial(share_kernel, width, rows, int(bool(extra))),
        grid=(depth,),
        in_specs=[SCALAR, stripe, whole(right)] + more_specs,
        out_specs=[block] * width,
        out_shape=[jax.ShapeDtypeStruct((depth, rows, columns), jnp.float32)]
        + [jax.ShapeDtypeStruct((depth, rows, columns), jnp.bfloat16)] * (width - 1),
        scratch_shapes=[pltpu.VMEM((width, rows, columns), jnp.float32)],
        compiler_params=kernel_params(),
        cost_estimate=lasting(6.0),
    )(spot, left, right, *extra)


class Exchange:
    def __init__(self, count):
        self.count = count
        self.depth = line_depth(count)
        self.width = count // self.depth
        self.me = lax.axis_index("expert")
        self.line = self.me // self.width
        self.lines = [[l * self.width + s for l in range(self.depth)] for s in range(self.width)]

    def flip(self, rows, mask):
        return lax.ppermute(rows, "expert", [(d, d ^ mask) for d in range(self.count)])

    def spread(self, rows):
        return lax.all_gather(rows, "expert", axis_index_groups=self.lines)

    def collect(self, parts):
        flat = parts.reshape(-1, parts.shape[-1])
        return lax.psum_scatter(
            flat, "expert", scatter_dimension=0, axis_index_groups=self.lines, tiled=True
        )

    def plane(self, blocks):
        return [blocks[0]] + [self.flip(blocks[b], b) for b in range(1, self.width)]

    def sum_plane(self, blocks):
        held = wide(blocks[0])
        for b in range(1, self.width):
            held = held + wide(self.flip(blocks[b], b))
        return held

    def sum_line(self, held):
        total = lax.dynamic_index_in_dim(held, self.line, 0, keepdims=False)
        for g in range(1, self.depth):
            part = lax.dynamic_index_in_dim(held, self.line ^ g, 0, keepdims=False)
            total = total + wide(self.flip(low(part), g * self.width))
        return total


def low(array):
    return array.astype(jnp.bfloat16)


def wide(array):
    return array.astype(jnp.float32)


def swap(rows):
    return lax.ppermute(rows, "tensor", [(0, 1), (1, 0)])


def half_of(array, side):
    width = array.shape[-1] // 2
    return lax.dynamic_slice_in_dim(array, side * width, width, array.ndim - 1)


def join_halves(mine, other, side):
    first = jnp.where(side == 0, mine, other)
    last = jnp.where(side == 0, other, mine)
    return jnp.concatenate([first, last], axis=-1)


def on_device(
    tokens,
    cotangent,
    norm_gain,
    ffn_gain,
    w_query,
    w_key,
    w_value,
    w_out,
    w_router,
    w_gate,
    w_up,
    w_down,
    routes,
    order,
    segments,
):
    seq_length, model_width = tokens.shape
    half_width = model_width // 2
    expert_count = w_router.shape[1]
    pick_count = routes.shape[1]
    capacity = 9 * seq_length * pick_count // (8 * expert_count)
    head_width = w_key.shape[1]
    span = w_query.shape[1]
    unit_count = w_down.shape[1]
    score_scale = 1.0 / math.sqrt(head_width)
    tile = 256
    link = Exchange(expert_count)
    depth, width = link.depth, link.width
    side = lax.axis_index("tensor")
    side_ref = side.astype(jnp.int32)[None]
    me_ref = jnp.stack([link.me, side]).astype(jnp.int32)
    line_ref = link.line.astype(jnp.int32)[None]

    third = half_width // 3
    widths = (2 * third, third)
    cot_slots = link.spread(half_of(cotangent, side))
    placed = place_table(routes, order[0], link.me, expert_count, capacity)
    tables = []
    for g in range(depth):
        table = jnp.concatenate([placed[g * width : (g + 1) * width], routes.T], axis=0)
        tables.append(table if g == 0 else link.flip(table, g * width))
    places = jnp.stack([table[:width] for table in tables])
    place_rows = places[:, :, None, :]
    starts = capacity * jnp.arange(width, dtype=jnp.int32)
    place_columns = jnp.where(places >= 0, places + starts[None, :, None], -1)
    place_columns = jnp.swapaxes(place_columns, 1, 2)
    route_columns = jnp.stack([low(table[width:].T) for table in tables])

    route_blocks = link.plane(
        pick_rows(jnp.zeros_like(line_ref), place_rows, route_columns, capacity)
    )
    route_rows = jnp.stack(route_blocks)

    cosine, sine = (jnp.asarray(t) for t in rope_constants(seq_length, head_width))
    first_in, query, keys, values, inverse_first = project(
        tokens, norm_gain[None], w_query, w_key, w_value, cosine, sine, tile
    )
    seg_row, seg_col = segments, segments[0][:, None]
    mixed, lse, branch = attend(
        query, keys, values, seg_row, seg_col, w_out, score_scale, tile
    )
    hidden, second_in, inverse_second, gates, *in_parts = second_norm(
        side_ref,
        tokens,
        branch,
        swap(branch),
        ffn_gain[None],
        w_router,
        routes,
        tile,
        widths,
        (place_rows, route_rows),
    )
    w_both = jnp.concatenate([w_gate[0], w_up[0]], axis=1)
    in_slots = [link.spread(hold(in_parts[0], cot_slots))]
    cot_blocks = pick_rows(line_ref, place_rows, cot_slots, capacity, None, (second_in, w_both))
    cot_came = link.plane(cot_blocks)
    in_slots.append(link.spread(hold(in_parts[1], in_slots[0], *cot_came[1:])))
    in_first = pick_rows(line_ref, place_rows, in_slots[0], capacity)
    in_came = [link.plane(in_first)]
    in_last = pick_rows(line_ref, place_rows, in_slots[1], capacity, None, in_came[0][1:])
    in_came.append(link.plane(in_last))
    cot_mine = pile(cot_came, in_last[1:])
    cot_other = swap(cot_mine)
    in_mine = [pile(in_came[0], (cot_mine,))]
    in_other = [swap(in_mine[0])]
    in_mine.append(pile(in_came[1], (in_other[0], cot_other)))
    in_other.append(swap(in_mine[1]))
    pieces, c_pieces = in_mine + in_other, [cot_mine, cot_other]

    pre, acts, terms, backs = expert_rows(
        me_ref, pieces, c_pieces, widths[::-1], route_rows, w_both, w_down[0], w_router
    )
    swapped = [swap(away) for away, _ in backs]
    first_came = link.plane(join_cores(backs[0][1], swapped[0], ()))
    out_away, *out_homes = down_rows(me_ref, acts, w_down[0], ())
    terms = hold(terms, out_away)[..., 0]
    terms = jnp.stack(link.plane([terms[b] for b in range(width)]), axis=1)
    blocks = join_cores(backs[1][1], swapped[1], (*first_came[1:], out_away))
    first_part, first_token = combine(line_ref, place_columns, first_came, blocks[1:])
    row_parts = [first_part]
    came = link.plane(blocks)
    last_part, last_token = combine(line_ref, place_columns, came, (first_token,))
    row_parts.append(last_part)
    out_blocks = join_cores(out_homes, swap(out_away), (last_token, terms))
    out_came = link.plane(out_blocks)
    row_mine = [link.collect(row_parts[0])]
    row_mine.append(link.collect(hold(row_parts[1], row_mine[0])))
    row_other = [swap(part) for part in row_mine]

    terms = hold(terms, *out_blocks[1:])
    slot_ids = jnp.arange(capacity, dtype=jnp.int32)
    local = jnp.sum(
        jnp.where(
            places[:, :, None, :] == slot_ids[None, None, :, None], terms[:, :, :, None], 0.0
        ),
        axis=2,
    )
    term_table = jnp.concatenate(
        [local[g] if g == 0 else link.flip(local[g], g * width) for g in range(depth)]
    )
    term_table = term_table + swap(term_table)
    term_table = term_table[jnp.arange(expert_count, dtype=jnp.int32) ^ link.me].T

    act_rows = hold(acts, *out_blocks[1:]).reshape(-1, unit_count)
    grads = [contract_rows(act_rows, piece.reshape(-1, piece.shape[3])) for piece in c_pieces]
    down_grad = join_halves(
        *grads, side
    )[None]
    pre = hold(pre, term_table, down_grad).reshape(-1, 2 * unit_count)
    grads = [contract_rows(piece.reshape(-1, piece.shape[3]), pre) for piece in pieces]
    first, last = jnp.concatenate(grads[:2]), jnp.concatenate(grads[2:])
    upper, lower = jnp.where(side == 0, first, last), jnp.where(side == 0, last, first)
    gate_grad = jnp.concatenate([upper[:, :unit_count], lower[:, :unit_count]])[None]
    up_grad = jnp.concatenate([upper[:, unit_count:], lower[:, unit_count:]])[None]

    d_hidden, d_branch, d_logits, ffn_gain_grad = settle(
        side_ref,
        row_mine,
        row_other,
        hidden,
        inverse_second,
        cotangent,
        gates,
        term_table,
        w_router,
        ffn_gain[None],
        tile,
        (down_grad, gate_grad, up_grad),
    )

    out_parts, _ = combine(line_ref, place_columns, out_came, (d_branch,))
    out_held = hold(out_parts, row_mine[1])
    spot_ref = (link.me % width).astype(jnp.int32)[None]
    shared_early = share_grads(
        spot_ref, d_branch, mixed, depth, width, (second_in, d_logits, ffn_gain_grad)
    )
    early_held = link.sum_plane(shared_early)

    d_all = attend_back(
        query,
        keys,
        values,
        seg_row,
        seg_col,
        lse,
        d_branch,
        w_out,
        cosine,
        sine,
        score_scale,
        tile,
        (*shared_early[1:], out_held),
    )
    d_first = first_grad(d_all, w_query, w_key, w_value, tile, (early_held,))
    input_grad = finish(
        d_first, swap(d_first), tokens, inverse_first, d_hidden, norm_gain[None], tile
    )
    shared = share_grads(spot_ref, first_in, hold(d_all, d_first), depth, width)
    shared = [hold(shared[0], input_grad), *shared[1:]]
    summed = link.sum_line(jnp.concatenate([link.sum_plane(shared), early_held], axis=2))
    columns = span + 2 * head_width
    qkv_grad, early_sum = summed[:, :columns], summed[:, columns:]
    out_grad = early_sum[:, :span].T
    router_grad, ffn_gain_grad = early_sum[:, span : span + expert_count], early_sum[:, -1]
    combined = wide(hold(link.collect(out_held), qkv_grad))
    output_half = low(half_of(hidden, side) + combined)
    output = join_halves(output_half, swap(output_half), side)
    rows = model_width // expert_count
    gain_part = jnp.zeros((rows,), jnp.float32)
    start = 0
    for weight in (w_query, w_key, w_value):
        mine = lax.dynamic_slice_in_dim(weight, link.me * rows, rows, 0)
        grads = qkv_grad[:, start : start + weight.shape[1]]
        gain_part = gain_part + jnp.sum(grads * wide(mine), axis=1)
        start += weight.shape[1]
    gain_part = gain_part / lax.dynamic_slice_in_dim(norm_gain, link.me * rows, rows, 0)
    norm_gain_grad = gain_part + swap(gain_part)
    return (
        output,
        input_grad,
        norm_gain_grad,
        ffn_gain_grad,
        qkv_grad[:, :span],
        qkv_grad[:, span : span + head_width],
        qkv_grad[:, span + head_width :],
        out_grad,
        router_grad,
        gate_grad,
        up_grad,
        down_grad,
    )


def solution(mesh):
    placed = (
        P("expert", None),
        P("expert", None),
        P(),
        P(),
        P(None, "tensor"),
        P(None, "tensor"),
        P(None, "tensor"),
        P("tensor", None),
        P(),
        P("expert", None, "tensor"),
        P("expert", None, "tensor"),
        P("expert", "tensor", None),
        P("expert", None),
        P("expert", None),
        P("expert", None),
    )
    return jax.shard_map(
        on_device,
        mesh=mesh,
        in_specs=placed,
        out_specs=(
            P("expert", None),
            P("expert", None),
            P("expert"),
            P("expert"),
            P("expert", "tensor"),
            P("expert", "tensor"),
            P("expert", "tensor"),
            P("tensor", "expert"),
            P("expert", None),
            P("expert", None, "tensor"),
            P("expert", None, "tensor"),
            P("expert", "tensor", None),
        ),
        check_vma=False,
    )
```

```python
import functools
import math

import jax
import jax.numpy as jnp
import numpy as np
from jax import lax
from jax.experimental import pallas as pl
from jax.experimental.pallas import tpu as pltpu
from jax.sharding import PartitionSpec as P

epsilon = 1e-06
rope_base = 1000000.0
masked_score = -1e30


def contract_rows(left, right):
    return lax.dot_general(
        left, right, (((0,), (0,)), ((), ())), preferred_element_type=jnp.float32
    )


def times_transposed(left, right):
    return lax.dot_general(
        left, right, (((1,), (1,)), ((), ())), preferred_element_type=jnp.float32
    )


def line_depth(count):
    depth = 1
    while depth * depth * 4 <= count:
        depth *= 2
    return depth


longest_block = 256
VMEM_LIMIT = 56 * 1024 * 1024


def kernel_params(*semantics):
    return pltpu.CompilerParams(vmem_limit_bytes=VMEM_LIMIT)


def lasting(microseconds):
    return pl.CostEstimate(
        flops=int(microseconds * 1.0e6), bytes_accessed=1024, transcendentals=0
    )


def hold_kernel(*refs):
    del refs


def hold(array, *earlier):
    return pl.pallas_call(
        hold_kernel,
        in_specs=anywhere((array, *earlier)),
        out_specs=pl.BlockSpec(memory_space=pl.ANY),
        out_shape=jax.ShapeDtypeStruct(array.shape, array.dtype),
        input_output_aliases={0: 0},
    )(array, *earlier)


def whole(array):
    return pl.BlockSpec(array.shape, lambda *_: (0,) * array.ndim)


def anywhere(arrays):
    return [pl.BlockSpec(memory_space=pl.ANY)] * len(arrays)


SCALAR = pl.BlockSpec(memory_space=pltpu.SMEM)


def dot(left, right, left_axis=1, right_axis=0):
    return lax.dot_general(
        left,
        right,
        (((left_axis,), (right_axis,)), ((), ())),
        preferred_element_type=jnp.float32,
    )


def rope_constants(seq_length, head_width):
    half = head_width // 2
    frequency = np.exp(-math.log(rope_base) * np.arange(half) * (2.0 / head_width))
    angle = np.arange(seq_length)[:, None] * frequency[None, :]
    cosine, sine = np.cos(angle), np.sin(angle)
    return (
        np.concatenate([cosine, cosine], axis=1).astype(np.float32),
        np.concatenate([-sine, sine], axis=1).astype(np.float32),
    )


def place_kernel(seq_length, capacity, keys_ref, out_ref):
    block = keys_ref[...]
    columns = block.T
    limit = seq_length * 1024
    for row in range(block.shape[0]):
        mine = block[row : row + 1, :]
        total = jnp.zeros((1, seq_length), jnp.float32)
        for start in range(0, seq_length, 256):
            less = columns[start : start + 256, row : row + 1] < mine
            total = total + jnp.sum(jnp.where(less, 1.0, 0.0), axis=0, keepdims=True)
        kept = (mine < limit) & (total < capacity)
        out_ref[row : row + 1, :] = jnp.where(kept, total, -1.0).astype(jnp.int32)


def place_table(routes, order, me, expert_count, capacity):
    seq_length = routes.shape[0]
    relabeled = (routes ^ me).T
    ranks = order.reshape(routes.shape).T
    labels = jnp.arange(expert_count, dtype=jnp.int32)
    hit = relabeled[:, None, :] == labels[None, :, None]
    rank = jnp.sum(jnp.where(hit, ranks[:, None, :] + 1, 0), axis=0)
    rank = jnp.where(rank > 0, rank, seq_length * 1024)
    spec = pl.BlockSpec((8, seq_length), lambda e: (e, 0))
    return pl.pallas_call(
        functools.partial(place_kernel, seq_length, capacity),
        grid=(expert_count // 8,),
        out_shape=jax.ShapeDtypeStruct(rank.shape, jnp.int32),
        in_specs=[spec],
        out_specs=spec,
        compiler_params=kernel_params(),
        cost_estimate=lasting(9.0 * expert_count / 16),
    )(rank)


def turn(values, cosine, sine):
    return values * cosine + pltpu.roll(values, values.shape[1] // 2, 1) * sine


def project_kernel(
    heads, x_ref, gain_ref, wq_ref, wk_ref, wv_ref, cos_ref, sin_ref, in_ref, q_ref, k_ref, v_ref, inv_ref
):
    source = x_ref[...].astype(jnp.float32)
    inverse = lax.rsqrt(jnp.mean(source * source, axis=1, keepdims=True) + epsilon)
    first = (source * inverse * gain_ref[...]).astype(jnp.bfloat16)
    in_ref[...] = first
    inv_ref[...] = inverse
    cosine, sine = cos_ref[...], sin_ref[...]
    size = cosine.shape[1]
    query = dot(first, wq_ref[...])
    for head in range(heads):
        span = slice(head * size, (head + 1) * size)
        q_ref[:, span] = turn(query[:, span], cosine, sine).astype(jnp.bfloat16)
    k_ref[...] = turn(dot(first, wk_ref[...]), cosine, sine).astype(jnp.bfloat16)
    v_ref[...] = dot(first, wv_ref[...]).astype(jnp.bfloat16)


def project(tokens, gain, w_query, w_key, w_value, cosine, sine, tile):
    length, model = tokens.shape
    size = w_key.shape[1]
    span = w_query.shape[1]

    def rows(columns):
        return pl.BlockSpec((tile, columns), lambda i: (i, 0))

    def shape(columns, kind=jnp.bfloat16):
        return jax.ShapeDtypeStruct((length, columns), kind)

    return pl.pallas_call(
        functools.partial(project_kernel, span // size),
        grid=(length // tile,),
        in_specs=[
            rows(model),
            whole(gain),
            whole(w_query),
            whole(w_key),
            whole(w_value),
            rows(size),
            rows(size),
        ],
        out_specs=[rows(model), rows(span), rows(size), rows(size), rows(1)],
        out_shape=[shape(model), shape(span), shape(size), shape(size), shape(1, jnp.float32)],
        compiler_params=kernel_params(),
        cost_estimate=lasting(9.0),
    )(tokens, gain, w_query, w_key, w_value, cosine, sine)


def attend_kernel(
    heads, scale, q_ref, k_ref, v_ref, segq_ref, segk_ref, wo_ref, mix_ref, lse_ref, branch_ref
):
    allowed = segk_ref[...] <= segq_ref[...]
    keys = k_ref[...]
    values = v_ref[...].T
    size = keys.shape[1]
    for head in range(heads):
        span = slice(head * size, (head + 1) * size)
        scores = dot(keys, q_ref[:, span], 1, 1)
        scores = jnp.where(allowed, scores * scale, masked_score)
        top = jnp.max(scores, axis=0, keepdims=True)
        spread = jnp.exp(scores - top)
        total = jnp.sum(spread, axis=0, keepdims=True)
        mixed = dot(values, spread.astype(jnp.bfloat16)) / total
        mix_ref[:, span] = mixed.T.astype(jnp.bfloat16)
        lse_ref[head : head + 1, :] = top + jnp.log(total)
    branch_ref[...] = dot(mix_ref[...], wo_ref[...]).astype(jnp.bfloat16)


def attend(query, keys, values, seg_row, seg_col, w_out, scale, tile):
    length, span = query.shape
    size = keys.shape[1]
    heads = span // size
    model = w_out.shape[1]
    rows = pl.BlockSpec((tile, span), lambda i: (i, 0))
    return pl.pallas_call(
        functools.partial(attend_kernel, heads, scale),
        grid=(length // tile,),
        in_specs=[
            rows,
            whole(keys),
            whole(values),
            pl.BlockSpec((1, tile), lambda i: (0, i)),
            whole(seg_col),
            whole(w_out),
        ],
        out_specs=[
            rows,
            pl.BlockSpec((heads, tile), lambda i: (0, i)),
            pl.BlockSpec((tile, model), lambda i: (i, 0)),
        ],
        out_shape=[
            jax.ShapeDtypeStruct((length, span), jnp.bfloat16),
            jax.ShapeDtypeStruct((heads, length), jnp.float32),
            jax.ShapeDtypeStruct((length, model), jnp.bfloat16),
        ],
        compiler_params=kernel_params(),
        cost_estimate=lasting(20.0),
    )(query, keys, values, seg_row, seg_col, w_out)


def second_kernel(
    outputs, side_ref, x_ref, a_ref, b_ref, gain_ref, router_ref, routes_ref, *refs
):
    refs = refs[len(refs) - outputs :]
    hidden_ref, in_ref, inv_ref, gate_ref, *parts = refs
    hidden = x_ref[...].astype(jnp.float32) + (
        a_ref[...].astype(jnp.float32) + b_ref[...].astype(jnp.float32)
    )
    inverse = lax.rsqrt(jnp.mean(hidden * hidden, axis=1, keepdims=True) + epsilon)
    second = (hidden * inverse * gain_ref[...]).astype(jnp.bfloat16)
    hidden_ref[...] = hidden
    in_ref[...] = second
    inv_ref[...] = inverse
    half = second.shape[1] // 2
    sent = jnp.where(side_ref[0] == 0, second[:, :half], second[:, half:])
    start = 0
    for part in parts:
        part[...] = sent[:, start : start + part.shape[1]]
        start += part.shape[1]
    logits = dot(second, router_ref[...])
    gate_ref[...] = routed_softmax(logits, routes_ref[...])


def routed_softmax(logits, routes):
    labels = lax.broadcasted_iota(jnp.int32, logits.shape, 1)
    picked = routes[:, 0:1] == labels
    for k in range(1, routes.shape[1]):
        picked = picked | (routes[:, k : k + 1] == labels)
    masked = jnp.where(picked, logits, masked_score)
    spread = jnp.exp(masked - jnp.max(masked, axis=1, keepdims=True))
    return spread / jnp.sum(spread, axis=1, keepdims=True)


def second_norm(side, tokens, mine, other, gain, router, routes, tile, widths, earlier):
    length, model = tokens.shape
    count = router.shape[1]

    def rows(columns):
        return pl.BlockSpec((tile, columns), lambda i: (i, 0))

    def shape(columns, kind=jnp.float32):
        return jax.ShapeDtypeStruct((length, columns), kind)

    return pl.pallas_call(
        functools.partial(second_kernel, 4 + len(widths)),
        grid=(length // tile,),
        in_specs=[
            SCALAR,
            rows(model),
            rows(model),
            rows(model),
            whole(gain),
            whole(router),
            rows(routes.shape[1]),
        ]
        + anywhere(earlier),
        out_specs=[rows(model), rows(model), rows(1), rows(count)] + [rows(w) for w in widths],
        out_shape=[shape(model), shape(model, jnp.bfloat16), shape(1), shape(count)]
        + [shape(w, jnp.bfloat16) for w in widths],
        compiler_params=kernel_params(),
        cost_estimate=lasting(9.0),
    )(side, tokens, mine, other, gain, router, routes, *earlier)


def chosen_slots(place_row, capacity):
    slot = lax.broadcasted_iota(jnp.int32, (capacity, place_row.shape[1]), 0)
    return jnp.where(place_row == slot, 1.0, 0.0).astype(jnp.bfloat16)


def pick_kernel(width, capacity, outputs, line_ref, tab_ref, slot_ref, *refs):
    outs = refs[len(refs) - outputs :]
    chosen = jnp.concatenate([chosen_slots(tab_ref[0, b], capacity) for b in range(width)])

    def give(rows, targets):
        for b in range(width):
            targets[b][0] = rows[b * capacity : (b + 1) * capacity].astype(jnp.bfloat16)

    give(dot(chosen, slot_ref[0]), outs[:width])
    if len(outs) > width:
        give(dot(chosen, refs[0][0]), outs[width:])


def pick_rows(line, tables, slots, capacity, small=None, earlier=()):
    count, width, _, length = tables.shape
    columns = slots.shape[2]
    if capacity % 16:
        slot = jnp.arange(capacity, dtype=jnp.int32)
        chosen = low(tables == slot[None, None, :, None])

        def taken(rows):
            picked = jnp.einsum("gbst,gtd->bgsd", chosen, rows, preferred_element_type=jnp.float32)
            return [low(picked[b]) for b in range(width)]

        near = slots[jnp.arange(count, dtype=jnp.int32) ^ line[0]]
        return taken(near) + ([] if small is None else taken(small))
    in_specs = [
        pl.BlockSpec((1, width, 1, length), lambda g, line: (g, 0, 0, 0)),
        pl.BlockSpec((1, length, columns), lambda g, line: (g ^ line[0], 0, 0)),
    ]
    out_specs = [pl.BlockSpec((1, capacity, columns), lambda g, line: (g, 0, 0))] * width
    out_shape = [jax.ShapeDtypeStruct((count, capacity, columns), jnp.bfloat16)] * width
    operands = [tables, slots]
    if small is not None:
        picks = small.shape[2]
        in_specs.append(pl.BlockSpec((1, length, picks), lambda g, line: (g, 0, 0)))
        out_specs += [pl.BlockSpec((1, capacity, picks), lambda g, line: (g, 0, 0))] * width
        out_shape += [jax.ShapeDtypeStruct((count, capacity, picks), jnp.bfloat16)] * width
        operands.append(small)
    return pl.pallas_call(
        functools.partial(pick_kernel, width, capacity, len(out_shape)),
        grid_spec=pltpu.PrefetchScalarGridSpec(
            num_scalar_prefetch=1,
            grid=(count,),
            in_specs=in_specs + anywhere(earlier),
            out_specs=out_specs,
        ),
        out_shape=out_shape,
        compiler_params=kernel_params(),
        cost_estimate=lasting(3.0 * count * columns / 768),
    )(line, *operands, *earlier)


def combine_kernel(width, capacity, line_ref, tab_ref, *refs):
    out_ref, token_ref = refs[-2:]
    token_ref[...] = jnp.zeros_like(token_ref)
    codes = tab_ref[0]
    total = width * capacity
    chosen = []
    for start in range(0, total, 128):
        size = min(128, total - start)
        slot = lax.broadcasted_iota(jnp.int32, (codes.shape[0], size), 1) + start
        hit = None
        for b in range(start // capacity, (start + size - 1) // capacity + 1):
            same = codes[:, b : b + 1] == slot
            hit = same if hit is None else hit | same
        chosen.append(jnp.where(hit, 1.0, 0.0).astype(jnp.bfloat16))
    rows = jnp.concatenate([refs[b][0] for b in range(width)])
    out_ref[0] = dot(jnp.concatenate(chosen, axis=1), rows).astype(out_ref.dtype)


def combine(line, table_columns, came, earlier=()):
    count, length, width = table_columns.shape
    _, capacity, columns = came[0].shape
    if capacity % 16:
        slot = jnp.arange(width * capacity, dtype=jnp.int32).reshape(width, capacity)
        chosen = low(table_columns[:, :, :, None] == slot)
        rows = jnp.stack(came)
        total = jnp.einsum("gtbs,bgsd->gtd", chosen, rows, preferred_element_type=jnp.float32)
        total = low(total[jnp.arange(count, dtype=jnp.int32) ^ line[0]])
        return total, total[:1, :8, :128]
    return pl.pallas_call(
        functools.partial(combine_kernel, width, capacity),
        grid_spec=pltpu.PrefetchScalarGridSpec(
            num_scalar_prefetch=1,
            grid=(count,),
            in_specs=[pl.BlockSpec((1, length, width), lambda g, line: (g, 0, 0))]
            + [pl.BlockSpec((1, capacity, columns), lambda g, line: (g, 0, 0))] * width
            + anywhere(earlier),
            out_specs=[
                pl.BlockSpec((1, length, columns), lambda g, line: (g ^ line[0], 0, 0)),
                pl.BlockSpec((1, 8, 128), lambda g, line: (0, 0, 0)),
            ],
        ),
        out_shape=[
            jax.ShapeDtypeStruct((count, length, columns), jnp.bfloat16),
            jax.ShapeDtypeStruct((1, 8, 128), jnp.float32),
        ],
        compiler_params=kernel_params(),
        cost_estimate=lasting(3.0 * count * columns / 768),
    )(line, table_columns, *came, *earlier)


def expert_kernel(count_in, count_cot, widths, width, me_ref, *refs):
    x_refs, refs = refs[: 2 * count_in], refs[2 * count_in :]
    c_refs, refs = refs[: 2 * count_cot], refs[2 * count_cot :]
    route_ref, wgu_ref, wd_ref, wr_ref, *outs = refs
    pre_ref, act_ref, term_ref = outs[:3]
    aways = outs[3 : 3 + len(widths)]
    homes = outs[3 + len(widths) :]
    side = me_ref[1]
    batch, _, capacity, _ = x_refs[0].shape
    half = sum(ref.shape[3] for ref in x_refs[:count_in])

    def flat(ref):
        return ref[...].reshape(batch * capacity, ref.shape[3])

    def keep(ref, rows):
        ref[...] = rows.reshape(ref.shape).astype(ref.dtype)

    def columns(which, start, size):
        return pl.ds(pl.multiple_of(which * half + start, 128), size)

    def spans(array_refs):
        count = len(array_refs) // 2
        for index, ref in enumerate(array_refs):
            which = side if index < count else 1 - side
            start = sum(r.shape[3] for r in array_refs[: index % count])
            yield flat(ref), columns(which, start, ref.shape[3])

    def through(weight_ref):
        total = None
        for rows, at in spans(x_refs):
            part = dot(rows, weight_ref[at, :])
            total = part if total is None else total + part
        return total

    both, logits = through(wgu_ref), through(wr_ref)
    units = both.shape[1] // 2
    gate_pre, up_pre = both[:, :units], both[:, units:]
    raw = None
    for rows, at in spans(c_refs):
        part = dot(rows, wd_ref[:, at], 1, 1)
        raw = part if raw is None else raw + part
    chance = routed_softmax(logits, flat(route_ref).astype(jnp.float32).astype(jnp.int32))
    label = lax.broadcasted_iota(jnp.int32, chance.shape, 1)
    gate = jnp.sum(jnp.where(label == me_ref[0], chance, 0.0), axis=1, keepdims=True)
    sig = jax.nn.sigmoid(gate_pre)
    silu = gate_pre * sig
    act = silu * up_pre
    keep(term_ref, jnp.sum(act * raw, axis=1, keepdims=True))
    keep(act_ref, act * gate)
    d_act = raw * gate
    d_gate = (d_act * up_pre * sig * (1.0 + gate_pre * (1.0 - sig))).astype(jnp.bfloat16)
    d_up = (d_act * silu).astype(jnp.bfloat16)
    d_both = jnp.concatenate([d_gate, d_up], axis=1)
    keep(pre_ref, d_both)
    start = 0
    for c, size in enumerate(widths):
        keep(aways[c], dot(d_both, wgu_ref[columns(1 - side, start, size), :], 1, 1))
        home = dot(d_both, wgu_ref[columns(side, start, size), :], 1, 1)
        home = home.astype(jnp.bfloat16).reshape(batch, capacity, size)
        give_homes(home, homes[c * width : (c + 1) * width])
        start += size


def give_homes(rows, homes):
    batch = rows.shape[0]
    for b in range(len(homes)):

        @pl.when(pl.program_id(0) == b // batch)
        def _(b=b):
            homes[b][0] = rows[b % batch]


def block_batch(width, capacity):
    return 1 if capacity % 16 else min(2, width)


def home_specs(width, batch, count, capacity, columns):
    return [
        pl.BlockSpec((1, capacity, columns), functools.partial(home_block, k // batch, count))
        for k in range(width)
    ]


def expert_rows(me, pieces, c_pieces, widths, routes, w_both, w_down, router):
    width, count, capacity, _ = pieces[0].shape
    units = w_down.shape[0]
    batch = block_batch(width, capacity)

    def rows(columns):
        return pl.BlockSpec((batch, 1, capacity, columns), lambda b, g: (b, g, 0, 0))

    def shape(columns, kind=jnp.bfloat16):
        return jax.ShapeDtypeStruct((width, count, capacity, columns), kind)

    out_specs = [rows(2 * units), rows(units), rows(1)] + [rows(size) for size in widths]
    out_shape = [shape(2 * units), shape(units), shape(1, jnp.float32)]
    out_shape += [shape(size) for size in widths]
    for size in widths:
        out_specs += home_specs(width, batch, count, capacity, size)
        out_shape += [jax.ShapeDtypeStruct((count, capacity, size), jnp.bfloat16)] * width
    outs = pl.pallas_call(
        functools.partial(expert_kernel, len(pieces) // 2, len(c_pieces) // 2, widths, width),
        grid=(width // batch, count),
        in_specs=[SCALAR]
        + [rows(piece.shape[3]) for piece in (*pieces, *c_pieces)]
        + [
            rows(routes.shape[3]),
            whole(w_both),
            whole(w_down),
            whole(router),
        ],
        out_specs=out_specs,
        out_shape=out_shape,
        compiler_params=kernel_params(),
        cost_estimate=lasting(10.0 * count),
    )(me, *pieces, *c_pieces, routes, w_both, w_down, router)
    aways, homes = outs[3 : 3 + len(widths)], outs[3 + len(widths) :]
    return (
        *outs[:3],
        [(aways[c], homes[c * width : (c + 1) * width]) for c in range(len(widths))],
    )


def pile_kernel(count, *refs):
    blocks, out_ref = refs[:count], refs[-1]
    for b in range(count):
        out_ref[b] = blocks[b][...]


def pile(blocks, earlier):
    slots, capacity, columns = blocks[0].shape
    count = len(blocks)
    return pl.pallas_call(
        functools.partial(pile_kernel, count),
        grid=(slots,),
        in_specs=[pl.BlockSpec((1, capacity, columns), lambda g: (g, 0, 0))] * count
        + anywhere(earlier),
        out_specs=pl.BlockSpec((count, 1, capacity, columns), lambda g: (0, g, 0, 0)),
        out_shape=jax.ShapeDtypeStruct((count, slots, capacity, columns), blocks[0].dtype),
        compiler_params=kernel_params(),
        cost_estimate=lasting(5.0),
    )(*blocks, *earlier)


def join_kernel(count, *refs):
    homes, swapped_ref, outs = refs[:count], refs[count], refs[len(refs) - count :]
    for b in range(count):
        total = homes[b][...].astype(jnp.float32) + swapped_ref[b].astype(jnp.float32)
        outs[b][...] = total.astype(jnp.bfloat16)


def join_cores(homes, swapped, earlier):
    slots, capacity, columns = homes[0].shape
    count = len(homes)
    block = pl.BlockSpec((1, capacity, columns), lambda g: (g, 0, 0))
    return pl.pallas_call(
        functools.partial(join_kernel, count),
        grid=(slots,),
        in_specs=[block] * count
        + [pl.BlockSpec((count, 1, capacity, columns), lambda g: (0, g, 0, 0))]
        + anywhere(earlier),
        out_specs=[block] * count,
        out_shape=[jax.ShapeDtypeStruct(homes[0].shape, jnp.bfloat16)] * count,
        compiler_params=kernel_params(),
        cost_estimate=lasting(7.0),
    )(*homes, swapped, *earlier)


def settle_kernel(pieces, side_ref, *refs):
    halves, refs = refs[: 2 * pieces], refs[2 * pieces :]
    hid_ref, inv_ref, cot_ref, gate_ref, term_ref, router_ref, gain_ref = refs[:7]
    dh_ref, db_ref, dl_ref, gg_ref = refs[-4:]
    gates, terms = gate_ref[...], term_ref[...]
    d_logits = gates * (terms - jnp.sum(gates * terms, axis=1, keepdims=True))
    d_logits = d_logits.astype(jnp.bfloat16)
    dl_ref[...] = jnp.zeros_like(dl_ref)
    dl_ref[:, : d_logits.shape[1]] = d_logits
    mine = jnp.concatenate([ref[...] for ref in halves[:pieces]], axis=1)
    other = jnp.concatenate([ref[...] for ref in halves[pieces:]], axis=1)
    first = side_ref[0] == 0
    rows = jnp.concatenate([jnp.where(first, mine, other), jnp.where(first, other, mine)], axis=1)
    d_second = rows.astype(jnp.float32) + dot(d_logits, router_ref[...], 1, 1)
    inverse = inv_ref[...]
    normed = hid_ref[...] * inverse
    scaled = d_second * gain_ref[...]
    gain_grad = jnp.sum(d_second * normed, axis=0, keepdims=True)

    @pl.when(pl.program_id(0) == 0)
    def _():
        gg_ref[...] = gain_grad

    @pl.when(pl.program_id(0) > 0)
    def _():
        gg_ref[...] += gain_grad

    center = jnp.mean(scaled * normed, axis=1, keepdims=True)
    d_hidden = cot_ref[...].astype(jnp.float32) + inverse * (scaled - normed * center)
    dh_ref[...] = d_hidden
    db_ref[...] = d_hidden.astype(jnp.bfloat16)


def settle(
    side, mine, other, hidden, inverse, cotangent, gates, terms, router, gain, tile, earlier
):
    length, model = hidden.shape
    count = router.shape[1]
    padded = count + 128 - count % 128

    def rows(columns):
        return pl.BlockSpec((tile, columns), lambda i: (i, 0))

    def shape(columns, kind=jnp.float32):
        return jax.ShapeDtypeStruct((length, columns), kind)

    return pl.pallas_call(
        functools.partial(settle_kernel, len(mine)),
        grid=(length // tile,),
        in_specs=[SCALAR]
        + [rows(piece.shape[1]) for piece in (*mine, *other)]
        + [rows(model), rows(1), rows(model), rows(count), rows(count), whole(router), whole(gain)]
        + anywhere(earlier),
        out_specs=[rows(model), rows(model), rows(padded), whole(gain)],
        out_shape=[
            shape(model),
            shape(model, jnp.bfloat16),
            shape(padded, jnp.bfloat16),
            jax.ShapeDtypeStruct(gain.shape, jnp.float32),
        ],
        compiler_params=kernel_params(),
        cost_estimate=lasting(10.0),
    )(side, *mine, *other, hidden, inverse, cotangent, gates, terms, router, gain, *earlier)


def finish_kernel(a_ref, b_ref, x_ref, inv_ref, dh_ref, gain_ref, out_ref):
    d_first = a_ref[...].astype(jnp.float32) + b_ref[...].astype(jnp.float32)
    inverse = inv_ref[...]
    normed = x_ref[...].astype(jnp.float32) * inverse
    scaled = d_first * gain_ref[...]
    center = jnp.mean(scaled * normed, axis=1, keepdims=True)
    out_ref[...] = dh_ref[...] + inverse * (scaled - normed * center)


def finish(mine, other, tokens, inverse, d_hidden, gain, tile):
    length, model = tokens.shape

    def rows(columns):
        return pl.BlockSpec((tile, columns), lambda i: (i, 0))

    return pl.pallas_call(
        finish_kernel,
        grid=(length // tile,),
        in_specs=[rows(model), rows(model), rows(model), rows(1), rows(model), whole(gain)],
        out_specs=rows(model),
        out_shape=jax.ShapeDtypeStruct((length, model), jnp.float32),
        compiler_params=kernel_params(),
        cost_estimate=lasting(8.0),
    )(mine, other, tokens, inverse, d_hidden, gain)


def home_block(k, count, b, g):
    return (jnp.where(b < k, 0, jnp.where(b > k, count - 1, g)), 0, 0)


def down_kernel(width, me_ref, act_ref, wd_ref, *refs):
    outs = refs[-1 - width :]
    away_ref, homes = outs[0], outs[1:]
    side = me_ref[1]
    batch, _, capacity, half = away_ref.shape
    mine = pl.ds(pl.multiple_of(side * half, half), half)
    other = pl.ds(pl.multiple_of((1 - side) * half, half), half)
    act = act_ref[...].reshape(batch * capacity, act_ref.shape[3])
    away_ref[...] = low(dot(act, wd_ref[:, other])).reshape(away_ref.shape)
    give_homes(low(dot(act, wd_ref[:, mine])).reshape(batch, capacity, half), homes)


def down_rows(me, act, w_down, earlier):
    width, count, capacity, units = act.shape
    half = w_down.shape[1] // 2
    batch = block_batch(width, capacity)

    def rows(columns):
        return pl.BlockSpec((batch, 1, capacity, columns), lambda b, g: (b, g, 0, 0))

    return pl.pallas_call(
        functools.partial(down_kernel, width),
        grid=(width // batch, count),
        in_specs=[SCALAR, rows(units), whole(w_down)] + anywhere(earlier),
        out_specs=[rows(half)] + home_specs(width, batch, count, capacity, half),
        out_shape=[jax.ShapeDtypeStruct((width, count, capacity, half), jnp.bfloat16)]
        + [jax.ShapeDtypeStruct((count, capacity, half), jnp.bfloat16)] * width,
        compiler_params=kernel_params(),
        cost_estimate=lasting(3.0 * count),
    )(me, act, w_down, *earlier)


def attend_back_kernel(
    heads,
    scale,
    tile,
    block,
    q_ref,
    k_ref,
    v_ref,
    segq_ref,
    segk_ref,
    lse_ref,
    db_ref,
    wo_ref,
    cos_ref,
    sin_ref,
    *refs,
):
    out_ref, dk_ref, dv_ref = refs[-3:]
    step = pl.program_id(0)
    length, size = k_ref.shape
    here = pl.ds(pl.multiple_of(step * tile, tile), tile)
    cosine, sine = cos_ref[here, :], sin_ref[here, :]

    def put(rows, start, array):
        out_ref[rows, start : start + size] = array.astype(jnp.bfloat16)

    @pl.when(step == 0)
    def _():
        dk_ref[...] = jnp.zeros_like(dk_ref)
        dv_ref[...] = jnp.zeros_like(dv_ref)

    d_mixed = dot(db_ref[...], wo_ref[...], 1, 1).astype(jnp.bfloat16)

    def work(seen):
        allowed = segk_ref[:seen] <= segq_ref[...]
        keys, values = k_ref[:seen], v_ref[:seen]
        keys_t = keys.T
        dk_total = jnp.zeros(keys.shape, jnp.float32)
        dv_total = jnp.zeros(keys.shape, jnp.float32)
        for head in range(heads):
            span = slice(head * size, (head + 1) * size)
            query = q_ref[:, span]
            d_head = d_mixed[:, span]
            scores = dot(keys, query, 1, 1) * scale - lse_ref[head : head + 1, :]
            probs = jnp.where(allowed, jnp.exp(scores), 0.0)
            d_probs = dot(values, d_head, 1, 1)
            scaled = probs * d_probs
            row_dot = jnp.sum(scaled, axis=0, keepdims=True)
            d_scores = (scale * (scaled - probs * row_dot)).astype(jnp.bfloat16)
            dv_total = dv_total + dot(probs.astype(jnp.bfloat16), d_head)
            dk_total = dk_total + dot(d_scores, query)
            d_query = dot(keys_t, d_scores).T
            put(here, head * size, turn(d_query, cosine, -sine))
        dk_ref[:seen] += dk_total
        dv_ref[:seen] += dv_total

    for at in range(length // tile):

        @pl.when(step == at)
        def _(at=at):
            work(min((at + 1) * tile + block, length))

    @pl.when(step == pl.num_programs(0) - 1)
    def _():
        base = heads * size
        put(slice(None), base, turn(dk_ref[...], cos_ref[...], -sin_ref[...]))
        put(slice(None), base + size, dv_ref[...])


def attend_back(
    query, keys, values, seg_row, seg_col, lse, d_branch, w_out, cosine, sine, scale, tile, earlier
):
    length, span = query.shape
    size = keys.shape[1]
    heads = span // size
    model = w_out.shape[1]
    out = jax.ShapeDtypeStruct((length, span + 2 * size), jnp.bfloat16)
    return pl.pallas_call(
        functools.partial(attend_back_kernel, heads, scale, tile, longest_block),
        grid=(length // tile,),
        in_specs=[
            pl.BlockSpec((tile, span), lambda i: (i, 0)),
            whole(keys),
            whole(values),
            pl.BlockSpec((1, tile), lambda i: (0, i)),
            whole(seg_col),
            pl.BlockSpec((heads, tile), lambda i: (0, i)),
            pl.BlockSpec((tile, model), lambda i: (i, 0)),
            whole(w_out),
            whole(cosine),
            whole(sine),
        ]
        + anywhere(earlier),
        out_specs=whole(out),
        out_shape=out,
        scratch_shapes=[pltpu.VMEM((length, size), jnp.float32)] * 2,
        compiler_params=kernel_params(),
        cost_estimate=lasting(28.0),
    )(query, keys, values, seg_row, seg_col, lse, d_branch, w_out, cosine, sine, *earlier)


def first_grad_kernel(d_ref, wq_ref, wk_ref, wv_ref, *refs):
    out_ref = refs[-1]
    span, size = wq_ref.shape[1], wk_ref.shape[1]
    total = dot(d_ref[:, :span], wq_ref[...], 1, 1)
    total = total + dot(d_ref[:, span : span + size], wk_ref[...], 1, 1)
    total = total + dot(d_ref[:, span + size :], wv_ref[...], 1, 1)
    out_ref[...] = total.astype(jnp.bfloat16)


def first_grad(d_all, w_query, w_key, w_value, tile, earlier):
    length, columns = d_all.shape
    model = w_query.shape[0]
    return pl.pallas_call(
        first_grad_kernel,
        grid=(length // tile,),
        in_specs=[
            pl.BlockSpec((tile, columns), lambda i: (i, 0)),
            whole(w_query),
            whole(w_key),
            whole(w_value),
        ]
        + anywhere(earlier),
        out_specs=pl.BlockSpec((tile, model), lambda i: (i, 0)),
        out_shape=jax.ShapeDtypeStruct((length, model), jnp.bfloat16),
        compiler_params=kernel_params(),
        cost_estimate=lasting(8.0),
    )(d_all, w_query, w_key, w_value, *earlier)


def share_kernel(width, rows, extra, spot_ref, left_ref, right_ref, *refs):
    kept_ref, *gone = refs[3 * extra : 3 * extra + width]
    hold_ref = refs[3 * extra + width]
    products = [(0, dot(left_ref[...], right_ref[...], 0, 0))]
    if extra:
        also_ref, picks_ref, row_ref = refs[:3]
        column = jnp.broadcast_to(row_ref[...], (8, row_ref.shape[1])).T[:, :1]
        more = dot(also_ref[...], picks_ref[...], 0, 0)
        lane = lax.broadcasted_iota(jnp.int32, more.shape, 1)
        last = more.shape[1] - 1
        products.append((right_ref.shape[1], jnp.where(lane == last, column, more)))
    for start, product in products:
        for s in range(width):
            part = product[s * rows : (s + 1) * rows]
            hold_ref[s, :, start : start + product.shape[1]] = part
    kept_ref[0] = hold_ref[spot_ref[0]]
    for b in range(1, width):
        gone[b - 1][0] = hold_ref[spot_ref[0] ^ b].astype(jnp.bfloat16)


def share_grads(spot, left, right, depth, width, extra=()):
    length, model = left.shape
    columns = right.shape[1] + (extra[1].shape[1] if extra else 0)
    rows = model // (depth * width)
    if (width * rows) % 128:
        product = dot(left, right, 0, 0)
        if extra:
            more = jnp.concatenate([dot(extra[0], extra[1], 0, 0)[:, :-1], extra[2].T], axis=1)
            product = jnp.concatenate([product, more], axis=1)
        parted = product.reshape(depth, width, rows, columns)
        blocks = [
            lax.dynamic_index_in_dim(parted, spot[0] ^ b, 1, keepdims=False) for b in range(width)
        ]
        return [blocks[0]] + [low(block) for block in blocks[1:]]
    block = pl.BlockSpec((1, rows, columns), lambda l: (l, 0, 0))
    stripe = pl.BlockSpec((length, width * rows), lambda l: (0, l))
    more_specs = []
    if extra:
        more_specs = [stripe, whole(extra[1]), pl.BlockSpec((1, width * rows), lambda l: (0, l))]
    return pl.pallas_call(
        functools.partial(share_kernel, width, rows, int(bool(extra))),
        grid=(depth,),
        in_specs=[SCALAR, stripe, whole(right)] + more_specs,
        out_specs=[block] * width,
        out_shape=[jax.ShapeDtypeStruct((depth, rows, columns), jnp.float32)]
        + [jax.ShapeDtypeStruct((depth, rows, columns), jnp.bfloat16)] * (width - 1),
        scratch_shapes=[pltpu.VMEM((width, rows, columns), jnp.float32)],
        compiler_params=kernel_params(),
        cost_estimate=lasting(6.0),
    )(spot, left, right, *extra)


class Exchange:
    def __init__(self, count):
        self.count = count
        self.depth = line_depth(count)
        self.width = count // self.depth
        self.me = lax.axis_index("expert")
        self.line = self.me // self.width
        self.lines = [[l * self.width + s for l in range(self.depth)] for s in range(self.width)]

    def flip(self, rows, mask):
        return lax.ppermute(rows, "expert", [(d, d ^ mask) for d in range(self.count)])

    def spread(self, rows):
        return lax.all_gather(rows, "expert", axis_index_groups=self.lines)

    def collect(self, parts):
        flat = parts.reshape(-1, parts.shape[-1])
        return lax.psum_scatter(
            flat, "expert", scatter_dimension=0, axis_index_groups=self.lines, tiled=True
        )

    def plane(self, blocks):
        return [blocks[0]] + [self.flip(blocks[b], b) for b in range(1, self.width)]

    def sum_plane(self, blocks):
        held = wide(blocks[0])
        for b in range(1, self.width):
            held = held + wide(self.flip(blocks[b], b))
        return held

    def sum_line(self, held):
        total = lax.dynamic_index_in_dim(held, self.line, 0, keepdims=False)
        for g in range(1, self.depth):
            part = lax.dynamic_index_in_dim(held, self.line ^ g, 0, keepdims=False)
            total = total + wide(self.flip(low(part), g * self.width))
        return total


def low(array):
    return array.astype(jnp.bfloat16)


def wide(array):
    return array.astype(jnp.float32)


def swap(rows):
    return lax.ppermute(rows, "tensor", [(0, 1), (1, 0)])


def half_of(array, side):
    width = array.shape[-1] // 2
    return lax.dynamic_slice_in_dim(array, side * width, width, array.ndim - 1)


def join_halves(mine, other, side):
    first = jnp.where(side == 0, mine, other)
    last = jnp.where(side == 0, other, mine)
    return jnp.concatenate([first, last], axis=-1)


def on_device(
    tokens,
    cotangent,
    norm_gain,
    ffn_gain,
    w_query,
    w_key,
    w_value,
    w_out,
    w_router,
    w_gate,
    w_up,
    w_down,
    routes,
    order,
    segments,
):
    seq_length, model_width = tokens.shape
    half_width = model_width // 2
    expert_count = w_router.shape[1]
    pick_count = routes.shape[1]
    capacity = 9 * seq_length * pick_count // (8 * expert_count)
    head_width = w_key.shape[1]
    span = w_query.shape[1]
    unit_count = w_down.shape[1]
    score_scale = 1.0 / math.sqrt(head_width)
    tile = 256
    link = Exchange(expert_count)
    depth, width = link.depth, link.width
    side = lax.axis_index("tensor")
    side_ref = side.astype(jnp.int32)[None]
    me_ref = jnp.stack([link.me, side]).astype(jnp.int32)
    line_ref = link.line.astype(jnp.int32)[None]

    third = half_width // 3
    widths = (2 * third, third)
    cot_slots = link.spread(half_of(cotangent, side))
    placed = place_table(routes, order[0], link.me, expert_count, capacity)
    tables = []
    for g in range(depth):
        table = jnp.concatenate([placed[g * width : (g + 1) * width], routes.T], axis=0)
        tables.append(table if g == 0 else link.flip(table, g * width))
    places = jnp.stack([table[:width] for table in tables])
    place_rows = places[:, :, None, :]
    starts = capacity * jnp.arange(width, dtype=jnp.int32)
    place_columns = jnp.where(places >= 0, places + starts[None, :, None], -1)
    place_columns = jnp.swapaxes(place_columns, 1, 2)
    route_columns = jnp.stack([low(table[width:].T) for table in tables])

    route_blocks = link.plane(
        pick_rows(jnp.zeros_like(line_ref), place_rows, route_columns, capacity)
    )
    route_rows = jnp.stack(route_blocks)

    cosine, sine = (jnp.asarray(t) for t in rope_constants(seq_length, head_width))
    first_in, query, keys, values, inverse_first = project(
        tokens, norm_gain[None], w_query, w_key, w_value, cosine, sine, tile
    )
    seg_row, seg_col = segments, segments[0][:, None]
    mixed, lse, branch = attend(
        query, keys, values, seg_row, seg_col, w_out, score_scale, tile
    )
    hidden, second_in, inverse_second, gates, *in_parts = second_norm(
        side_ref,
        tokens,
        branch,
        swap(branch),
        ffn_gain[None],
        w_router,
        routes,
        tile,
        widths,
        (place_rows, route_rows),
    )
    w_both = jnp.concatenate([w_gate[0], w_up[0]], axis=1)
    in_slots = [link.spread(hold(in_parts[0], cot_slots))]
    cot_blocks = pick_rows(line_ref, place_rows, cot_slots, capacity, None, (second_in, w_both))
    cot_came = link.plane(cot_blocks)
    in_slots.append(link.spread(hold(in_parts[1], in_slots[0], *cot_came[1:])))
    in_first = pick_rows(line_ref, place_rows, in_slots[0], capacity)
    in_came = [link.plane(in_first)]
    in_last = pick_rows(line_ref, place_rows, in_slots[1], capacity, None, in_came[0][1:])
    in_came.append(link.plane(in_last))
    cot_mine = pile(cot_came, in_last[1:])
    cot_other = swap(cot_mine)
    in_mine = [pile(in_came[0], (cot_mine,))]
    in_other = [swap(in_mine[0])]
    in_mine.append(pile(in_came[1], (in_other[0], cot_other)))
    in_other.append(swap(in_mine[1]))
    pieces, c_pieces = in_mine + in_other, [cot_mine, cot_other]

    pre, acts, terms, backs = expert_rows(
        me_ref, pieces, c_pieces, widths[::-1], route_rows, w_both, w_down[0], w_router
    )
    swapped = [swap(away) for away, _ in backs]
    first_came = link.plane(join_cores(backs[0][1], swapped[0], ()))
    out_away, *out_homes = down_rows(me_ref, acts, w_down[0], ())
    terms = hold(terms, out_away)[..., 0]
    terms = jnp.stack(link.plane([terms[b] for b in range(width)]), axis=1)
    blocks = join_cores(backs[1][1], swapped[1], (*first_came[1:], out_away))
    first_part, first_token = combine(line_ref, place_columns, first_came, blocks[1:])
    row_parts = [first_part]
    came = link.plane(blocks)
    last_part, last_token = combine(line_ref, place_columns, came, (first_token,))
    row_parts.append(last_part)
    out_blocks = join_cores(out_homes, swap(out_away), (last_token, terms))
    out_came = link.plane(out_blocks)
    row_mine = [link.collect(row_parts[0])]
    row_mine.append(link.collect(hold(row_parts[1], row_mine[0])))
    row_other = [swap(part) for part in row_mine]

    terms = hold(terms, *out_blocks[1:])
    slot_ids = jnp.arange(capacity, dtype=jnp.int32)
    local = jnp.sum(
        jnp.where(
            places[:, :, None, :] == slot_ids[None, None, :, None], terms[:, :, :, None], 0.0
        ),
        axis=2,
    )
    term_table = jnp.concatenate(
        [local[g] if g == 0 else link.flip(local[g], g * width) for g in range(depth)]
    )
    term_table = term_table + swap(term_table)
    term_table = term_table[jnp.arange(expert_count, dtype=jnp.int32) ^ link.me].T

    act_rows = hold(acts, *out_blocks[1:]).reshape(-1, unit_count)
    grads = [contract_rows(act_rows, piece.reshape(-1, piece.shape[3])) for piece in c_pieces]
    down_grad = join_halves(
        *grads, side
    )[None]
    pre = hold(pre, term_table, down_grad).reshape(-1, 2 * unit_count)
    grads = [contract_rows(piece.reshape(-1, piece.shape[3]), pre) for piece in pieces]
    first, last = jnp.concatenate(grads[:2]), jnp.concatenate(grads[2:])
    upper, lower = jnp.where(side == 0, first, last), jnp.where(side == 0, last, first)
    gate_grad = jnp.concatenate([upper[:, :unit_count], lower[:, :unit_count]])[None]
    up_grad = jnp.concatenate([upper[:, unit_count:], lower[:, unit_count:]])[None]

    d_hidden, d_branch, d_logits, ffn_gain_grad = settle(
        side_ref,
        row_mine,
        row_other,
        hidden,
        inverse_second,
        cotangent,
        gates,
        term_table,
        w_router,
        ffn_gain[None],
        tile,
        (down_grad, gate_grad, up_grad),
    )

    out_parts, _ = combine(line_ref, place_columns, out_came, (d_branch,))
    out_held = hold(out_parts, row_mine[1])
    spot_ref = (link.me % width).astype(jnp.int32)[None]
    shared_early = share_grads(
        spot_ref, d_branch, mixed, depth, width, (second_in, d_logits, ffn_gain_grad)
    )
    early_held = link.sum_plane(shared_early)

    d_all = attend_back(
        query,
        keys,
        values,
        seg_row,
        seg_col,
        lse,
        d_branch,
        w_out,
        cosine,
        sine,
        score_scale,
        tile,
        (*shared_early[1:], out_held),
    )
    d_first = first_grad(d_all, w_query, w_key, w_value, tile, (early_held,))
    input_grad = finish(
        d_first, swap(d_first), tokens, inverse_first, d_hidden, norm_gain[None], tile
    )
    shared = share_grads(spot_ref, first_in, hold(d_all, d_first), depth, width)
    shared = [hold(shared[0], input_grad), *shared[1:]]
    qkv_held = link.sum_plane(shared)
    summed = link.sum_line(jnp.concatenate([qkv_held, early_held], axis=2))
    columns = span + 2 * head_width
    qkv_grad, early_sum = summed[:, :columns], summed[:, columns:]
    out_grad = early_sum[:, :span].T
    router_grad, ffn_gain_grad = early_sum[:, span : span + expert_count], early_sum[:, -1]
    combined = wide(hold(link.collect(out_held), qkv_held))
    output_half = low(half_of(hidden, side) + combined)
    output = join_halves(output_half, swap(output_half), side)
    rows = model_width // expert_count
    gain_part = jnp.zeros((rows,), jnp.float32)
    start = 0
    for weight in (w_query, w_key, w_value):
        mine = lax.dynamic_slice_in_dim(weight, link.me * rows, rows, 0)
        grads = qkv_grad[:, start : start + weight.shape[1]]
        gain_part = gain_part + jnp.sum(grads * wide(mine), axis=1)
        start += weight.shape[1]
    gain_part = gain_part / lax.dynamic_slice_in_dim(norm_gain, link.me * rows, rows, 0)
    norm_gain_grad = gain_part + swap(gain_part)
    return (
        output,
        input_grad,
        norm_gain_grad,
        ffn_gain_grad,
        qkv_grad[:, :span],
        qkv_grad[:, span : span + head_width],
        qkv_grad[:, span + head_width :],
        out_grad,
        router_grad,
        gate_grad,
        up_grad,
        down_grad,
    )


def solution(mesh):
    placed = (
        P("expert", None),
        P("expert", None),
        P(),
        P(),
        P(None, "tensor"),
        P(None, "tensor"),
        P(None, "tensor"),
        P("tensor", None),
        P(),
        P("expert", None, "tensor"),
        P("expert", None, "tensor"),
        P("expert", "tensor", None),
        P("expert", None),
        P("expert", None),
        P("expert", None),
    )
    return jax.shard_map(
        on_device,
        mesh=mesh,
        in_specs=placed,
        out_specs=(
            P("expert", None),
            P("expert", None),
            P("expert"),
            P("expert"),
            P("expert", "tensor"),
            P("expert", "tensor"),
            P("expert", "tensor"),
            P("tensor", "expert"),
            P("expert", None),
            P("expert", None, "tensor"),
            P("expert", None, "tensor"),
            P("expert", "tensor", None),
        ),
        check_vma=False,
    )
```

```python
import functools
import math

import jax
import jax.numpy as jnp
import numpy as np
from jax import lax
from jax.experimental import pallas as pl
from jax.experimental.pallas import tpu as pltpu
from jax.sharding import PartitionSpec as P

epsilon = 1e-06
rope_base = 1000000.0
masked_score = -1e30


def contract_rows(left, right):
    return lax.dot_general(
        left, right, (((0,), (0,)), ((), ())), preferred_element_type=jnp.float32
    )


def times_transposed(left, right):
    return lax.dot_general(
        left, right, (((1,), (1,)), ((), ())), preferred_element_type=jnp.float32
    )


def line_depth(count):
    depth = 1
    while depth * depth * 4 <= count:
        depth *= 2
    return depth


longest_block = 256
VMEM_LIMIT = 56 * 1024 * 1024


def kernel_params(*semantics):
    return pltpu.CompilerParams(vmem_limit_bytes=VMEM_LIMIT)


def lasting(microseconds):
    return pl.CostEstimate(
        flops=int(microseconds * 1.0e6), bytes_accessed=1024, transcendentals=0
    )


def hold_kernel(*refs):
    del refs


def hold(array, *earlier):
    return pl.pallas_call(
        hold_kernel,
        in_specs=anywhere((array, *earlier)),
        out_specs=pl.BlockSpec(memory_space=pl.ANY),
        out_shape=jax.ShapeDtypeStruct(array.shape, array.dtype),
        input_output_aliases={0: 0},
    )(array, *earlier)


def whole(array):
    return pl.BlockSpec(array.shape, lambda *_: (0,) * array.ndim)


def anywhere(arrays):
    return [pl.BlockSpec(memory_space=pl.ANY)] * len(arrays)


SCALAR = pl.BlockSpec(memory_space=pltpu.SMEM)


def dot(left, right, left_axis=1, right_axis=0):
    return lax.dot_general(
        left,
        right,
        (((left_axis,), (right_axis,)), ((), ())),
        preferred_element_type=jnp.float32,
    )


def rope_constants(seq_length, head_width):
    half = head_width // 2
    frequency = np.exp(-math.log(rope_base) * np.arange(half) * (2.0 / head_width))
    angle = np.arange(seq_length)[:, None] * frequency[None, :]
    cosine, sine = np.cos(angle), np.sin(angle)
    return (
        np.concatenate([cosine, cosine], axis=1).astype(np.float32),
        np.concatenate([-sine, sine], axis=1).astype(np.float32),
    )


def place_kernel(seq_length, capacity, keys_ref, out_ref):
    block = keys_ref[...]
    columns = block.T
    limit = seq_length * 1024
    for row in range(block.shape[0]):
        mine = block[row : row + 1, :]
        total = jnp.zeros((1, seq_length), jnp.float32)
        for start in range(0, seq_length, 256):
            less = columns[start : start + 256, row : row + 1] < mine
            total = total + jnp.sum(jnp.where(less, 1.0, 0.0), axis=0, keepdims=True)
        kept = (mine < limit) & (total < capacity)
        out_ref[row : row + 1, :] = jnp.where(kept, total, -1.0).astype(jnp.int32)


def place_table(routes, order, me, expert_count, capacity):
    seq_length = routes.shape[0]
    relabeled = (routes ^ me).T
    ranks = order.reshape(routes.shape).T
    labels = jnp.arange(expert_count, dtype=jnp.int32)
    hit = relabeled[:, None, :] == labels[None, :, None]
    rank = jnp.sum(jnp.where(hit, ranks[:, None, :] + 1, 0), axis=0)
    rank = jnp.where(rank > 0, rank, seq_length * 1024)
    spec = pl.BlockSpec((8, seq_length), lambda e: (e, 0))
    return pl.pallas_call(
        functools.partial(place_kernel, seq_length, capacity),
        grid=(expert_count // 8,),
        out_shape=jax.ShapeDtypeStruct(rank.shape, jnp.int32),
        in_specs=[spec],
        out_specs=spec,
        compiler_params=kernel_params(),
        cost_estimate=lasting(9.0 * expert_count / 16),
    )(rank)


def turn(values, cosine, sine):
    return values * cosine + pltpu.roll(values, values.shape[1] // 2, 1) * sine


def project_kernel(
    heads, x_ref, gain_ref, wq_ref, wk_ref, wv_ref, cos_ref, sin_ref, in_ref, q_ref, k_ref, v_ref, inv_ref
):
    source = x_ref[...].astype(jnp.float32)
    inverse = lax.rsqrt(jnp.mean(source * source, axis=1, keepdims=True) + epsilon)
    first = (source * inverse * gain_ref[...]).astype(jnp.bfloat16)
    in_ref[...] = first
    inv_ref[...] = inverse
    cosine, sine = cos_ref[...], sin_ref[...]
    size = cosine.shape[1]
    query = dot(first, wq_ref[...])
    for head in range(heads):
        span = slice(head * size, (head + 1) * size)
        q_ref[:, span] = turn(query[:, span], cosine, sine).astype(jnp.bfloat16)
    k_ref[...] = turn(dot(first, wk_ref[...]), cosine, sine).astype(jnp.bfloat16)
    v_ref[...] = dot(first, wv_ref[...]).astype(jnp.bfloat16)


def project(tokens, gain, w_query, w_key, w_value, cosine, sine, tile):
    length, model = tokens.shape
    size = w_key.shape[1]
    span = w_query.shape[1]

    def rows(columns):
        return pl.BlockSpec((tile, columns), lambda i: (i, 0))

    def shape(columns, kind=jnp.bfloat16):
        return jax.ShapeDtypeStruct((length, columns), kind)

    return pl.pallas_call(
        functools.partial(project_kernel, span // size),
        grid=(length // tile,),
        in_specs=[
            rows(model),
            whole(gain),
            whole(w_query),
            whole(w_key),
            whole(w_value),
            rows(size),
            rows(size),
        ],
        out_specs=[rows(model), rows(span), rows(size), rows(size), rows(1)],
        out_shape=[shape(model), shape(span), shape(size), shape(size), shape(1, jnp.float32)],
        compiler_params=kernel_params(),
        cost_estimate=lasting(9.0),
    )(tokens, gain, w_query, w_key, w_value, cosine, sine)


def attend_kernel(
    heads, scale, q_ref, k_ref, v_ref, segq_ref, segk_ref, wo_ref, mix_ref, lse_ref, branch_ref
):
    allowed = segk_ref[...] <= segq_ref[...]
    keys = k_ref[...]
    values = v_ref[...].T
    size = keys.shape[1]
    for head in range(heads):
        span = slice(head * size, (head + 1) * size)
        scores = dot(keys, q_ref[:, span], 1, 1)
        scores = jnp.where(allowed, scores * scale, masked_score)
        top = jnp.max(scores, axis=0, keepdims=True)
        spread = jnp.exp(scores - top)
        total = jnp.sum(spread, axis=0, keepdims=True)
        mixed = dot(values, spread.astype(jnp.bfloat16)) / total
        mix_ref[:, span] = mixed.T.astype(jnp.bfloat16)
        lse_ref[head : head + 1, :] = top + jnp.log(total)
    branch_ref[...] = dot(mix_ref[...], wo_ref[...]).astype(jnp.bfloat16)


def attend(query, keys, values, seg_row, seg_col, w_out, scale, tile):
    length, span = query.shape
    size = keys.shape[1]
    heads = span // size
    model = w_out.shape[1]
    rows = pl.BlockSpec((tile, span), lambda i: (i, 0))
    return pl.pallas_call(
        functools.partial(attend_kernel, heads, scale),
        grid=(length // tile,),
        in_specs=[
            rows,
            whole(keys),
            whole(values),
            pl.BlockSpec((1, tile), lambda i: (0, i)),
            whole(seg_col),
            whole(w_out),
        ],
        out_specs=[
            rows,
            pl.BlockSpec((heads, tile), lambda i: (0, i)),
            pl.BlockSpec((tile, model), lambda i: (i, 0)),
        ],
        out_shape=[
            jax.ShapeDtypeStruct((length, span), jnp.bfloat16),
            jax.ShapeDtypeStruct((heads, length), jnp.float32),
            jax.ShapeDtypeStruct((length, model), jnp.bfloat16),
        ],
        compiler_params=kernel_params(),
        cost_estimate=lasting(20.0),
    )(query, keys, values, seg_row, seg_col, w_out)


def second_kernel(
    outputs, side_ref, x_ref, a_ref, b_ref, gain_ref, router_ref, routes_ref, *refs
):
    refs = refs[len(refs) - outputs :]
    hidden_ref, in_ref, inv_ref, gate_ref, *parts = refs
    hidden = x_ref[...].astype(jnp.float32) + (
        a_ref[...].astype(jnp.float32) + b_ref[...].astype(jnp.float32)
    )
    inverse = lax.rsqrt(jnp.mean(hidden * hidden, axis=1, keepdims=True) + epsilon)
    second = (hidden * inverse * gain_ref[...]).astype(jnp.bfloat16)
    hidden_ref[...] = hidden
    in_ref[...] = second
    inv_ref[...] = inverse
    half = second.shape[1] // 2
    sent = jnp.where(side_ref[0] == 0, second[:, :half], second[:, half:])
    start = 0
    for part in parts:
        part[...] = sent[:, start : start + part.shape[1]]
        start += part.shape[1]
    logits = dot(second, router_ref[...])
    gate_ref[...] = routed_softmax(logits, routes_ref[...])


def routed_softmax(logits, routes):
    labels = lax.broadcasted_iota(jnp.int32, logits.shape, 1)
    picked = routes[:, 0:1] == labels
    for k in range(1, routes.shape[1]):
        picked = picked | (routes[:, k : k + 1] == labels)
    masked = jnp.where(picked, logits, masked_score)
    spread = jnp.exp(masked - jnp.max(masked, axis=1, keepdims=True))
    return spread / jnp.sum(spread, axis=1, keepdims=True)


def second_norm(side, tokens, mine, other, gain, router, routes, tile, widths, earlier):
    length, model = tokens.shape
    count = router.shape[1]

    def rows(columns):
        return pl.BlockSpec((tile, columns), lambda i: (i, 0))

    def shape(columns, kind=jnp.float32):
        return jax.ShapeDtypeStruct((length, columns), kind)

    return pl.pallas_call(
        functools.partial(second_kernel, 4 + len(widths)),
        grid=(length // tile,),
        in_specs=[
            SCALAR,
            rows(model),
            rows(model),
            rows(model),
            whole(gain),
            whole(router),
            rows(routes.shape[1]),
        ]
        + anywhere(earlier),
        out_specs=[rows(model), rows(model), rows(1), rows(count)] + [rows(w) for w in widths],
        out_shape=[shape(model), shape(model, jnp.bfloat16), shape(1), shape(count)]
        + [shape(w, jnp.bfloat16) for w in widths],
        compiler_params=kernel_params(),
        cost_estimate=lasting(9.0),
    )(side, tokens, mine, other, gain, router, routes, *earlier)


def chosen_slots(place_row, capacity):
    slot = lax.broadcasted_iota(jnp.int32, (capacity, place_row.shape[1]), 0)
    return jnp.where(place_row == slot, 1.0, 0.0).astype(jnp.bfloat16)


def pick_kernel(width, capacity, outputs, line_ref, tab_ref, slot_ref, *refs):
    outs = refs[len(refs) - outputs :]
    chosen = jnp.concatenate([chosen_slots(tab_ref[0, b], capacity) for b in range(width)])

    def give(rows, targets):
        for b in range(width):
            targets[b][0] = rows[b * capacity : (b + 1) * capacity].astype(jnp.bfloat16)

    give(dot(chosen, slot_ref[0]), outs[:width])
    if len(outs) > width:
        give(dot(chosen, refs[0][0]), outs[width:])


def pick_rows(line, tables, slots, capacity, small=None, earlier=()):
    count, width, _, length = tables.shape
    columns = slots.shape[2]
    if capacity % 16:
        slot = jnp.arange(capacity, dtype=jnp.int32)
        chosen = low(tables == slot[None, None, :, None])

        def taken(rows):
            picked = jnp.einsum("gbst,gtd->bgsd", chosen, rows, preferred_element_type=jnp.float32)
            return [low(picked[b]) for b in range(width)]

        near = slots[jnp.arange(count, dtype=jnp.int32) ^ line[0]]
        return taken(near) + ([] if small is None else taken(small))
    in_specs = [
        pl.BlockSpec((1, width, 1, length), lambda g, line: (g, 0, 0, 0)),
        pl.BlockSpec((1, length, columns), lambda g, line: (g ^ line[0], 0, 0)),
    ]
    out_specs = [pl.BlockSpec((1, capacity, columns), lambda g, line: (g, 0, 0))] * width
    out_shape = [jax.ShapeDtypeStruct((count, capacity, columns), jnp.bfloat16)] * width
    operands = [tables, slots]
    if small is not None:
        picks = small.shape[2]
        in_specs.append(pl.BlockSpec((1, length, picks), lambda g, line: (g, 0, 0)))
        out_specs += [pl.BlockSpec((1, capacity, picks), lambda g, line: (g, 0, 0))] * width
        out_shape += [jax.ShapeDtypeStruct((count, capacity, picks), jnp.bfloat16)] * width
        operands.append(small)
    return pl.pallas_call(
        functools.partial(pick_kernel, width, capacity, len(out_shape)),
        grid_spec=pltpu.PrefetchScalarGridSpec(
            num_scalar_prefetch=1,
            grid=(count,),
            in_specs=in_specs + anywhere(earlier),
            out_specs=out_specs,
        ),
        out_shape=out_shape,
        compiler_params=kernel_params(),
        cost_estimate=lasting(3.0 * count * columns / 768),
    )(line, *operands, *earlier)


def combine_kernel(width, capacity, line_ref, tab_ref, *refs):
    out_ref, token_ref = refs[-2:]
    token_ref[...] = jnp.zeros_like(token_ref)
    codes = tab_ref[0]
    total = width * capacity
    chosen = []
    for start in range(0, total, 128):
        size = min(128, total - start)
        slot = lax.broadcasted_iota(jnp.int32, (codes.shape[0], size), 1) + start
        hit = None
        for b in range(start // capacity, (start + size - 1) // capacity + 1):
            same = codes[:, b : b + 1] == slot
            hit = same if hit is None else hit | same
        chosen.append(jnp.where(hit, 1.0, 0.0).astype(jnp.bfloat16))
    rows = jnp.concatenate([refs[b][0] for b in range(width)])
    out_ref[0] = dot(jnp.concatenate(chosen, axis=1), rows).astype(out_ref.dtype)


def combine(line, table_columns, came, earlier=()):
    count, length, width = table_columns.shape
    _, capacity, columns = came[0].shape
    if capacity % 16:
        slot = jnp.arange(width * capacity, dtype=jnp.int32).reshape(width, capacity)
        chosen = low(table_columns[:, :, :, None] == slot)
        rows = jnp.stack(came)
        total = jnp.einsum("gtbs,bgsd->gtd", chosen, rows, preferred_element_type=jnp.float32)
        total = low(total[jnp.arange(count, dtype=jnp.int32) ^ line[0]])
        return total, total[:1, :8, :128]
    return pl.pallas_call(
        functools.partial(combine_kernel, width, capacity),
        grid_spec=pltpu.PrefetchScalarGridSpec(
            num_scalar_prefetch=1,
            grid=(count,),
            in_specs=[pl.BlockSpec((1, length, width), lambda g, line: (g, 0, 0))]
            + [pl.BlockSpec((1, capacity, columns), lambda g, line: (g, 0, 0))] * width
            + anywhere(earlier),
            out_specs=[
                pl.BlockSpec((1, length, columns), lambda g, line: (g ^ line[0], 0, 0)),
                pl.BlockSpec((1, 8, 128), lambda g, line: (0, 0, 0)),
            ],
        ),
        out_shape=[
            jax.ShapeDtypeStruct((count, length, columns), jnp.bfloat16),
            jax.ShapeDtypeStruct((1, 8, 128), jnp.float32),
        ],
        compiler_params=kernel_params(),
        cost_estimate=lasting(3.0 * count * columns / 768),
    )(line, table_columns, *came, *earlier)


def expert_kernel(count_in, count_cot, widths, width, me_ref, *refs):
    x_refs, refs = refs[: 2 * count_in], refs[2 * count_in :]
    c_refs, refs = refs[: 2 * count_cot], refs[2 * count_cot :]
    route_ref, wgu_ref, wd_ref, wr_ref, *outs = refs
    pre_ref, act_ref, term_ref = outs[:3]
    aways = outs[3 : 3 + len(widths)]
    homes = outs[3 + len(widths) :]
    side = me_ref[1]
    batch, _, capacity, _ = x_refs[0].shape
    half = sum(ref.shape[3] for ref in x_refs[:count_in])

    def flat(ref):
        return ref[...].reshape(batch * capacity, ref.shape[3])

    def keep(ref, rows):
        ref[...] = rows.reshape(ref.shape).astype(ref.dtype)

    def columns(which, start, size):
        return pl.ds(pl.multiple_of(which * half + start, 128), size)

    def spans(array_refs):
        count = len(array_refs) // 2
        for index, ref in enumerate(array_refs):
            which = side if index < count else 1 - side
            start = sum(r.shape[3] for r in array_refs[: index % count])
            yield flat(ref), columns(which, start, ref.shape[3])

    def through(weight_ref):
        total = None
        for rows, at in spans(x_refs):
            part = dot(rows, weight_ref[at, :])
            total = part if total is None else total + part
        return total

    both, logits = through(wgu_ref), through(wr_ref)
    units = both.shape[1] // 2
    gate_pre, up_pre = both[:, :units], both[:, units:]
    raw = None
    for rows, at in spans(c_refs):
        part = dot(rows, wd_ref[:, at], 1, 1)
        raw = part if raw is None else raw + part
    chance = routed_softmax(logits, flat(route_ref).astype(jnp.float32).astype(jnp.int32))
    label = lax.broadcasted_iota(jnp.int32, chance.shape, 1)
    gate = jnp.sum(jnp.where(label == me_ref[0], chance, 0.0), axis=1, keepdims=True)
    sig = jax.nn.sigmoid(gate_pre)
    silu = gate_pre * sig
    act = silu * up_pre
    keep(term_ref, jnp.sum(act * raw, axis=1, keepdims=True))
    keep(act_ref, act * gate)
    d_act = raw * gate
    d_gate = (d_act * up_pre * sig * (1.0 + gate_pre * (1.0 - sig))).astype(jnp.bfloat16)
    d_up = (d_act * silu).astype(jnp.bfloat16)
    d_both = jnp.concatenate([d_gate, d_up], axis=1)
    keep(pre_ref, d_both)
    start = 0
    for c, size in enumerate(widths):
        keep(aways[c], dot(d_both, wgu_ref[columns(1 - side, start, size), :], 1, 1))
        home = dot(d_both, wgu_ref[columns(side, start, size), :], 1, 1)
        home = home.astype(jnp.bfloat16).reshape(batch, capacity, size)
        give_homes(home, homes[c * width : (c + 1) * width])
        start += size


def give_homes(rows, homes):
    batch = rows.shape[0]
    for b in range(len(homes)):

        @pl.when(pl.program_id(0) == b // batch)
        def _(b=b):
            homes[b][0] = rows[b % batch]


def block_batch(width, capacity):
    return 1 if capacity % 16 else min(2, width)


def home_specs(width, batch, count, capacity, columns):
    return [
        pl.BlockSpec((1, capacity, columns), functools.partial(home_block, k // batch, count))
        for k in range(width)
    ]


def expert_rows(me, pieces, c_pieces, widths, routes, w_both, w_down, router):
    width, count, capacity, _ = pieces[0].shape
    units = w_down.shape[0]
    batch = block_batch(width, capacity)

    def rows(columns):
        return pl.BlockSpec((batch, 1, capacity, columns), lambda b, g: (b, g, 0, 0))

    def shape(columns, kind=jnp.bfloat16):
        return jax.ShapeDtypeStruct((width, count, capacity, columns), kind)

    out_specs = [rows(2 * units), rows(units), rows(1)] + [rows(size) for size in widths]
    out_shape = [shape(2 * units), shape(units), shape(1, jnp.float32)]
    out_shape += [shape(size) for size in widths]
    for size in widths:
        out_specs += home_specs(width, batch, count, capacity, size)
        out_shape += [jax.ShapeDtypeStruct((count, capacity, size), jnp.bfloat16)] * width
    outs = pl.pallas_call(
        functools.partial(expert_kernel, len(pieces) // 2, len(c_pieces) // 2, widths, width),
        grid=(width // batch, count),
        in_specs=[SCALAR]
        + [rows(piece.shape[3]) for piece in (*pieces, *c_pieces)]
        + [
            rows(routes.shape[3]),
            whole(w_both),
            whole(w_down),
            whole(router),
        ],
        out_specs=out_specs,
        out_shape=out_shape,
        compiler_params=kernel_params(),
        cost_estimate=lasting(10.0 * count),
    )(me, *pieces, *c_pieces, routes, w_both, w_down, router)
    aways, homes = outs[3 : 3 + len(widths)], outs[3 + len(widths) :]
    return (
        *outs[:3],
        [(aways[c], homes[c * width : (c + 1) * width]) for c in range(len(widths))],
    )


def pile_kernel(count, *refs):
    blocks, out_ref = refs[:count], refs[-1]
    for b in range(count):
        out_ref[b] = blocks[b][...]


def pile(blocks, earlier):
    slots, capacity, columns = blocks[0].shape
    count = len(blocks)
    return pl.pallas_call(
        functools.partial(pile_kernel, count),
        grid=(slots,),
        in_specs=[pl.BlockSpec((1, capacity, columns), lambda g: (g, 0, 0))] * count
        + anywhere(earlier),
        out_specs=pl.BlockSpec((count, 1, capacity, columns), lambda g: (0, g, 0, 0)),
        out_shape=jax.ShapeDtypeStruct((count, slots, capacity, columns), blocks[0].dtype),
        compiler_params=kernel_params(),
        cost_estimate=lasting(5.0),
    )(*blocks, *earlier)


def join_kernel(count, *refs):
    homes, swapped_ref, outs = refs[:count], refs[count], refs[len(refs) - count :]
    for b in range(count):
        total = homes[b][...].astype(jnp.float32) + swapped_ref[b].astype(jnp.float32)
        outs[b][...] = total.astype(jnp.bfloat16)


def join_cores(homes, swapped, earlier):
    slots, capacity, columns = homes[0].shape
    count = len(homes)
    block = pl.BlockSpec((1, capacity, columns), lambda g: (g, 0, 0))
    return pl.pallas_call(
        functools.partial(join_kernel, count),
        grid=(slots,),
        in_specs=[block] * count
        + [pl.BlockSpec((count, 1, capacity, columns), lambda g: (0, g, 0, 0))]
        + anywhere(earlier),
        out_specs=[block] * count,
        out_shape=[jax.ShapeDtypeStruct(homes[0].shape, jnp.bfloat16)] * count,
        compiler_params=kernel_params(),
        cost_estimate=lasting(7.0),
    )(*homes, swapped, *earlier)


def settle_kernel(pieces, side_ref, *refs):
    halves, refs = refs[: 2 * pieces], refs[2 * pieces :]
    hid_ref, inv_ref, cot_ref, gate_ref, term_ref, router_ref, gain_ref = refs[:7]
    dh_ref, db_ref, dl_ref, gg_ref = refs[-4:]
    gates, terms = gate_ref[...], term_ref[...]
    d_logits = gates * (terms - jnp.sum(gates * terms, axis=1, keepdims=True))
    d_logits = d_logits.astype(jnp.bfloat16)
    dl_ref[...] = jnp.zeros_like(dl_ref)
    dl_ref[:, : d_logits.shape[1]] = d_logits
    mine = jnp.concatenate([ref[...] for ref in halves[:pieces]], axis=1)
    other = jnp.concatenate([ref[...] for ref in halves[pieces:]], axis=1)
    first = side_ref[0] == 0
    rows = jnp.concatenate([jnp.where(first, mine, other), jnp.where(first, other, mine)], axis=1)
    d_second = rows.astype(jnp.float32) + dot(d_logits, router_ref[...], 1, 1)
    inverse = inv_ref[...]
    normed = hid_ref[...] * inverse
    scaled = d_second * gain_ref[...]
    gain_grad = jnp.sum(d_second * normed, axis=0, keepdims=True)

    @pl.when(pl.program_id(0) == 0)
    def _():
        gg_ref[...] = gain_grad

    @pl.when(pl.program_id(0) > 0)
    def _():
        gg_ref[...] += gain_grad

    center = jnp.mean(scaled * normed, axis=1, keepdims=True)
    d_hidden = cot_ref[...].astype(jnp.float32) + inverse * (scaled - normed * center)
    dh_ref[...] = d_hidden
    db_ref[...] = d_hidden.astype(jnp.bfloat16)


def settle(
    side, mine, other, hidden, inverse, cotangent, gates, terms, router, gain, tile, earlier
):
    length, model = hidden.shape
    count = router.shape[1]
    padded = count + 128 - count % 128

    def rows(columns):
        return pl.BlockSpec((tile, columns), lambda i: (i, 0))

    def shape(columns, kind=jnp.float32):
        return jax.ShapeDtypeStruct((length, columns), kind)

    return pl.pallas_call(
        functools.partial(settle_kernel, len(mine)),
        grid=(length // tile,),
        in_specs=[SCALAR]
        + [rows(piece.shape[1]) for piece in (*mine, *other)]
        + [rows(model), rows(1), rows(model), rows(count), rows(count), whole(router), whole(gain)]
        + anywhere(earlier),
        out_specs=[rows(model), rows(model), rows(padded), whole(gain)],
        out_shape=[
            shape(model),
            shape(model, jnp.bfloat16),
            shape(padded, jnp.bfloat16),
            jax.ShapeDtypeStruct(gain.shape, jnp.float32),
        ],
        compiler_params=kernel_params(),
        cost_estimate=lasting(10.0),
    )(side, *mine, *other, hidden, inverse, cotangent, gates, terms, router, gain, *earlier)


def finish_kernel(a_ref, b_ref, x_ref, inv_ref, dh_ref, gain_ref, out_ref):
    d_first = a_ref[...].astype(jnp.float32) + b_ref[...].astype(jnp.float32)
    inverse = inv_ref[...]
    normed = x_ref[...].astype(jnp.float32) * inverse
    scaled = d_first * gain_ref[...]
    center = jnp.mean(scaled * normed, axis=1, keepdims=True)
    out_ref[...] = dh_ref[...] + inverse * (scaled - normed * center)


def finish(mine, other, tokens, inverse, d_hidden, gain, tile):
    length, model = tokens.shape

    def rows(columns):
        return pl.BlockSpec((tile, columns), lambda i: (i, 0))

    return pl.pallas_call(
        finish_kernel,
        grid=(length // tile,),
        in_specs=[rows(model), rows(model), rows(model), rows(1), rows(model), whole(gain)],
        out_specs=rows(model),
        out_shape=jax.ShapeDtypeStruct((length, model), jnp.float32),
        compiler_params=kernel_params(),
        cost_estimate=lasting(8.0),
    )(mine, other, tokens, inverse, d_hidden, gain)


def home_block(k, count, b, g):
    return (jnp.where(b < k, 0, jnp.where(b > k, count - 1, g)), 0, 0)


def down_kernel(width, me_ref, act_ref, wd_ref, *refs):
    outs = refs[-1 - width :]
    away_ref, homes = outs[0], outs[1:]
    side = me_ref[1]
    batch, _, capacity, half = away_ref.shape
    mine = pl.ds(pl.multiple_of(side * half, half), half)
    other = pl.ds(pl.multiple_of((1 - side) * half, half), half)
    act = act_ref[...].reshape(batch * capacity, act_ref.shape[3])
    away_ref[...] = low(dot(act, wd_ref[:, other])).reshape(away_ref.shape)
    give_homes(low(dot(act, wd_ref[:, mine])).reshape(batch, capacity, half), homes)


def down_rows(me, act, w_down, earlier):
    width, count, capacity, units = act.shape
    half = w_down.shape[1] // 2
    batch = block_batch(width, capacity)

    def rows(columns):
        return pl.BlockSpec((batch, 1, capacity, columns), lambda b, g: (b, g, 0, 0))

    return pl.pallas_call(
        functools.partial(down_kernel, width),
        grid=(width // batch, count),
        in_specs=[SCALAR, rows(units), whole(w_down)] + anywhere(earlier),
        out_specs=[rows(half)] + home_specs(width, batch, count, capacity, half),
        out_shape=[jax.ShapeDtypeStruct((width, count, capacity, half), jnp.bfloat16)]
        + [jax.ShapeDtypeStruct((count, capacity, half), jnp.bfloat16)] * width,
        compiler_params=kernel_params(),
        cost_estimate=lasting(3.0 * count),
    )(me, act, w_down, *earlier)


def attend_back_kernel(
    heads,
    scale,
    tile,
    block,
    q_ref,
    k_ref,
    v_ref,
    segq_ref,
    segk_ref,
    lse_ref,
    db_ref,
    wo_ref,
    cos_ref,
    sin_ref,
    *refs,
):
    out_ref, dk_ref, dv_ref = refs[-3:]
    step = pl.program_id(0)
    length, size = k_ref.shape
    here = pl.ds(pl.multiple_of(step * tile, tile), tile)
    cosine, sine = cos_ref[here, :], sin_ref[here, :]

    def put(rows, start, array):
        out_ref[rows, start : start + size] = array.astype(jnp.bfloat16)

    @pl.when(step == 0)
    def _():
        dk_ref[...] = jnp.zeros_like(dk_ref)
        dv_ref[...] = jnp.zeros_like(dv_ref)

    d_mixed = dot(db_ref[...], wo_ref[...], 1, 1).astype(jnp.bfloat16)

    def work(seen):
        allowed = segk_ref[:seen] <= segq_ref[...]
        keys, values = k_ref[:seen], v_ref[:seen]
        keys_t = keys.T
        dk_total = jnp.zeros(keys.shape, jnp.float32)
        dv_total = jnp.zeros(keys.shape, jnp.float32)
        for head in range(heads):
            span = slice(head * size, (head + 1) * size)
            query = q_ref[:, span]
            d_head = d_mixed[:, span]
            offset = lse_ref[head : head + 1, :] * math.log2(math.e)
            scores = dot(keys, query, 1, 1) * (scale * math.log2(math.e)) - offset
            probs = jnp.where(allowed, jnp.exp2(scores), 0.0)
            d_probs = dot(values, d_head, 1, 1)
            scaled = probs * d_probs
            row_dot = jnp.sum(scaled, axis=0, keepdims=True)
            d_scores = (scaled - probs * row_dot).astype(jnp.bfloat16)
            dv_total = dv_total + dot(probs.astype(jnp.bfloat16), d_head)
            dk_total = dk_total + dot(d_scores, query)
            d_query = (dot(keys_t, d_scores) * scale).T
            put(here, head * size, turn(d_query, cosine, -sine))
        dk_ref[:seen] += dk_total * scale
        dv_ref[:seen] += dv_total

    for at in range(length // tile):

        @pl.when(step == at)
        def _(at=at):
            work(min((at + 1) * tile + block, length))

    @pl.when(step == pl.num_programs(0) - 1)
    def _():
        base = heads * size
        put(slice(None), base, turn(dk_ref[...], cos_ref[...], -sin_ref[...]))
        put(slice(None), base + size, dv_ref[...])


def attend_back(
    query, keys, values, seg_row, seg_col, lse, d_branch, w_out, cosine, sine, scale, tile, earlier
):
    length, span = query.shape
    size = keys.shape[1]
    heads = span // size
    model = w_out.shape[1]
    out = jax.ShapeDtypeStruct((length, span + 2 * size), jnp.bfloat16)
    return pl.pallas_call(
        functools.partial(attend_back_kernel, heads, scale, tile, longest_block),
        grid=(length // tile,),
        in_specs=[
            pl.BlockSpec((tile, span), lambda i: (i, 0)),
            whole(keys),
            whole(values),
            pl.BlockSpec((1, tile), lambda i: (0, i)),
            whole(seg_col),
            pl.BlockSpec((heads, tile), lambda i: (0, i)),
            pl.BlockSpec((tile, model), lambda i: (i, 0)),
            whole(w_out),
            whole(cosine),
            whole(sine),
        ]
        + anywhere(earlier),
        out_specs=whole(out),
        out_shape=out,
        scratch_shapes=[pltpu.VMEM((length, size), jnp.float32)] * 2,
        compiler_params=kernel_params(),
        cost_estimate=lasting(28.0),
    )(query, keys, values, seg_row, seg_col, lse, d_branch, w_out, cosine, sine, *earlier)


def first_grad_kernel(d_ref, wq_ref, wk_ref, wv_ref, *refs):
    out_ref = refs[-1]
    span, size = wq_ref.shape[1], wk_ref.shape[1]
    total = dot(d_ref[:, :span], wq_ref[...], 1, 1)
    total = total + dot(d_ref[:, span : span + size], wk_ref[...], 1, 1)
    total = total + dot(d_ref[:, span + size :], wv_ref[...], 1, 1)
    out_ref[...] = total.astype(jnp.bfloat16)


def first_grad(d_all, w_query, w_key, w_value, tile, earlier):
    length, columns = d_all.shape
    model = w_query.shape[0]
    return pl.pallas_call(
        first_grad_kernel,
        grid=(length // tile,),
        in_specs=[
            pl.BlockSpec((tile, columns), lambda i: (i, 0)),
            whole(w_query),
            whole(w_key),
            whole(w_value),
        ]
        + anywhere(earlier),
        out_specs=pl.BlockSpec((tile, model), lambda i: (i, 0)),
        out_shape=jax.ShapeDtypeStruct((length, model), jnp.bfloat16),
        compiler_params=kernel_params(),
        cost_estimate=lasting(8.0),
    )(d_all, w_query, w_key, w_value, *earlier)


def share_kernel(width, rows, extra, spot_ref, left_ref, right_ref, *refs):
    kept_ref, *gone = refs[3 * extra : 3 * extra + width]
    hold_ref = refs[3 * extra + width]
    products = [(0, dot(left_ref[...], right_ref[...], 0, 0))]
    if extra:
        also_ref, picks_ref, row_ref = refs[:3]
        column = jnp.broadcast_to(row_ref[...], (8, row_ref.shape[1])).T[:, :1]
        more = dot(also_ref[...], picks_ref[...], 0, 0)
        lane = lax.broadcasted_iota(jnp.int32, more.shape, 1)
        last = more.shape[1] - 1
        products.append((right_ref.shape[1], jnp.where(lane == last, column, more)))
    for start, product in products:
        for s in range(width):
            part = product[s * rows : (s + 1) * rows]
            hold_ref[s, :, start : start + product.shape[1]] = part
    kept_ref[0] = hold_ref[spot_ref[0]]
    for b in range(1, width):
        gone[b - 1][0] = hold_ref[spot_ref[0] ^ b].astype(jnp.bfloat16)


def share_grads(spot, left, right, depth, width, extra=()):
    length, model = left.shape
    columns = right.shape[1] + (extra[1].shape[1] if extra else 0)
    rows = model // (depth * width)
    if (width * rows) % 128:
        product = dot(left, right, 0, 0)
        if extra:
            more = jnp.concatenate([dot(extra[0], extra[1], 0, 0)[:, :-1], extra[2].T], axis=1)
            product = jnp.concatenate([product, more], axis=1)
        parted = product.reshape(depth, width, rows, columns)
        blocks = [
            lax.dynamic_index_in_dim(parted, spot[0] ^ b, 1, keepdims=False) for b in range(width)
        ]
        return [blocks[0]] + [low(block) for block in blocks[1:]]
    block = pl.BlockSpec((1, rows, columns), lambda l: (l, 0, 0))
    stripe = pl.BlockSpec((length, width * rows), lambda l: (0, l))
    more_specs = []
    if extra:
        more_specs = [stripe, whole(extra[1]), pl.BlockSpec((1, width * rows), lambda l: (0, l))]
    return pl.pallas_call(
        functools.partial(share_kernel, width, rows, int(bool(extra))),
        grid=(depth,),
        in_specs=[SCALAR, stripe, whole(right)] + more_specs,
        out_specs=[block] * width,
        out_shape=[jax.ShapeDtypeStruct((depth, rows, columns), jnp.float32)]
        + [jax.ShapeDtypeStruct((depth, rows, columns), jnp.bfloat16)] * (width - 1),
        scratch_shapes=[pltpu.VMEM((width, rows, columns), jnp.float32)],
        compiler_params=kernel_params(),
        cost_estimate=lasting(6.0),
    )(spot, left, right, *extra)


class Exchange:
    def __init__(self, count):
        self.count = count
        self.depth = line_depth(count)
        self.width = count // self.depth
        self.me = lax.axis_index("expert")
        self.line = self.me // self.width
        self.lines = [[l * self.width + s for l in range(self.depth)] for s in range(self.width)]

    def flip(self, rows, mask):
        return lax.ppermute(rows, "expert", [(d, d ^ mask) for d in range(self.count)])

    def spread(self, rows):
        return lax.all_gather(rows, "expert", axis_index_groups=self.lines)

    def collect(self, parts):
        flat = parts.reshape(-1, parts.shape[-1])
        return lax.psum_scatter(
            flat, "expert", scatter_dimension=0, axis_index_groups=self.lines, tiled=True
        )

    def plane(self, blocks):
        return [blocks[0]] + [self.flip(blocks[b], b) for b in range(1, self.width)]

    def sum_plane(self, blocks):
        held = wide(blocks[0])
        for b in range(1, self.width):
            held = held + wide(self.flip(blocks[b], b))
        return held

    def sum_line(self, held):
        total = lax.dynamic_index_in_dim(held, self.line, 0, keepdims=False)
        for g in range(1, self.depth):
            part = lax.dynamic_index_in_dim(held, self.line ^ g, 0, keepdims=False)
            total = total + wide(self.flip(low(part), g * self.width))
        return total


def low(array):
    return array.astype(jnp.bfloat16)


def wide(array):
    return array.astype(jnp.float32)


def swap(rows):
    return lax.ppermute(rows, "tensor", [(0, 1), (1, 0)])


def half_of(array, side):
    width = array.shape[-1] // 2
    return lax.dynamic_slice_in_dim(array, side * width, width, array.ndim - 1)


def join_halves(mine, other, side):
    first = jnp.where(side == 0, mine, other)
    last = jnp.where(side == 0, other, mine)
    return jnp.concatenate([first, last], axis=-1)


def on_device(
    tokens,
    cotangent,
    norm_gain,
    ffn_gain,
    w_query,
    w_key,
    w_value,
    w_out,
    w_router,
    w_gate,
    w_up,
    w_down,
    routes,
    order,
    segments,
):
    seq_length, model_width = tokens.shape
    half_width = model_width // 2
    expert_count = w_router.shape[1]
    pick_count = routes.shape[1]
    capacity = 9 * seq_length * pick_count // (8 * expert_count)
    head_width = w_key.shape[1]
    span = w_query.shape[1]
    unit_count = w_down.shape[1]
    score_scale = 1.0 / math.sqrt(head_width)
    tile = 256
    link = Exchange(expert_count)
    depth, width = link.depth, link.width
    side = lax.axis_index("tensor")
    side_ref = side.astype(jnp.int32)[None]
    me_ref = jnp.stack([link.me, side]).astype(jnp.int32)
    line_ref = link.line.astype(jnp.int32)[None]

    third = half_width // 3
    widths = (2 * third, third)
    cot_slots = link.spread(half_of(cotangent, side))
    placed = place_table(routes, order[0], link.me, expert_count, capacity)
    tables = []
    for g in range(depth):
        table = jnp.concatenate([placed[g * width : (g + 1) * width], routes.T], axis=0)
        tables.append(table if g == 0 else link.flip(table, g * width))
    places = jnp.stack([table[:width] for table in tables])
    place_rows = places[:, :, None, :]
    starts = capacity * jnp.arange(width, dtype=jnp.int32)
    place_columns = jnp.where(places >= 0, places + starts[None, :, None], -1)
    place_columns = jnp.swapaxes(place_columns, 1, 2)
    route_columns = jnp.stack([low(table[width:].T) for table in tables])

    route_blocks = link.plane(
        pick_rows(jnp.zeros_like(line_ref), place_rows, route_columns, capacity)
    )
    route_rows = jnp.stack(route_blocks)

    cosine, sine = (jnp.asarray(t) for t in rope_constants(seq_length, head_width))
    first_in, query, keys, values, inverse_first = project(
        tokens, norm_gain[None], w_query, w_key, w_value, cosine, sine, tile
    )
    seg_row, seg_col = segments, segments[0][:, None]
    mixed, lse, branch = attend(
        query, keys, values, seg_row, seg_col, w_out, score_scale, tile
    )
    hidden, second_in, inverse_second, gates, *in_parts = second_norm(
        side_ref,
        tokens,
        branch,
        swap(branch),
        ffn_gain[None],
        w_router,
        routes,
        tile,
        widths,
        (place_rows, route_rows),
    )
    w_both = jnp.concatenate([w_gate[0], w_up[0]], axis=1)
    in_slots = [link.spread(hold(in_parts[0], cot_slots))]
    cot_blocks = pick_rows(line_ref, place_rows, cot_slots, capacity, None, (second_in, w_both))
    cot_came = link.plane(cot_blocks)
    in_slots.append(link.spread(hold(in_parts[1], in_slots[0], *cot_came[1:])))
    in_first = pick_rows(line_ref, place_rows, in_slots[0], capacity)
    in_came = [link.plane(in_first)]
    in_last = pick_rows(line_ref, place_rows, in_slots[1], capacity, None, in_came[0][1:])
    in_came.append(link.plane(in_last))
    cot_mine = pile(cot_came, in_last[1:])
    cot_other = swap(cot_mine)
    in_mine = [pile(in_came[0], (cot_mine,))]
    in_other = [swap(in_mine[0])]
    in_mine.append(pile(in_came[1], (in_other[0], cot_other)))
    in_other.append(swap(in_mine[1]))
    pieces, c_pieces = in_mine + in_other, [cot_mine, cot_other]

    pre, acts, terms, backs = expert_rows(
        me_ref, pieces, c_pieces, widths[::-1], route_rows, w_both, w_down[0], w_router
    )
    swapped = [swap(away) for away, _ in backs]
    first_came = link.plane(join_cores(backs[0][1], swapped[0], ()))
    out_away, *out_homes = down_rows(me_ref, acts, w_down[0], ())
    terms = hold(terms, out_away)[..., 0]
    terms = jnp.stack(link.plane([terms[b] for b in range(width)]), axis=1)
    blocks = join_cores(backs[1][1], swapped[1], (*first_came[1:], out_away))
    first_part, first_token = combine(line_ref, place_columns, first_came, blocks[1:])
    row_parts = [first_part]
    came = link.plane(blocks)
    last_part, last_token = combine(line_ref, place_columns, came, (first_token,))
    row_parts.append(last_part)
    out_blocks = join_cores(out_homes, swap(out_away), (last_token, terms))
    out_came = link.plane(out_blocks)
    row_mine = [link.collect(row_parts[0])]
    row_mine.append(link.collect(hold(row_parts[1], row_mine[0])))
    row_other = [swap(part) for part in row_mine]

    terms = hold(terms, *out_blocks[1:])
    slot_ids = jnp.arange(capacity, dtype=jnp.int32)
    local = jnp.sum(
        jnp.where(
            places[:, :, None, :] == slot_ids[None, None, :, None], terms[:, :, :, None], 0.0
        ),
        axis=2,
    )
    term_table = jnp.concatenate(
        [local[g] if g == 0 else link.flip(local[g], g * width) for g in range(depth)]
    )
    term_table = term_table + swap(term_table)
    term_table = term_table[jnp.arange(expert_count, dtype=jnp.int32) ^ link.me].T

    act_rows = hold(acts, *out_blocks[1:]).reshape(-1, unit_count)
    grads = [contract_rows(act_rows, piece.reshape(-1, piece.shape[3])) for piece in c_pieces]
    down_grad = join_halves(
        *grads, side
    )[None]
    pre = hold(pre, term_table, down_grad).reshape(-1, 2 * unit_count)
    grads = [contract_rows(piece.reshape(-1, piece.shape[3]), pre) for piece in pieces]
    first, last = jnp.concatenate(grads[:2]), jnp.concatenate(grads[2:])
    upper, lower = jnp.where(side == 0, first, last), jnp.where(side == 0, last, first)
    gate_grad = jnp.concatenate([upper[:, :unit_count], lower[:, :unit_count]])[None]
    up_grad = jnp.concatenate([upper[:, unit_count:], lower[:, unit_count:]])[None]

    d_hidden, d_branch, d_logits, ffn_gain_grad = settle(
        side_ref,
        row_mine,
        row_other,
        hidden,
        inverse_second,
        cotangent,
        gates,
        term_table,
        w_router,
        ffn_gain[None],
        tile,
        (down_grad, gate_grad, up_grad),
    )

    out_parts, _ = combine(line_ref, place_columns, out_came, (d_branch,))
    out_held = hold(out_parts, row_mine[1])
    spot_ref = (link.me % width).astype(jnp.int32)[None]
    shared_early = share_grads(
        spot_ref, d_branch, mixed, depth, width, (second_in, d_logits, ffn_gain_grad)
    )
    early_held = link.sum_plane(shared_early)

    d_all = attend_back(
        query,
        keys,
        values,
        seg_row,
        seg_col,
        lse,
        d_branch,
        w_out,
        cosine,
        sine,
        score_scale,
        tile,
        (*shared_early[1:], out_held),
    )
    d_first = first_grad(d_all, w_query, w_key, w_value, tile, (early_held,))
    input_grad = finish(
        d_first, swap(d_first), tokens, inverse_first, d_hidden, norm_gain[None], tile
    )
    shared = share_grads(spot_ref, first_in, hold(d_all, d_first), depth, width)
    shared = [hold(shared[0], input_grad), *shared[1:]]
    qkv_held = link.sum_plane(shared)
    summed = link.sum_line(jnp.concatenate([qkv_held, early_held], axis=2))
    columns = span + 2 * head_width
    qkv_grad, early_sum = summed[:, :columns], summed[:, columns:]
    out_grad = early_sum[:, :span].T
    router_grad, ffn_gain_grad = early_sum[:, span : span + expert_count], early_sum[:, -1]
    combined = wide(hold(link.collect(out_held), qkv_held))
    output_half = low(half_of(hidden, side) + combined)
    output = join_halves(output_half, swap(output_half), side)
    rows = model_width // expert_count
    gain_part = jnp.zeros((rows,), jnp.float32)
    start = 0
    for weight in (w_query, w_key, w_value):
        mine = lax.dynamic_slice_in_dim(weight, link.me * rows, rows, 0)
        grads = qkv_grad[:, start : start + weight.shape[1]]
        gain_part = gain_part + jnp.sum(grads * wide(mine), axis=1)
        start += weight.shape[1]
    gain_part = gain_part / lax.dynamic_slice_in_dim(norm_gain, link.me * rows, rows, 0)
    norm_gain_grad = gain_part + swap(gain_part)
    return (
        output,
        input_grad,
        norm_gain_grad,
        ffn_gain_grad,
        qkv_grad[:, :span],
        qkv_grad[:, span : span + head_width],
        qkv_grad[:, span + head_width :],
        out_grad,
        router_grad,
        gate_grad,
        up_grad,
        down_grad,
    )


def solution(mesh):
    placed = (
        P("expert", None),
        P("expert", None),
        P(),
        P(),
        P(None, "tensor"),
        P(None, "tensor"),
        P(None, "tensor"),
        P("tensor", None),
        P(),
        P("expert", None, "tensor"),
        P("expert", None, "tensor"),
        P("expert", "tensor", None),
        P("expert", None),
        P("expert", None),
        P("expert", None),
    )
    return jax.shard_map(
        on_device,
        mesh=mesh,
        in_specs=placed,
        out_specs=(
            P("expert", None),
            P("expert", None),
            P("expert"),
            P("expert"),
            P("expert", "tensor"),
            P("expert", "tensor"),
            P("expert", "tensor"),
            P("tensor", "expert"),
            P("expert", None),
            P("expert", None, "tensor"),
            P("expert", None, "tensor"),
            P("expert", "tensor", None),
        ),
        check_vma=False,
    )
```
